256 devices in a mesh: az: 16 (over y_lo, z), ax: 8 (over x, y_hi), rad: 2 (over core).
Axes of the slice: x: 4, y: 4 (y_hi: 2, y_lo: 2; y = y_hi * 2 + y_lo), z: 8, core: 2. Of those that a mesh axis runs over, the one named last changes fastest.
Arguments:
- source: float32 [3, 128, 32, 4096], P(None, 'ax', 'rad', 'az'), may hold values from -24 to 24
- region: int32 [128, 32, 4096], P('ax', 'rad', 'az'), may hold values from 0 to 3, as said below
- skew_shift: int32 [128], P('ax'), may hold values from 0 to 4095
Outputs:
- solution: float32 [3, 128, 32, 4096], P(None, 'ax', 'rad', 'az')
- residual: float32 [3, 128, 32, 4096], P(None, 'ax', 'rad', 'az')
- harmonics: float32 [2, 128, 16, 256], P(None, ('ax', 'az'), 'rad')
The draws below stay inside these ranges and needn't reach their ends.
Inputs may be any that keep to these rules, and one draw needn't show every extreme that they name: `region`: 0 air, 1 iron, 2 magnet, 3 copper; the radial rows 8 to 23 are air.
All inputs are finite; a program needn't handle non-finite values.
Results may differ from the reference program's by a relative error of at most 0.0003.
Values sent between devices are 32-bit elements; how exact they have to be, the bound alone decides.
No kernel may reach another device: no remote copies, remote signals or barrier semaphores. Data moves between devices by JAX's collectives and lax.ppermute only.
A program may use at most 64 MiB of HBM per device.

```python
import math
import jax
import jax.numpy as jnp
from jax import lax

NA = 4096
MH = 256
GAP = 16
NZ = 128
NR = 32


def draw_region(key, part):
    key = jax.random.fold_in(key, 7)
    material = jax.random.randint(key, (NZ, NR, NA), 0, 4)
    radial = jnp.arange(NR)[None, :, None]
    gap_rows = (radial >= NR // 2 - GAP // 2) & (radial < NR // 2 + GAP // 2)
    return jnp.where(gap_rows, 0, material).astype(jnp.int32)


def plant(values, own_key, smallest, top_value):
    dims = values.shape
    index_at = [jax.random.randint(jax.random.fold_in(own_key, axis), (), 0, dims[axis]) for axis in range(len(dims))]
    values = values.at[tuple(index_at)].set(smallest)
    longest = dims.index(max(dims))
    index_at[longest] = (index_at[longest] + 1) % dims[longest]
    return values.at[tuple(index_at)].set(top_value)


def shard_levels(stream_key, dims, split, smallest, largest):
    factor_of, own = 1.0, jax.random.fold_in(stream_key, 6)
    for axis_at, shards_of in split:
        steps = jnp.exp(jax.random.uniform(jax.random.fold_in(own, axis_at), (shards_of,), jnp.float32, smallest / len(split), largest / len(split)))
        factor_of = factor_of * jnp.repeat(steps, dims[axis_at] // shards_of).reshape([-1 if axis == axis_at else 1 for axis in range(len(dims))])
    return factor_of


def centred(key, extent, spread, limit, shards=(), held_as=jnp.bfloat16):
    loudness = shard_levels(key, extent, shards, -0.22, 0.18) if shards else 1.0
    values = jax.random.normal(key, extent, jnp.float32) * spread * loudness
    return jnp.minimum(jnp.maximum(values, -limit), limit).astype(held_as)


def setup_inputs(seed: int = 0) -> dict:
    key_list = jax.random.split(jax.random.key(seed), 4)
    source = centred(key_list[0], (3, NZ, NR, NA), 4.0, 24.0, ((1, 8), (2, 2), (3, 16)), jnp.float32)
    region = draw_region(jax.random.fold_in(key_list[3], 71), 0)
    skew_shift = plant(jax.random.randint(key_list[2], (NZ,), 0, NA), jax.random.fold_in(key_list[2], 1), 0, NA - 1).astype(jnp.int32)
    return {"source": source, "region": region, "skew_shift": skew_shift}


cheb_center = 7.1
cheb_radius = 6.9
ratio_sigma = cheb_center / cheb_radius
rho_first = 1.0 / ratio_sigma
rho_second = 1.0 / (2.0 * ratio_sigma - rho_first)
keep_weight = rho_second * rho_first
fresh_weight = 2.0 * rho_second / cheb_radius

def materials(region):
    reluct = jnp.where(region == 1, 0.05, jnp.where(region == 2, 0.95, 1.0)).astype(jnp.float32)
    mass_term = jnp.where(region == 0, 0.2, jnp.where(region == 1, 1.5, jnp.where(region == 2, 0.6, 2.0))).astype(jnp.float32)
    return (reluct, mass_term)

def forward_diff(field, dim_index):
    length = field.shape[dim_index]
    result = lax.slice_in_dim(field, 1, length, axis=dim_index) - lax.slice_in_dim(field, 0, length - 1, axis=dim_index)
    for other_dim in range(3):
        if other_dim != dim_index:
            result = lax.slice_in_dim(result, 0, result.shape[other_dim] - 1, axis=other_dim)
    return result

def backward_diff(field, dim_index):
    length = field.shape[dim_index]
    result = lax.slice_in_dim(field, 1, length, axis=dim_index) - lax.slice_in_dim(field, 0, length - 1, axis=dim_index)
    for other_dim in range(3):
        if other_dim != dim_index:
            result = lax.slice_in_dim(result, 1, result.shape[other_dim], axis=other_dim)
    return result

def curl_with(differ, parts):
    return jnp.stack([differ(parts[2], 1) - differ(parts[1], 2), differ(parts[0], 2) - differ(parts[2], 0), differ(parts[1], 0) - differ(parts[0], 1)])

def apply_operator(field, coeff_ext):
    reluct = coeff_ext[0][:-1, :-1, :-1]
    flux_all = curl_with(forward_diff, field)
    strength = reluct[None] * flux_all
    image = curl_with(backward_diff, strength) + coeff_ext[1][None, 1:-1, 1:-1, 1:-1] * field[:, 1:-1, 1:-1, 1:-1]
    return (image, flux_all[:, 1:, 1:, 1:])

def pad_rim(field):
    lead = [(0, 0)] * (field.ndim - 3)
    wrapped = jnp.pad(field, lead + [(0, 0), (0, 0), (1, 1)], mode='wrap')
    return jnp.pad(wrapped, lead + [(1, 1), (1, 1), (0, 0)])

def reference(source, region, skew_shift):
    reluct, mass_term = materials(region)
    coeff_ext = pad_rim(jnp.stack([reluct, mass_term]))
    first_step = source / cheb_center
    first_image, first_flux = apply_operator(pad_rim(first_step), coeff_ext)
    resid_one = source - first_image
    second_step = keep_weight * first_step + fresh_weight * resid_one
    second_image, second_flux = apply_operator(pad_rim(second_step), coeff_ext)
    solution = first_step + second_step
    residual = resid_one - second_image
    flux = first_flux + second_flux
    gap_start = NR // 2 - GAP // 2
    radial_part = flux[1, :, gap_start:gap_start + GAP]
    azimuth_part = flux[2, :, gap_start:gap_start + GAP]
    stress = 0.5 * (radial_part * radial_part - azimuth_part * azimuth_part)
    shifted = (jnp.arange(NA, dtype=jnp.int32)[None, :] + skew_shift.astype(jnp.int32)[:, None]) % NA
    rolled = jnp.take_along_axis(stress, jnp.broadcast_to(shifted[:, None, :], stress.shape), axis=2)
    spectrum = jnp.fft.fft(rolled, axis=2)[:, :, :MH]
    harmonics = jnp.stack([jnp.real(spectrum), jnp.imag(spectrum)]) / math.sqrt(NA)
    return (solution, residual, harmonics.astype(source.dtype))
```

```python
import functools
import math

import jax
import jax.numpy as jnp
import numpy as np
from jax import lax
from jax.experimental import pallas as pl
from jax.experimental.pallas import tpu as pltpu
from jax.sharding import PartitionSpec as P

NA = 4096
MH = 256
F32 = jnp.float32

cheb_center = 7.1
cheb_radius = 6.9
ratio_sigma = cheb_center / cheb_radius
rho_first = 1.0 / ratio_sigma
rho_second = 1.0 / (2.0 * ratio_sigma - rho_first)
keep_weight = rho_second * rho_first
fresh_weight = 2.0 * rho_second / cheb_radius

FIRST = 1.0 / cheb_center
SECOND_SRC = keep_weight / cheb_center + fresh_weight
SECOND_A = fresh_weight / cheb_center
SUM_SRC = FIRST + SECOND_SRC

VMEM = pl.BlockSpec(memory_space=pltpu.VMEM)
SMEM = pl.BlockSpec(memory_space=pltpu.SMEM)


def materials(code):
    iron, magnet, outside = code == 1.0, code == 2.0, code < 0.0
    reluct = jnp.where(iron, 0.05, jnp.where(magnet, 0.95, jnp.where(outside, 0.0, 1.0)))
    mass = jnp.where(
        iron,
        1.5,
        jnp.where(magnet, 0.6, jnp.where(outside, 0.0, jnp.where(code == 0.0, 0.2, 2.0))),
    )
    return reluct.astype(F32), mass.astype(F32)


def roll(x, shift, axis):
    return pltpu.roll(x, shift % x.shape[axis], axis)


def from_partner(shape, core):
    sub = lax.broadcasted_iota(jnp.int32, shape, len(shape) - 2)
    return (jnp.where(sub < 4, 1, 0) + core) == 1


def curl(v0, v1, v2, v0a, v1a, v0r, v2r, v1n, v2n):
    return (
        (v2r - v2) - (v1a - v1),
        (v0a - v0) - (v2n - v2),
        (v1n - v1) - (v0r - v0),
    )


def stress_kernel(info, src, reg, sw1, up, dn, sw2, out, v, g, u, hs):
    core, lo, hi = info[0], info[1].astype(F32), info[2].astype(F32)
    gap = pl.ds(pl.multiple_of(8 * (1 - core), 8), 8)
    other = pl.ds(pl.multiple_of(8 * core, 8), 8)
    pick3 = from_partner((16, 8, 256), core)
    pick = from_partner((8, 256), core)
    for c in range(3):
        v[c, 2:18, 0:8, :] = src[c, :, gap, :]
        v[c, 2:18, 8:16, :] = jnp.where(pick3, sw1[c], src[c, :, other, :])
        v[c, 1, 0:8, :] = up[c, 1, gap, :] * lo
        v[c, 1, 8:16, :] = jnp.where(pick, sw2[2 * c + 1], up[c, 1, other, :]) * lo
        v[c, 18, 0:8, :] = dn[c, gap, :] * hi
        v[c, 18, 8:16, :] = jnp.where(pick, sw2[8 + c], dn[c, other, :]) * hi
        if c > 0:
            v[c, 19, 0:8, :] = dn[3 + c, gap, :] * hi
            v[c, 19, 8:16, :] = jnp.where(pick, sw2[11 + c], dn[3 + c, other, :]) * hi
    g[2:18, 0:8, :] = reg[:, gap, :].astype(F32)
    g[2:18, 8:16, :] = jnp.where(pick3, sw1[3], reg[:, other, :].astype(F32))
    g[1, 0:8, :] = (up[3, 1, gap, :] + 1.0) * lo - 1.0
    g[1, 8:16, :] = (jnp.where(pick, sw2[7], up[3, 1, other, :]) + 1.0) * lo - 1.0
    g[18, 0:8, :] = (dn[3, gap, :] + 1.0) * hi - 1.0
    g[18, 8:16, :] = (jnp.where(pick, sw2[11], dn[3, other, :]) + 1.0) * hi - 1.0

    lane = lax.broadcasted_iota(jnp.int32, (16, 256), 1)
    last_lane, first_lane = lane == 255, lane == 0

    def after(x):
        return jnp.where(last_lane, 0.0, roll(x, -1, 1))

    def before(x):
        return jnp.where(first_lane, 0.0, roll(x, 1, 1))

    def strength(i):
        v0, v1, v2 = v[0, i], v[1, i], v[2, i]
        reluct, mass = materials(g[i])
        c0, c1, c2 = curl(
            v0, v1, v2, after(v0), after(v1), roll(v0, -1, 0), roll(v2, -1, 0), v[1, i + 1], v[2, i + 1]
        )
        return (v0, v1, v2), (reluct * c0, reluct * c1, reluct * c2), mass

    _, (_, h1_first, h2_first), _ = strength(1)

    def first_pass(i, carry):
        h1_prev, h2_prev = carry
        (v0, v1, v2), (h0, h1, h2), mass = strength(i)
        a0 = (h2 - roll(h2, 1, 0)) - (h1 - before(h1)) + mass * v0
        a1 = (h0 - before(h0)) - (h2 - h2_prev) + mass * v1
        a2 = (h1 - h1_prev) - (h0 - roll(h0, 1, 0)) + mass * v2
        inside = jnp.where(i == 18, hi, 1.0)
        u[0, i - 2] = (SUM_SRC * v0 - SECOND_A * a0) * inside
        u[1, i - 2] = (SUM_SRC * v1 - SECOND_A * a1) * inside
        u[2, i - 2] = (SUM_SRC * v2 - SECOND_A * a2) * inside
        hs[0, i - 2] = h0[:, 128:]
        hs[1, i - 2] = h1[:, 128:]
        return (h1, h2)

    lax.fori_loop(2, 19, first_pass, (h1_first, h2_first))

    lane = lax.broadcasted_iota(jnp.int32, (8, 128), 1)
    group = ((lane + 4) & 127) >> 3
    at_last, at_first = lane == 127, lane == 0
    f = SECOND_A

    def second_pass(z, carry):
        u0, u1, u2 = u[0, z], u[1, z], u[2, z]
        flux1 = (after(u0) - u0) - (u[2, z + 1] - u2)
        flux2 = (u[1, z + 1] - u1) - (roll(u0, -1, 0) - u0)
        flux1, flux2 = flux1[:8], flux2[:8]
        out[z, :, 0:256] = 0.5 * (flux1 * flux1 - flux2 * flux2)
        f1l, f1r, f2l, f2r = flux1[:, :128], flux1[:, 128:], flux2[:, :128], flux2[:, 128:]
        h1 = hs[1, z]
        fh1 = f * h1[:8]
        curl_h = f * ((hs[0, z + 1] - hs[0, z]) + (roll(h1, -1, 0) - h1))[:8]
        rel, _ = materials(g[z + 2, :, 128:])
        rel_n, _ = materials(g[z + 3, :, 128:])
        rel_up = f * roll(rel, -1, 0)[:8]
        rel_dn = f * roll(rel, 1, 0)[:8]
        rel_n_dn = f * roll(rel_n, 1, 0)[:8]
        v0, v1 = v[0, z + 2, :, :128], v[1, z + 2, :, :128]
        v0_up = roll(v0, -1, 0)[:8]
        v1_dn = roll(v1, 1, 0)[:8]
        v0, v1 = v0[:8], v1[:8]
        v0_p, v0_m = v[0, z + 3, 0:8, :128], v[0, z + 1, 0:8, :128]
        v1_p = v[1, z + 3, :, :128]
        v1_p_dn = roll(v1_p, 1, 0)[:8]
        v1_p = v1_p[:8]
        inside = jnp.where(z == 15, hi, 1.0)
        r_a = u0[:8, :128] + f * ((v0_p + v0_m) - (3.0 + inside) * v0 + (v1_p - v1))
        r_b = f * ((v1_p - v1) + v0)
        r_c = f1l + f * v0
        r_d = f2l - r_b
        parts = (
            (0, jnp.where(at_first, roll(fh1, 1, 1), jnp.where(at_last, f1r - fh1, f1r))),
            (1, jnp.where(at_first, roll(curl_h, 1, 1), f2r)),
            (2, jnp.where(at_last, -rel_n_dn, 0.0)),
            (3, jnp.where(at_last, rel_dn, 0.0)),
            (4, jnp.where(at_first, roll(rel_up, 1, 1), jnp.where(at_last, -rel_up, 0.0))),
            (8, jnp.where(at_first, r_c, jnp.where(at_last, roll(r_a, -1, 1), roll(f * v0, -2, 1)))),
            (9, jnp.where(at_first, r_d, jnp.where(at_last, roll(r_b, -1, 1), 0.0))),
            (10, roll(v1_p_dn, -1, 1)),
            (11, roll(v1_dn, -1, 1)),
            (12, jnp.where(at_first, v0_up, roll(v0_up, -1, 1))),
        )
        extra = jnp.zeros((8, 128), F32)
        for k, part in parts:
            extra = jnp.where(group == k, roll(part, 8 * k, 1) if k else part, extra)
        out[z, :, 256:384] = extra
        return carry

    lax.fori_loop(0, 16, second_pass, 0)


def stress_call(info, src, reg, sw1, up, dn, sw2):
    return pl.pallas_call(
        stress_kernel,
        out_shape=jax.ShapeDtypeStruct((16, 8, 384), F32),
        in_specs=[SMEM] + [VMEM] * 6,
        out_specs=VMEM,
        scratch_shapes=[
            pltpu.VMEM((3, 20, 16, 256), F32),
            pltpu.VMEM((20, 16, 256), F32),
            pltpu.VMEM((3, 17, 16, 256), F32),
            pltpu.VMEM((2, 17, 16, 128), F32),
        ],
        compiler_params=pltpu.CompilerParams(vmem_limit_bytes=16 * 2**20),
        cost_estimate=pl.CostEstimate(flops=20_000_000, bytes_accessed=2_000_000, transcendentals=0),
        name="stress",
    )(info, src, reg, sw1, up, dn, sw2)


def rims_kernel(info, src, reg, sw1, up, dn, sw2, field, up_out, dn_out):
    core, lo, hi = info[0], info[1].astype(F32), info[2].astype(F32)
    pick3 = from_partner((16, 8, 256), core)
    pick = from_partner((8, 256), core)
    for c in range(4):
        empty = 0.0 if c < 3 else -1.0
        field[c, 2:18, 0:16, :] = src[c] if c < 3 else reg[...].astype(F32)
        field[c, 2:18, 16:24, :] = jnp.where(pick3, sw1[c], empty)

        def put(i, value, beside, valid):
            field[c, i, 0:16, :] = (value - empty) * valid + empty
            field[c, i, 16:24, :] = jnp.where(pick, (beside - empty) * valid + empty, empty)

        put(0, up[c, 0], sw2[2 * c], lo)
        put(1, up[c, 1], sw2[2 * c + 1], lo)
        put(18, dn[c], sw2[8 + c], hi)
        if c in (1, 2):
            put(19, dn[3 + c], sw2[11 + c], hi)
        else:
            field[c, 19] = jnp.full((24, 256), empty, F32)
    lane = lax.broadcasted_iota(jnp.int32, (24, 128), 1) >> 1
    for t in range(2):
        up_acc = jnp.zeros((24, 128), F32)
        dn_acc = jnp.zeros((24, 128), F32)
        for k in range(64):
            q = 64 * t + k
            if q >= 80:
                break
            c, i = q // 20, q % 20
            here = lane == k
            up_acc = jnp.where(here, roll(field[c, i, :, 128:], 2 * k + 2, 1), up_acc)
            dn_acc = jnp.where(here, roll(field[c, i, :, :128], 2 * k, 1), dn_acc)
        up_out[:, 128 * t : 128 * t + 128] = up_acc
        dn_out[:, 128 * t : 128 * t + 128] = dn_acc


def rims_call(info, src, reg, sw1, up, dn, sw2):
    return pl.pallas_call(
        rims_kernel,
        out_shape=[
            jax.ShapeDtypeStruct((4, 20, 24, 256), F32),
            jax.ShapeDtypeStruct((24, 256), F32),
            jax.ShapeDtypeStruct((24, 256), F32),
        ],
        in_specs=[SMEM] + [VMEM] * 6,
        out_specs=[VMEM] * 3,
        compiler_params=pltpu.CompilerParams(vmem_limit_bytes=16 * 2**20),
        cost_estimate=pl.CostEstimate(flops=2_000_000, bytes_accessed=4_000_000, transcendentals=0),
        name="rims",
    )(info, src, reg, sw1, up, dn, sw2)


def steps_kernel(field, left, right, sol, res, v, s):
    lane = lax.broadcasted_iota(jnp.int32, (24, 128), 1)
    for c in range(4):
        v[c, :, :, 0:256] = field[c]
        for i in range(20):
            q = 20 * c + i
            t, k = q // 64, q % 64
            tile = slice(128 * t, 128 * t + 128)
            v[c, i, :, 256:384] = jnp.where(
                lane < 64, roll(right[:, tile], -2 * k, 1), roll(left[:, tile], -2 * k - 2, 1)
            )

    def strength(w, i, reluct):
        v0, v1, v2 = w[0, i], w[1, i], w[2, i]
        c0, c1, c2 = curl(
            v0,
            v1,
            v2,
            roll(v0, -1, 1),
            roll(v1, -1, 1),
            roll(v0, -1, 0),
            roll(v2, -1, 0),
            w[1, i + 1],
            w[2, i + 1],
        )
        return (v0, v1, v2), (reluct * c0, reluct * c1, reluct * c2)

    def operator(w, i, code, h1_prev, h2_prev):
        reluct, mass = materials(code)
        (v0, v1, v2), (h0, h1, h2) = strength(w, i, reluct)
        a0 = (h2 - roll(h2, 1, 0)) - (h1 - roll(h1, 1, 1)) + mass * v0
        a1 = (h0 - roll(h0, 1, 1)) - (h2 - h2_prev) + mass * v1
        a2 = (h1 - h1_prev) - (h0 - roll(h0, 1, 0)) + mass * v2
        return (v0, v1, v2), (a0, a1, a2), (h1, h2), mass

    def step_plane(i, carry):
        vs, a, carry, mass = operator(v, i, v[3, i], *carry)
        inside = mass > 0.0
        for c in range(3):
            s[c, i] = jnp.where(inside, SECOND_SRC * vs[c] - SECOND_A * a[c], 0.0)
        return vs, a, carry

    _, (_, h1, h2) = strength(v, 0, materials(v[3, 0])[0])
    _, _, carry = step_plane(1, (h1, h2))

    def first_pass(i, carry):
        vs, a, carry = step_plane(i, carry)
        for c in range(3):
            own = vs[c][:16, :256]
            res[c, i - 2] = own - FIRST * a[c][:16, :256]
            sol[c, i - 2] = FIRST * own + s[c, i, 0:16, 0:256]
        return carry

    carry = lax.fori_loop(2, 18, first_pass, carry)
    step_plane(18, carry)

    _, (_, h1, h2) = strength(s, 1, materials(v[3, 1])[0])

    def second_pass(i, carry):
        _, a, carry, _ = operator(s, i, v[3, i], *carry)
        for c in range(3):
            res[c, i - 2] = res[c, i - 2] - a[c][:16, :256]
        return carry

    lax.fori_loop(2, 18, second_pass, (h1, h2))


def steps_call(field, left, right):
    return pl.pallas_call(
        steps_kernel,
        out_shape=[jax.ShapeDtypeStruct((3, 16, 16, 256), F32)] * 2,
        in_specs=[VMEM] * 3,
        out_specs=[VMEM] * 2,
        scratch_shapes=[
            pltpu.VMEM((4, 20, 24, 384), F32),
            pltpu.VMEM((3, 19, 24, 384), F32),
        ],
        compiler_params=pltpu.CompilerParams(vmem_limit_bytes=24 * 2**20),
        cost_estimate=pl.CostEstimate(flops=60_000_000, bytes_accessed=6_000_000, transcendentals=0),
        name="steps",
    )(field, left, right)


def harmonics_kernel(block, basis_hi, basis_lo, cosine, sine, out):
    lane = lax.broadcasted_iota(jnp.int32, (16, 8, 128), 2)
    seam = block[:, :, 256:384]
    right = roll(jnp.concatenate([seam[1:], seam[:1]], axis=0).reshape(128, 128), 64, 1)
    seam = seam.reshape(128, 128)
    total, product = seam + right, seam * right
    flux1 = total + roll(product, -16, 1) + roll(product, -24, 1)
    flux2 = roll(total, -8, 1) + roll(product, -32, 1)
    fixed = (0.5 * (flux1 * flux1 - flux2 * flux2)).reshape(16, 8, 128)
    moved = jnp.concatenate([fixed[15:], fixed[:15]], axis=0)
    low = jnp.where(lane == 0, moved, block[:, :, 0:128])
    high = jnp.where(lane >= 126, fixed, block[:, :, 128:256])
    x = jnp.concatenate([low.reshape(128, 128), high.reshape(128, 128)], axis=1)
    x_hi = x.astype(jnp.bfloat16)
    x_lo = (x - x_hi.astype(F32)).astype(jnp.bfloat16)

    def dot(a, b):
        return jnp.dot(a, b[...], preferred_element_type=F32)

    local = dot(x_hi, basis_hi) + (dot(x_hi, basis_lo) + dot(x_lo, basis_hi))
    local = local.reshape(16, 8, 2 * MH)
    real = jnp.zeros((8, MH), F32)
    imag = jnp.zeros((8, MH), F32)
    for j in range(16):
        c, s = cosine[j : j + 1, :], sine[j : j + 1, :]
        pc, ps = local[j, :, :MH], local[j, :, MH:]
        real = real + (pc * c - ps * s)
        imag = imag - (pc * s + ps * c)
    out[0, 0] = real
    out[1, 0] = imag


def harmonics_call(block, cosine, sine):
    turns = np.arange(256)[:, None] * np.arange(MH)[None, :] / NA
    angle = 2.0 * math.pi * turns
    basis = np.concatenate([np.cos(angle), np.sin(angle)], axis=1) / math.sqrt(NA)
    hi = basis.astype(jnp.bfloat16)
    lo = (basis - hi.astype(np.float64)).astype(jnp.bfloat16)
    return pl.pallas_call(
        harmonics_kernel,
        out_shape=jax.ShapeDtypeStruct((2, 1, 8, MH), F32),
        in_specs=[VMEM] * 5,
        out_specs=VMEM,
        compiler_params=pltpu.CompilerParams(vmem_limit_bytes=8 * 2**20),
        cost_estimate=pl.CostEstimate(flops=100_000_000, bytes_accessed=1_000_000, transcendentals=0),
        name="harmonics",
    )(block, jnp.asarray(hi), jnp.asarray(lo), cosine, sine)


def ring(axis, size, step):
    return functools.partial(
        lax.ppermute, axis_name=axis, perm=[(i, (i + step) % size) for i in range(size)]
    )


def on_device(source, region, skew_shift):
    n_az, n_ax = lax.axis_size("az"), lax.axis_size("ax")
    az, ax, rad = lax.axis_index("az"), lax.axis_index("ax"), lax.axis_index("rad")
    info = jnp.stack([rad, (ax > 0).astype(jnp.int32), (ax < n_ax - 1).astype(jnp.int32)])
    edge = region.astype(F32)
    up = jnp.concatenate([source[:, 14:16], edge[None, 14:16]], axis=0)
    dn = jnp.concatenate([source[:, 0], edge[None, 0], source[1:3, 1]], axis=0)
    up = ring("ax", n_ax, 1)(up)
    dn = ring("ax", n_ax, -1)(dn)
    swap = ring("rad", 2, 1)
    start = 8 * (1 - rad)
    sw1 = swap(
        jnp.concatenate(
            [
                lax.dynamic_slice_in_dim(source, start, 8, axis=2),
                lax.dynamic_slice_in_dim(edge, start, 8, axis=1)[None],
            ],
            axis=0,
        )
    )
    rim = jnp.concatenate([up.reshape(8, 16, 256), dn], axis=0)
    sw2 = swap(lax.dynamic_slice_in_dim(rim, start, 8, axis=1))
    stress = stress_call(info, source, region, sw1, up, dn, sw2)
    block = lax.all_to_all(stress, "az", split_axis=0, concat_axis=0, tiled=True)
    field, az_up, az_dn = rims_call(info, source, region, sw1, up, dn, sw2)
    left = ring("az", n_az, 1)(az_up)
    right = ring("az", n_az, -1)(az_dn)
    solution, residual = steps_call(field, left, right)
    shift = lax.dynamic_slice_in_dim(skew_shift, az, 1)
    offset = 256 * jnp.arange(16, dtype=jnp.int32) - shift
    turns = (offset[:, None] * jnp.arange(MH, dtype=jnp.int32)[None, :]) & (NA - 1)
    angle = turns.astype(F32) * (2.0 * math.pi / NA)
    harmonics = harmonics_call(block, jnp.cos(angle), jnp.sin(angle))
    return (solution, residual, harmonics)


def solution(mesh):
    in_specs = (P(None, "ax", "rad", "az"), P("ax", "rad", "az"), P("ax"))
    out_specs = (
        P(None, "ax", "rad", "az"),
        P(None, "ax", "rad", "az"),
        P(None, ("ax", "az"), "rad", None),
    )
    return jax.shard_map(
        on_device, mesh=mesh, in_specs=in_specs, out_specs=out_specs, check_vma=False
    )
```

```python
import functools
import math

import jax
import jax.numpy as jnp
import numpy as np
from jax import lax
from jax.experimental import pallas as pl
from jax.experimental.pallas import tpu as pltpu
from jax.sharding import PartitionSpec as P

NA = 4096
MH = 256
F32 = jnp.float32

cheb_center = 7.1
cheb_radius = 6.9
ratio_sigma = cheb_center / cheb_radius
rho_first = 1.0 / ratio_sigma
rho_second = 1.0 / (2.0 * ratio_sigma - rho_first)
keep_weight = rho_second * rho_first
fresh_weight = 2.0 * rho_second / cheb_radius

FIRST = 1.0 / cheb_center
SECOND_SRC = keep_weight / cheb_center + fresh_weight
SECOND_A = fresh_weight / cheb_center
SUM_SRC = FIRST + SECOND_SRC

VMEM = pl.BlockSpec(memory_space=pltpu.VMEM)
SMEM = pl.BlockSpec(memory_space=pltpu.SMEM)
HBM = pl.BlockSpec(memory_space=pltpu.HBM)

UNROLL = 2
SEND_KIB = 54784


def materials(code):
    iron, magnet, outside = code == 1.0, code == 2.0, code < 0.0
    reluct = jnp.where(iron, 0.05, jnp.where(magnet, 0.95, jnp.where(outside, 0.0, 1.0)))
    mass = jnp.where(
        iron,
        1.5,
        jnp.where(magnet, 0.6, jnp.where(outside, 0.0, jnp.where(code == 0.0, 0.2, 2.0))),
    )
    return reluct.astype(F32), mass.astype(F32)


def roll(x, shift, axis):
    return pltpu.roll(x, shift % x.shape[axis], axis)


def from_partner(shape, core):
    sub = lax.broadcasted_iota(jnp.int32, shape, len(shape) - 2)
    return (sub >= 6 * core) & (sub < 6 * core + 2)


class Kept:
    planes = 48
    of_field, of_step, of_res = (0, 1, 13, 14, 15), (1, 2, 13, 14), (1, 14)

    def field(self, c, z):
        return 5 * c + self.of_field.index(z)

    def step(self, c, z):
        return 20 + 4 * c + self.of_step.index(z)

    def res(self, c, z):
        return (32 + 2 * c + self.of_res.index(z), slice(0, 16))

    def strips(self, c, side):
        return (38 + c, slice(None), slice(128 * side, 128 * side + 128))

    def stress(self, z):
        return (42 + z // 3, slice(8 * (z % 3), 8 * (z % 3) + 8))


class Rim:
    planes = 12 + 6 + 4 + 1

    def step(self, c, z):
        return 4 * c + (-1, 0, 15, 16).index(z)

    def res(self, c, z):
        return (12 + 2 * c + (0, 15).index(z), slice(0, 16))

    def strips(self, c, side):
        return (18 + c, slice(None), slice(128 * side, 128 * side + 128))

    code = 22


KEPT, RIM = Kept(), Rim()


def gap_tile(x, core):
    return jnp.where(core == 1, x[0:8], x[8:16])


def loop(first, last, body, unroll):
    rounds = (last - first) // unroll

    def several(t, carry):
        for k in range(unroll):
            body(first + t * unroll + k)
        return carry

    lax.fori_loop(0, rounds, several, 0)
    for k in range(first + rounds * unroll, last):
        body(k)


def curl(v0, v1, v2, v0a, v1a, v0r, v2r, v1n, v2n):
    return (
        (v2r - v2) - (v1a - v1),
        (v0a - v0) - (v2n - v2),
        (v1n - v1) - (v0r - v0),
    )


def strength(v0, v1, v2, v1n, v2n, reluct):
    c0, c1, c2 = curl(
        v0, v1, v2, roll(v0, -1, 1), roll(v1, -1, 1), roll(v0, -1, 0), roll(v2, -1, 0), v1n, v2n
    )
    return reluct * c0, reluct * c1, reluct * c2


def image(v, h, h1p, h2p, mass):
    h0, h1, h2 = h
    return (
        (h2 - roll(h2, 1, 0)) - (h1 - roll(h1, 1, 1)) + mass * v[0],
        (h0 - roll(h0, 1, 1)) - (h2 - h2p) + mass * v[1],
        (h1 - h1p) - (h0 - roll(h0, 1, 0)) + mass * v[2],
    )


def second_of(v, a, mass):
    return [jnp.where(mass > 0.0, SECOND_SRC * v[c] - SECOND_A * a[c], 0.0) for c in range(3)]


def fluxes(u0, u1, u2, u1n, u2n):
    return (roll(u0, -1, 1) - u0) - (u2n - u2), (u1n - u1) - (roll(u0, -1, 0) - u0)


def stress_of(u0, u1, u2, u1n, u2n, core):
    flux1, flux2 = fluxes(u0, u1, u2, u1n, u2n)
    flux1, flux2 = gap_tile(flux1, core), gap_tile(flux2, core)
    return 0.5 * (flux1 * flux1 - flux2 * flux2)


def pack_plane(rights, lefts, x, i, lane):
    here = (lane >= 6 * i) & (lane < 6 * i + 6)
    right = jnp.where(here, roll(x[:, 128:], 6 * i + 4, 1), rights)
    left = jnp.where(here, roll(x[:, :128], 6 * i + 2, 1), lefts)
    return right, left


def send_kernel(src, reg, up, dn, rows, sems):
    pairs = [
        (reg.at[14:16], rows.at[0:2]),
        (reg.at[0], rows.at[2]),
        (src.at[1, 1], dn.at[4]),
        (src.at[2, 1], dn.at[5]),
    ]
    for c in range(3):
        pairs.append((src.at[c, 14:16], up.at[2 * c : 2 * c + 2]))
        pairs.append((src.at[c, 0], dn.at[c]))
    copies = [pltpu.make_async_copy(x, y, sems.at[n]) for n, (x, y) in enumerate(pairs)]
    for copy in copies:
        copy.start()
    for copy in copies:
        copy.wait()
    up[6:8] = rows[0:2].astype(F32)
    dn[3] = rows[2].astype(F32)


def send_call(src, reg):
    shapes = [(8, 16, 256), (6, 16, 256)]
    return pl.pallas_call(
        send_kernel,
        out_shape=[jax.ShapeDtypeStruct(shape, F32) for shape in shapes],
        in_specs=[HBM, HBM],
        out_specs=[VMEM] * 2,
        scratch_shapes=[pltpu.VMEM((3, 16, 256), jnp.int32), pltpu.SemaphoreType.DMA((10,))],
        compiler_params=pltpu.CompilerParams(vmem_limit_bytes=SEND_KIB * 2**10),
        name="send",
    )(src, reg)


def beside_kernel(src, reg, _, sw):
    core = lax.axis_index("rad")
    tile = pl.ds(pl.multiple_of(8 * (1 - core), 8), 8)
    sub = lax.broadcasted_iota(jnp.int32, (16, 8, 256), 1) >> 1
    packed = jnp.zeros((16, 8, 256), F32)
    for c in range(4):
        rows = src[c, :, tile, :] if c < 3 else reg[:, tile, :].astype(F32)
        first = pltpu.roll(rows, 2 * c, 1) if c else rows
        last = pltpu.roll(rows, (2 * c + 2) % 8, 1) if c < 3 else rows
        packed = jnp.where(sub == c, jnp.where(core == 1, first, last), packed)
    sw[...] = packed


def call(kernel, name, outs, scratch, limit, in_specs, out_specs):
    return pl.pallas_call(
        kernel,
        out_shape=[jax.ShapeDtypeStruct(shape, F32) for shape in outs],
        in_specs=in_specs,
        out_specs=out_specs,
        scratch_shapes=[pltpu.VMEM(x, F32) if isinstance(x, tuple) else x for x in scratch],
        compiler_params=pltpu.CompilerParams(vmem_limit_bytes=limit * 2**20),
        cost_estimate=pl.CostEstimate(flops=10_000_000, bytes_accessed=2_000_000, transcendentals=0),
        name=name,
    )


def inner_kernel(src, reg, sw, kept, flag, sol_out, res_out, field, s, hh, sol, res, ids, sems):
    flag[...] = jnp.zeros(flag.shape, F32)
    core = lax.axis_index("rad")
    pick = from_partner((8, 256), core)
    lane = lax.broadcasted_iota(jnp.int32, (24, 128), 1)
    copies = [pltpu.make_async_copy(src.at[c], field.at[c, :, 0:16, :], sems.at[c]) for c in range(3)]
    copies.append(pltpu.make_async_copy(reg, ids, sems.at[3]))
    for copy in copies:
        copy.start()
    for copy in copies:
        copy.wait()

    def assemble(z):
        for c in range(4):
            first = roll(sw[z], -2 * c, 0) if c else sw[z]
            last = roll(sw[z], 6 - 2 * c, 0) if c < 3 else sw[z]
            rows = jnp.where(core == 1, last, first)
            field[c, z, 16:24, :] = jnp.where(pick, rows, 0.0 if c < 3 else -1.0)
        field[3, z, 0:16, :] = ids[z].astype(F32)

    loop(0, 16, assemble, 4)

    def vec(z):
        return [field[c, z] for c in range(3)]

    def first_h(z):
        reluct, _ = materials(field[3, z])
        h = strength(*vec(z), field[1, z + 1], field[2, z + 1], reluct)
        for c in range(3):
            hh[c, z] = h[c]

    loop(0, 15, first_h, UNROLL)

    def first_a(z):
        v = vec(z)
        _, mass = materials(field[3, z])
        a = image(v, [hh[c, z] for c in range(3)], hh[1, z - 1], hh[2, z - 1], mass)
        step = second_of(v, a, mass)
        for c in range(3):
            s[c, z] = step[c]
            res[c, z] = (v[c] - FIRST * a[c])[:16]
            sol[c, z] = (FIRST * v[c] + step[c])[:16]

    loop(1, 15, first_a, UNROLL)

    copies = [pltpu.make_async_copy(sol, sol_out, sems.at[0])]
    copies[0].start()

    def stress_plane(z):
        u0, u1, u2 = [FIRST * field[c, z] + s[c, z] for c in range(3)]
        u1n, u2n = [FIRST * field[c, z + 1] + s[c, z + 1] for c in (1, 2)]
        kept[KEPT.stress(z)] = stress_of(u0, u1, u2, u1n, u2n, core)

    for z in range(1, 14):
        stress_plane(z)

    def second_h(z):
        reluct, _ = materials(field[3, z])
        h = strength(s[0, z], s[1, z], s[2, z], s[1, z + 1], s[2, z + 1], reluct)
        for c in range(3):
            hh[c, z] = h[c]

    loop(1, 14, second_h, UNROLL)

    def second_a(z):
        _, mass = materials(field[3, z])
        v = [s[c, z] for c in range(3)]
        a = image(v, [hh[c, z] for c in range(3)], hh[1, z - 1], hh[2, z - 1], mass)
        for c in range(3):
            res[c, z] = res[c, z] - a[c][:16]

    loop(2, 14, second_a, UNROLL)
    copies.append(pltpu.make_async_copy(res, res_out, sems.at[1]))
    copies[1].start()
    for c in range(3):
        for z in KEPT.of_step:
            kept[KEPT.step(c, z)] = s[c, z]
        for z in KEPT.of_res:
            kept[KEPT.res(c, z)] = res[c, z]
    for c in range(4):
        for z in KEPT.of_field:
            kept[KEPT.field(c, z)] = field[c, z]

    for c in range(4):
        right = left = jnp.full((24, 128), 0.0 if c < 3 else -1.0, F32)
        for z in range(16):
            right, left = pack_plane(right, left, field[c, z], z + 2, lane)
        kept[KEPT.strips(c, 0)] = right
        kept[KEPT.strips(c, 1)] = left

    for copy in copies:
        copy.wait()


def rim_kernel(kept, up, dn, sw2, _, hbm, rim, az_up, az_dn, w, out, sem):
    core, ax = lax.axis_index("rad"), lax.axis_index("ax")
    lo = jnp.where(ax > 0, 1.0, 0.0)
    hi = jnp.where(ax < lax.axis_size("ax") - 1, 1.0, 0.0)
    pick = from_partner((8, 256), core)
    for c in range(4):
        empty = 0.0 if c < 3 else -1.0

        def put(i, value, beside, valid):
            w[c, i, 0:16, :] = (value - empty) * valid + empty
            w[c, i, 16:24, :] = jnp.where(pick, (beside - empty) * valid + empty, empty)

        put(0, up[2 * c], sw2[2 * c], lo)
        put(1, up[2 * c + 1], sw2[2 * c + 1], lo)
        put(6, dn[c], sw2[8 + c], hi)
        if c in (1, 2):
            put(7, dn[3 + c], sw2[11 + c], hi)
        else:
            w[c, 7] = jnp.full((24, 256), empty, F32)
        w[c, 2] = kept[KEPT.field(c, 0)]
        w[c, 3] = kept[KEPT.field(c, 1)]
        w[c, 4] = kept[KEPT.field(c, 14)]
        w[c, 5] = kept[KEPT.field(c, 15)]

    def vec(i):
        return [w[c, i] for c in range(3)]

    def h_of(i, reluct):
        return strength(*vec(i), w[1, i + 1], w[2, i + 1], reluct)

    def rims(i, zs):
        _, h1, h2 = h_of(i, materials(w[3, i])[0])
        steps = []
        for n in range(2):
            reluct, mass = materials(w[3, i + 1 + n])
            h = h_of(i + 1 + n, reluct)
            v = vec(i + 1 + n)
            a = image(v, h, h1, h2, mass)
            h1, h2 = h[1], h[2]
            step = second_of(v, a, mass)
            for c in range(3):
                rim[RIM.step(c, zs[n])] = step[c]
                if zs[n] in (0, 15):
                    rim[RIM.res(c, zs[n])] = (v[c] - FIRST * a[c])[:16]
            steps.append([FIRST * v[c] + step[c] for c in range(3)])
        return steps

    rim[RIM.code] = w[3, 1]
    _, u_first = rims(0, (-1, 0))
    u_last, u_after = rims(4, (15, 16))
    u_one = [FIRST * w[c, 3] + kept[KEPT.step(c, 1)] for c in range(3)]
    u_14 = [FIRST * w[c, 4] + kept[KEPT.step(c, 14)] for c in range(3)]
    for z in range(1, 14):
        out[z, :, 0:256] = kept[KEPT.stress(z)]
    out[0, :, 0:256] = stress_of(*u_first, u_one[1], u_one[2], core)
    out[14, :, 0:256] = stress_of(*u_14, u_last[1], u_last[2], core)
    out[15, :, 0:256] = stress_of(*u_last, u_after[1], u_after[2], core)

    lane = lax.broadcasted_iota(jnp.int32, (24, 128), 1)
    plane = (lane * 43) >> 8
    k = lane - 6 * plane
    right, left = [], []
    for c in range(4):
        r, l = kept[KEPT.strips(c, 0)], kept[KEPT.strips(c, 1)]
        for i, n in ((0, 0), (1, 1), (18, 6), (19, 7)):
            r, l = pack_plane(r, l, w[c, n], i, lane)
        empty = 0.0 if c < 3 else -1.0
        r = jnp.where(k < 4, r, empty)
        l = jnp.where(k > 1, l, empty)
        rim[RIM.strips(c, 0)] = r
        rim[RIM.strips(c, 1)] = l
        right.append(r)
        left.append(l)
    for msg, x in ((az_up, right), (az_dn, left)):
        msg[0] = jnp.where(
            k < 2, roll(x[2], -2, 1), jnp.where(k < 4, x[0], roll(x[1], 2, 1))
        )
        msg[1] = x[3]

    f = SECOND_A

    def partial(x):
        reluct, mass = materials(x[3])
        v = x[:3]
        h = strength(*v, roll(v[1], -6, 1), roll(v[2], -6, 1), reluct)
        a = image(v, h, roll(h[1], 6, 1), roll(h[2], 6, 1), mass)
        step = second_of(v, a, mass)
        u = [FIRST * v[c] + step[c] for c in range(3)]
        return reluct, h, u, fluxes(*u, roll(u[1], -6, 1), roll(u[2], -6, 1))

    reluct, (h0, h1, _), _, (flux1, flux2) = partial(right)
    fh1 = f * h1
    rest = f * ((roll(h0, -6, 1) - h0) + (roll(h1, -1, 0) - h1))
    rel_up, rel_dn = f * roll(reluct, -1, 0), f * roll(reluct, 1, 0)
    a_part = jnp.where(
        k < 2,
        roll(jnp.where(k == 3, flux1 - fh1, flux1), -2, 1),
        jnp.where(k == 2, roll(fh1, -1, 1), jnp.where(k < 5, roll(flux2, 1, 1), roll(rest, 2, 1))),
    )
    x_part = jnp.where(
        k == 1,
        -roll(rel_dn, -8, 1),
        jnp.where(k == 4, -roll(rel_up, 1, 1), jnp.where(k == 5, roll(rel_up, 2, 1), 0.0)),
    )
    z_part = jnp.where(k == 1, roll(rel_dn, -2, 1), 0.0)

    _, _, u, (flux1, flux2) = partial(left)
    v0, v1 = left[0], left[1]
    v1n = roll(v1, -6, 1)
    v1_dn = roll(v1, 1, 0)
    v0_up = roll(v0, -1, 0)
    inside = jnp.where(plane == 17, hi, 1.0)
    r_a = u[0] + f * ((roll(v0, -6, 1) + roll(v0, 6, 1)) - (3.0 + inside) * v0 + (v1n - v1))
    r_b = f * ((v1n - v1) + v0)
    b_part = jnp.where(
        k == 0,
        roll(f * v0, -2, 1),
        jnp.where(
            k == 1,
            roll(r_a, -1, 1),
            jnp.where(
                k == 2,
                flux1 + f * v0,
                jnp.where(k == 4, roll(r_b, 2, 1), jnp.where(k == 5, roll(flux2 - r_b, 3, 1), 0.0)),
            ),
        ),
    )
    y_part = jnp.where(
        k == 1, roll(v1_dn, -7, 1), jnp.where(k == 4, roll(v0_up, 2, 1), roll(v0_up, 3, 1))
    )
    w_part = roll(v1_dn, -1, 1)

    lane = lax.broadcasted_iota(jnp.int32, (8, 128), 1)
    group = lane >> 3
    parts = [
        (n, gap_tile(x, core))
        for n, x in ((0, a_part), (1, x_part), (2, z_part), (8, b_part), (9, y_part), (10, w_part))
    ]
    for z in range(16):
        extra = jnp.zeros((8, 128), F32)
        for n, part in parts:
            extra = jnp.where(group == n, roll(part, 8 * n - 6 * (z + 2), 1), extra)
        out[z, :, 256:384] = extra
    copy = pltpu.make_async_copy(out, hbm, sem.at[0])
    copy.start()
    copy.wait()


def edge_kernel(skew, kept, rim, sol_in, res_in, sol, out, table):
    offset = 256 * lax.broadcasted_iota(jnp.int32, (16, MH), 0) - skew[lax.axis_index("az")]
    turns = (offset * lax.broadcasted_iota(jnp.int32, (16, MH), 1)) & (NA - 1)
    angle = turns.astype(F32) * (2.0 * math.pi / NA)
    table[0] = jnp.cos(angle)
    table[1] = jnp.sin(angle)

    def step(z, c):
        return rim[RIM.step(c, z)] if z in (-1, 0, 15, 16) else kept[KEPT.step(c, z)]

    def materials_of(z):
        return materials(rim[RIM.code] if z < 0 else kept[KEPT.field(3, z)])

    def h_of(z):
        return strength(
            step(z, 0), step(z, 1), step(z, 2), step(z + 1, 1), step(z + 1, 2), materials_of(z)[0]
        )

    for z in (0, 14):
        _, h1, h2 = h_of(z - 1)
        for n in range(2):
            h = h_of(z + n)
            a = image([step(z + n, c) for c in range(3)], h, h1, h2, materials_of(z + n)[1])
            h1, h2 = h[1], h[2]
            for c in range(3):
                x = z + n
                before = rim[RIM.res(c, x)] if x in (0, 15) else kept[KEPT.res(c, x)]
                out[c, x] = before - a[c][:16]
    for c in range(3):
        out[c, 2:14] = res_in[c, 2:14]
        sol[c, 1:15] = sol_in[c, 1:15]
        for z in (0, 15):
            sol[c, z] = FIRST * kept[KEPT.field(c, z)][:16] + rim[RIM.step(c, z)][:16]


def seam_kernel(rim, sol_in, res_in, from_left, from_right, sol, res, a_sol, a_res, sems):
    lane = lax.broadcasted_iota(jnp.int32, (24, 128), 1)
    plane = (lane * 43) >> 8
    k = lane - 6 * plane

    def full(x, msg, halo, shifts):
        return [
            jnp.where(halo, roll(msg[t], shift, 1) if shift else msg[t], x[c])
            for c, (t, shift) in enumerate(zip((0, 0, 0, 1), shifts))
        ]

    def solve(x):
        reluct, mass = materials(x[3])
        v = x[:3]
        h = strength(*v, roll(v[1], -6, 1), roll(v[2], -6, 1), reluct)
        a = image(v, h, roll(h[1], 6, 1), roll(h[2], 6, 1), mass)
        step = second_of(v, a, mass)
        h = strength(*step, roll(step[1], -6, 1), roll(step[2], -6, 1), reluct)
        a2 = image(step, h, roll(h[1], 6, 1), roll(h[2], 6, 1), mass)
        return (
            [(FIRST * v[c] + step[c])[:16] for c in range(3)],
            [(v[c] - FIRST * a[c] - a2[c])[:16] for c in range(3)],
        )

    right = solve(full([rim[RIM.strips(c, 0)] for c in range(4)], from_right, k > 3, (2, 0, 4, 2)))
    left = solve(full([rim[RIM.strips(c, 1)] for c in range(4)], from_left, k < 2, (-2, -4, 0, -2)))
    lane = lax.broadcasted_iota(jnp.int32, (16, 128), 1)
    copies = []
    for z in range(16):
        i = z + 2
        for n, buf in ((0, a_sol), (1, a_res)):
            for c in range(3):
                x = (sol_in, res_in)[n][c, z]
                buf[z // 4, c, z % 4, :, 0:128] = jnp.where(
                    lane < 2, roll(left[n][c], -(6 * i + 2), 1), x[:, :128]
                )
                buf[z // 4, c, z % 4, :, 128:256] = jnp.where(
                    lane >= 126, roll(right[n][c], 124 - 6 * i, 1), x[:, 128:]
                )
        if z % 4 == 3:
            t = z // 4
            for n, (buf, dst) in enumerate(((a_sol, sol), (a_res, res))):
                copy = pltpu.make_async_copy(
                    buf.at[t], dst.at[:, pl.ds(4 * t, 4)], sems.at[n, t]
                )
                copy.start()
                copies.append(copy)
    for copy in copies:
        copy.wait()


def seam_call(*args):
    out = jax.ShapeDtypeStruct((3, 16, 16, 256), F32)
    return pl.pallas_call(
        seam_kernel,
        out_shape=[out, out],
        in_specs=[VMEM] * len(args),
        out_specs=[HBM] * 2,
        scratch_shapes=[
            pltpu.VMEM((4, 3, 4, 16, 256), F32),
            pltpu.VMEM((4, 3, 4, 16, 256), F32),
            pltpu.SemaphoreType.DMA((2, 4)),
        ],
        compiler_params=pltpu.CompilerParams(vmem_limit_bytes=12 * 2**20),
        cost_estimate=pl.CostEstimate(flops=4_000_000, bytes_accessed=4_000_000, transcendentals=0),
        name="seams",
    )(*args)


def harmonics_kernel(block, basis_hi, basis_lo, table, out):
    lane = lax.broadcasted_iota(jnp.int32, (16, 8, 128), 2)
    seam = block[:, :, 256:384]
    right = roll(jnp.concatenate([seam[1:], seam[:1]], axis=0).reshape(128, 128), 64, 1)
    seam = seam.reshape(128, 128)
    product = seam * right
    flux = seam + right + roll(product, -8, 1) + roll(product, -16, 1)
    square = 0.5 * (flux * flux)
    fixed = roll(square - roll(square, -3, 1), -2, 1).reshape(16, 8, 128)
    moved = jnp.concatenate([fixed[15:], fixed[:15]], axis=0)
    low = jnp.where(lane == 0, moved, block[:, :, 0:128])
    high = jnp.where(lane >= 126, fixed, block[:, :, 128:256])
    x = jnp.concatenate([low.reshape(128, 128), high.reshape(128, 128)], axis=1)
    x_hi = x.astype(jnp.bfloat16)
    x_lo = (x - x_hi.astype(F32)).astype(jnp.bfloat16)

    def dot(a, b):
        return jnp.dot(a, b[...], preferred_element_type=F32)

    local = dot(x_hi, basis_hi) + (dot(x_hi, basis_lo) + dot(x_lo, basis_hi))
    local = local.reshape(16, 8, 2 * MH)
    real = jnp.zeros((8, MH), F32)
    imag = jnp.zeros((8, MH), F32)
    for j in range(16):
        c, s = table[0, j : j + 1, :], table[1, j : j + 1, :]
        pc, ps = local[j, :, :MH], local[j, :, MH:]
        real = real + (pc * c - ps * s)
        imag = imag - (pc * s + ps * c)
    out[0, 0] = real
    out[1, 0] = imag


def harmonics_call(block, table):
    turns = np.arange(256)[:, None] * np.arange(MH)[None, :] / NA
    angle = 2.0 * math.pi * turns
    basis = np.concatenate([np.cos(angle), np.sin(angle)], axis=1) / math.sqrt(NA)
    hi = basis.astype(jnp.bfloat16)
    lo = (basis - hi.astype(np.float64)).astype(jnp.bfloat16)
    return pl.pallas_call(
        harmonics_kernel,
        out_shape=jax.ShapeDtypeStruct((2, 1, 8, MH), F32),
        in_specs=[VMEM] * 4,
        out_specs=VMEM,
        compiler_params=pltpu.CompilerParams(vmem_limit_bytes=8 * 2**20),
        cost_estimate=pl.CostEstimate(flops=100_000_000, bytes_accessed=1_000_000, transcendentals=0),
        name="harmonics",
    )(block, jnp.asarray(hi), jnp.asarray(lo), table)


def ring(axis, size, step):
    return functools.partial(
        lax.ppermute, axis_name=axis, perm=[(i, (i + step) % size) for i in range(size)]
    )


def on_device(source, region, skew_shift):
    n_az, n_ax = lax.axis_size("az"), lax.axis_size("ax")
    rad = lax.axis_index("rad")
    up, dn = send_call(source, region)
    (sw,) = call(
        beside_kernel, "beside", [(16, 8, 256)], [], 4, [VMEM, VMEM, pl.BlockSpec(memory_space=pl.ANY)], [VMEM]
    )(source, region, up)
    up = ring("ax", n_ax, 1)(up)
    dn = ring("ax", n_ax, -1)(dn)
    swap = ring("rad", 2, 1)
    sw = swap(sw)
    block, tall = (3, 16, 16, 256), (16, 24, 256)
    kept, flag, sol, res = call(
        inner_kernel,
        "inner",
        [(Kept.planes, 24, 256), (8, 128), block, block],
        [
            (4, *tall),
            (3, *tall),
            (3, *tall),
            block,
            block,
            pltpu.VMEM((16, 16, 256), jnp.int32),
            pltpu.SemaphoreType.DMA((4,)),
        ],
        16,
        [HBM, HBM, VMEM],
        [VMEM, VMEM, HBM, HBM],
    )(source, region, sw)
    start, flag = lax.optimization_barrier((8 * (1 - rad), flag))
    sw2 = swap(lax.dynamic_slice_in_dim(jnp.concatenate([up, dn], axis=0), start, 8, axis=1))
    stress, rim, az_up, az_dn = call(
        rim_kernel,
        "rim",
        [(16, 8, 384), (Rim.planes, 24, 256), (2, 24, 128), (2, 24, 128)],
        [(4, 8, 24, 256), (16, 8, 384), pltpu.SemaphoreType.DMA((1,))],
        8,
        [VMEM] * 4 + [pl.BlockSpec(memory_space=pl.ANY)],
        [HBM, VMEM, VMEM, VMEM],
    )(kept, up, dn, sw2, flag)
    circle = lax.all_to_all(stress, "az", split_axis=0, concat_axis=0, tiled=True)
    from_left = ring("az", n_az, 1)(az_up)
    from_right = ring("az", n_az, -1)(az_dn)
    sol, res, table = call(
        edge_kernel, "edge", [block, block, (2, 16, MH)], [], 8, [SMEM] + [VMEM] * 4, [VMEM] * 3
    )(skew_shift, kept, rim, sol, res)
    solution, residual = seam_call(rim, sol, res, from_left, from_right)
    harmonics = harmonics_call(circle, table)
    return (solution, residual, harmonics)


def solution(mesh):
    in_specs = (P(None, "ax", "rad", "az"), P("ax", "rad", "az"), P("ax"))
    out_specs = (
        P(None, "ax", "rad", "az"),
        P(None, "ax", "rad", "az"),
        P(None, ("ax", "az"), "rad", None),
    )
    return jax.shard_map(
        on_device, mesh=mesh, in_specs=in_specs, out_specs=out_specs, check_vma=False
    )
```

```python
import functools
import math

import jax
import jax.numpy as jnp
import numpy as np
from jax import lax
from jax.experimental import pallas as pl
from jax.experimental.pallas import tpu as pltpu
from jax.sharding import PartitionSpec as P

NA = 4096
MH = 256
F32 = jnp.float32

cheb_center = 7.1
cheb_radius = 6.9
ratio_sigma = cheb_center / cheb_radius
rho_first = 1.0 / ratio_sigma
rho_second = 1.0 / (2.0 * ratio_sigma - rho_first)
keep_weight = rho_second * rho_first
fresh_weight = 2.0 * rho_second / cheb_radius

FIRST = 1.0 / cheb_center
SECOND_SRC = keep_weight / cheb_center + fresh_weight
SECOND_A = fresh_weight / cheb_center
SUM_SRC = FIRST + SECOND_SRC

VMEM = pl.BlockSpec(memory_space=pltpu.VMEM)
SMEM = pl.BlockSpec(memory_space=pltpu.SMEM)
HBM = pl.BlockSpec(memory_space=pltpu.HBM)

UNROLL = 2
SEND_KIB = 54656


def materials(code):
    iron, magnet, outside = code == 1.0, code == 2.0, code < 0.0
    reluct = jnp.where(iron, 0.05, jnp.where(magnet, 0.95, jnp.where(outside, 0.0, 1.0)))
    mass = jnp.where(
        iron,
        1.5,
        jnp.where(magnet, 0.6, jnp.where(outside, 0.0, jnp.where(code == 0.0, 0.2, 2.0))),
    )
    return reluct.astype(F32), mass.astype(F32)


def roll(x, shift, axis):
    return pltpu.roll(x, shift % x.shape[axis], axis)


def from_partner(shape, core):
    sub = lax.broadcasted_iota(jnp.int32, shape, len(shape) - 2)
    return (sub >= 6 * core) & (sub < 6 * core + 2)


class Kept:
    planes = 48
    of_field, of_step, of_res = (0, 1, 13, 14, 15), (1, 2, 13, 14), (1, 14)

    def field(self, c, z):
        return 5 * c + self.of_field.index(z)

    def step(self, c, z):
        return 20 + 4 * c + self.of_step.index(z)

    def res(self, c, z):
        return (32 + 2 * c + self.of_res.index(z), slice(0, 16))

    def strips(self, c, side):
        return (38 + c, slice(None), slice(128 * side, 128 * side + 128))

    def stress(self, z):
        return (42 + z // 3, slice(8 * (z % 3), 8 * (z % 3) + 8))


class Rim:
    planes = 12 + 6 + 4 + 1

    def step(self, c, z):
        return 4 * c + (-1, 0, 15, 16).index(z)

    def res(self, c, z):
        return (12 + 2 * c + (0, 15).index(z), slice(0, 16))

    def strips(self, c, side):
        return (18 + c, slice(None), slice(128 * side, 128 * side + 128))

    code = 22


KEPT, RIM = Kept(), Rim()


def gap_tile(x, core):
    return jnp.where(core == 1, x[0:8], x[8:16])


def loop(first, last, body, unroll):
    rounds = (last - first) // unroll

    def several(t, carry):
        for k in range(unroll):
            body(first + t * unroll + k)
        return carry

    lax.fori_loop(0, rounds, several, 0)
    for k in range(first + rounds * unroll, last):
        body(k)


def curl(v0, v1, v2, v0a, v1a, v0r, v2r, v1n, v2n):
    return (
        (v2r - v2) - (v1a - v1),
        (v0a - v0) - (v2n - v2),
        (v1n - v1) - (v0r - v0),
    )


def strength(v0, v1, v2, v1n, v2n, reluct):
    c0, c1, c2 = curl(
        v0, v1, v2, roll(v0, -1, 1), roll(v1, -1, 1), roll(v0, -1, 0), roll(v2, -1, 0), v1n, v2n
    )
    return reluct * c0, reluct * c1, reluct * c2


def image(v, h, h1p, h2p, mass):
    h0, h1, h2 = h
    return (
        (h2 - roll(h2, 1, 0)) - (h1 - roll(h1, 1, 1)) + mass * v[0],
        (h0 - roll(h0, 1, 1)) - (h2 - h2p) + mass * v[1],
        (h1 - h1p) - (h0 - roll(h0, 1, 0)) + mass * v[2],
    )


def second_of(v, a, mass):
    return [jnp.where(mass > 0.0, SECOND_SRC * v[c] - SECOND_A * a[c], 0.0) for c in range(3)]


def fluxes(u0, u1, u2, u1n, u2n):
    return (roll(u0, -1, 1) - u0) - (u2n - u2), (u1n - u1) - (roll(u0, -1, 0) - u0)


def stress_of(u0, u1, u2, u1n, u2n, core):
    flux1, flux2 = fluxes(u0, u1, u2, u1n, u2n)
    flux1, flux2 = gap_tile(flux1, core), gap_tile(flux2, core)
    return 0.5 * (flux1 * flux1 - flux2 * flux2)


def pack_plane(rights, lefts, x, i, lane):
    here = (lane >= 6 * i) & (lane < 6 * i + 6)
    right = jnp.where(here, roll(x[:, 128:], 6 * i + 4, 1), rights)
    left = jnp.where(here, roll(x[:, :128], 6 * i + 2, 1), lefts)
    return right, left


def send_kernel(src, reg, up, dn, sw, rows, ids, tiles, sems):
    core = lax.axis_index("rad")
    tile = pl.ds(pl.multiple_of(8 * (1 - core), 8), 8)
    pairs = [(reg.at[:, tile, :], ids)]
    for c in range(3):
        pairs.append((src.at[c, :, tile, :], tiles.at[c]))
    later = [
        (reg.at[14:16], rows.at[0:2]),
        (reg.at[0], rows.at[2]),
        (src.at[1, 1], dn.at[4]),
        (src.at[2, 1], dn.at[5]),
    ]
    for c in range(3):
        later.append((src.at[c, 14:16], up.at[2 * c : 2 * c + 2]))
        later.append((src.at[c, 0], dn.at[c]))
    copies = [
        pltpu.make_async_copy(x, y, sems.at[n]) for n, (x, y) in enumerate(pairs + later)
    ]
    for copy in copies:
        copy.start()
    for copy in copies[:4]:
        copy.wait()
    sub = lax.broadcasted_iota(jnp.int32, (16, 8, 256), 1) >> 1
    packed = jnp.zeros((16, 8, 256), F32)
    for c in range(4):
        x = tiles[c] if c < 3 else ids[...].astype(F32)
        first = pltpu.roll(x, 2 * c, 1) if c else x
        last = pltpu.roll(x, (2 * c + 2) % 8, 1) if c < 3 else x
        packed = jnp.where(sub == c, jnp.where(core == 1, first, last), packed)
    sw[...] = packed
    for copy in copies[4:]:
        copy.wait()
    up[6:8] = rows[0:2].astype(F32)
    dn[3] = rows[2].astype(F32)


def send_call(src, reg):
    shapes = [(8, 16, 256), (6, 16, 256), (16, 8, 256)]
    return pl.pallas_call(
        send_kernel,
        out_shape=[jax.ShapeDtypeStruct(shape, F32) for shape in shapes],
        in_specs=[HBM, HBM],
        out_specs=[VMEM] * 3,
        scratch_shapes=[
            pltpu.VMEM((3, 16, 256), jnp.int32),
            pltpu.VMEM((16, 8, 256), jnp.int32),
            pltpu.VMEM((3, 16, 8, 256), F32),
            pltpu.SemaphoreType.DMA((14,)),
        ],
        compiler_params=pltpu.CompilerParams(vmem_limit_bytes=SEND_KIB * 2**10),
        name="send",
    )(src, reg)


def partner_rows(packed, c, core):
    first = roll(packed, -2 * c, 0) if c else packed
    last = roll(packed, 6 - 2 * c, 0) if c < 3 else packed
    return jnp.where(core == 1, last, first)


def call(kernel, name, outs, scratch, limit, in_specs, out_specs):
    return pl.pallas_call(
        kernel,
        out_shape=[
            pltpu.HBM(shape, F32) if spec is HBM else jax.ShapeDtypeStruct(shape, F32)
            for shape, spec in zip(outs, out_specs)
        ],
        in_specs=in_specs,
        out_specs=out_specs,
        scratch_shapes=[pltpu.VMEM(x, F32) if isinstance(x, tuple) else x for x in scratch],
        compiler_params=pltpu.CompilerParams(vmem_limit_bytes=limit * 2**20),
        cost_estimate=pl.CostEstimate(flops=10_000_000, bytes_accessed=2_000_000, transcendentals=0),
        name=name,
    )


def inner_kernel(src, reg, sw, kept, sol_out, res_out, field, s, hh, sol, res, ids, sems):
    core = lax.axis_index("rad")
    pick = from_partner((8, 256), core)
    lane = lax.broadcasted_iota(jnp.int32, (24, 128), 1)
    copies = [pltpu.make_async_copy(src.at[c], field.at[c, :, 0:16, :], sems.at[c]) for c in range(3)]
    copies.append(pltpu.make_async_copy(reg, ids, sems.at[3]))
    for copy in copies:
        copy.start()
    for copy in copies:
        copy.wait()

    def assemble(z):
        for c in range(4):
            rows = partner_rows(sw[z], c, core)
            field[c, z, 16:24, :] = jnp.where(pick, rows, 0.0 if c < 3 else -1.0)
        field[3, z, 0:16, :] = ids[z].astype(F32)

    loop(0, 16, assemble, 4)

    def vec(z):
        return [field[c, z] for c in range(3)]

    def first_h(z):
        reluct, _ = materials(field[3, z])
        h = strength(*vec(z), field[1, z + 1], field[2, z + 1], reluct)
        for c in range(3):
            hh[c, z] = h[c]

    loop(0, 15, first_h, UNROLL)

    def first_a(z):
        v = vec(z)
        _, mass = materials(field[3, z])
        a = image(v, [hh[c, z] for c in range(3)], hh[1, z - 1], hh[2, z - 1], mass)
        step = second_of(v, a, mass)
        for c in range(3):
            s[c, z] = step[c]
            res[c, z] = (v[c] - FIRST * a[c])[:16]
            sol[c, z] = (FIRST * v[c] + step[c])[:16]

    loop(1, 15, first_a, UNROLL)

    copies = [pltpu.make_async_copy(sol, sol_out, sems.at[0])]
    copies[0].start()

    def stress_plane(z):
        u0, u1, u2 = [FIRST * field[c, z] + s[c, z] for c in range(3)]
        u1n, u2n = [FIRST * field[c, z + 1] + s[c, z + 1] for c in (1, 2)]
        kept[KEPT.stress(z)] = stress_of(u0, u1, u2, u1n, u2n, core)

    for z in range(1, 14):
        stress_plane(z)

    def second_h(z):
        reluct, _ = materials(field[3, z])
        h = strength(s[0, z], s[1, z], s[2, z], s[1, z + 1], s[2, z + 1], reluct)
        for c in range(3):
            hh[c, z] = h[c]

    loop(1, 14, second_h, UNROLL)

    def second_a(z):
        _, mass = materials(field[3, z])
        v = [s[c, z] for c in range(3)]
        a = image(v, [hh[c, z] for c in range(3)], hh[1, z - 1], hh[2, z - 1], mass)
        for c in range(3):
            res[c, z] = res[c, z] - a[c][:16]

    loop(2, 14, second_a, UNROLL)
    copies.append(pltpu.make_async_copy(res, res_out, sems.at[1]))
    copies[1].start()
    for c in range(3):
        for z in KEPT.of_step:
            kept[KEPT.step(c, z)] = s[c, z]
        for z in KEPT.of_res:
            kept[KEPT.res(c, z)] = res[c, z]
    for c in range(4):
        for z in KEPT.of_field:
            kept[KEPT.field(c, z)] = field[c, z]

    for c in range(4):
        right = left = jnp.full((24, 128), 0.0 if c < 3 else -1.0, F32)
        for z in range(16):
            right, left = pack_plane(right, left, field[c, z], z + 2, lane)
        kept[KEPT.strips(c, 0)] = right
        kept[KEPT.strips(c, 1)] = left

    for copy in copies:
        copy.wait()


def rim_kernel(kept, up, dn, hbm, az_up, az_dn, rim, w, out, up_msg, dn_msg, sem):
    core, ax = lax.axis_index("rad"), lax.axis_index("ax")
    lo = jnp.where(ax > 0, 1.0, 0.0)
    hi = jnp.where(ax < lax.axis_size("ax") - 1, 1.0, 0.0)
    pick = from_partner((8, 256), core)
    for c in range(4):
        empty = 0.0 if c < 3 else -1.0

        def put(i, value, beside, valid):
            w[c, i, 0:16, :] = (value - empty) * valid + empty
            w[c, i, 16:24, :] = jnp.where(pick, (beside - empty) * valid + empty, empty)

        put(0, up[2 * c], partner_rows(up[8, 0:8], c, core), lo)
        put(1, up[2 * c + 1], partner_rows(up[8, 8:16], c, core), lo)
        put(6, dn[c], partner_rows(dn[6, 0:8], c, core), hi)
        if c in (1, 2):
            put(7, dn[3 + c], partner_rows(dn[6, 8:16], c, core), hi)
        else:
            w[c, 7] = jnp.full((24, 256), empty, F32)
        w[c, 2] = kept[KEPT.field(c, 0)]
        w[c, 3] = kept[KEPT.field(c, 1)]
        w[c, 4] = kept[KEPT.field(c, 14)]
        w[c, 5] = kept[KEPT.field(c, 15)]

    def vec(i):
        return [w[c, i] for c in range(3)]

    def h_of(i, reluct):
        return strength(*vec(i), w[1, i + 1], w[2, i + 1], reluct)

    def rims(i, zs):
        _, h1, h2 = h_of(i, materials(w[3, i])[0])
        steps = []
        for n in range(2):
            reluct, mass = materials(w[3, i + 1 + n])
            h = h_of(i + 1 + n, reluct)
            v = vec(i + 1 + n)
            a = image(v, h, h1, h2, mass)
            h1, h2 = h[1], h[2]
            step = second_of(v, a, mass)
            for c in range(3):
                rim[RIM.step(c, zs[n])] = step[c]
                if zs[n] in (0, 15):
                    rim[RIM.res(c, zs[n])] = (v[c] - FIRST * a[c])[:16]
            steps.append([FIRST * v[c] + step[c] for c in range(3)])
        return steps

    rim[RIM.code] = w[3, 1]
    _, u_first = rims(0, (-1, 0))
    u_last, u_after = rims(4, (15, 16))
    u_one = [FIRST * w[c, 3] + kept[KEPT.step(c, 1)] for c in range(3)]
    u_14 = [FIRST * w[c, 4] + kept[KEPT.step(c, 14)] for c in range(3)]
    for z in range(1, 14):
        out[z, :, 0:256] = kept[KEPT.stress(z)]
    out[0, :, 0:256] = stress_of(*u_first, u_one[1], u_one[2], core)
    out[14, :, 0:256] = stress_of(*u_14, u_last[1], u_last[2], core)
    out[15, :, 0:256] = stress_of(*u_last, u_after[1], u_after[2], core)
    main, last = [slice(0, 256), slice(256, 384)]
    copies = [pltpu.make_async_copy(out.at[:, :, main], hbm.at[:, :, main], sem.at[0])]
    copies[0].start()

    lane = lax.broadcasted_iota(jnp.int32, (24, 128), 1)
    plane = (lane * 43) >> 8
    k = lane - 6 * plane
    right, left = [], []
    for c in range(4):
        r, l = kept[KEPT.strips(c, 0)], kept[KEPT.strips(c, 1)]
        for i, n in ((0, 0), (1, 1), (18, 6), (19, 7)):
            r, l = pack_plane(r, l, w[c, n], i, lane)
        empty = 0.0 if c < 3 else -1.0
        r = jnp.where(k < 4, r, empty)
        l = jnp.where(k > 1, l, empty)
        rim[RIM.strips(c, 0)] = r
        rim[RIM.strips(c, 1)] = l
        right.append(r)
        left.append(l)
    for msg, x in ((up_msg, right), (dn_msg, left)):
        msg[0] = jnp.where(
            k < 2, roll(x[2], -2, 1), jnp.where(k < 4, x[0], roll(x[1], 2, 1))
        )
        msg[1] = x[3]
    copies.append(pltpu.make_async_copy(up_msg, az_up, sem.at[1]))
    copies.append(pltpu.make_async_copy(dn_msg, az_dn, sem.at[2]))
    copies[1].start()
    copies[2].start()

    f = SECOND_A

    def partial(x):
        reluct, mass = materials(x[3])
        v = x[:3]
        h = strength(*v, roll(v[1], -6, 1), roll(v[2], -6, 1), reluct)
        a = image(v, h, roll(h[1], 6, 1), roll(h[2], 6, 1), mass)
        step = second_of(v, a, mass)
        u = [FIRST * v[c] + step[c] for c in range(3)]
        return reluct, h, u, fluxes(*u, roll(u[1], -6, 1), roll(u[2], -6, 1))

    reluct, (h0, h1, _), _, (flux1, flux2) = partial(right)
    fh1 = f * h1
    rest = f * ((roll(h0, -6, 1) - h0) + (roll(h1, -1, 0) - h1))
    rel_up, rel_dn = f * roll(reluct, -1, 0), f * roll(reluct, 1, 0)
    a_part = jnp.where(
        k < 2,
        roll(jnp.where(k == 3, flux1 - fh1, flux1), -2, 1),
        jnp.where(k == 2, roll(fh1, -1, 1), jnp.where(k < 5, roll(flux2, 1, 1), roll(rest, 2, 1))),
    )
    x_part = jnp.where(
        k == 1,
        -roll(rel_dn, -8, 1),
        jnp.where(k == 4, -roll(rel_up, 1, 1), jnp.where(k == 5, roll(rel_up, 2, 1), 0.0)),
    )
    z_part = jnp.where(k == 1, roll(rel_dn, -2, 1), 0.0)

    _, _, u, (flux1, flux2) = partial(left)
    v0, v1 = left[0], left[1]
    v1n = roll(v1, -6, 1)
    v1_dn = roll(v1, 1, 0)
    v0_up = roll(v0, -1, 0)
    inside = jnp.where(plane == 17, hi, 1.0)
    r_a = u[0] + f * ((roll(v0, -6, 1) + roll(v0, 6, 1)) - (3.0 + inside) * v0 + (v1n - v1))
    r_b = f * ((v1n - v1) + v0)
    b_part = jnp.where(
        k == 0,
        roll(f * v0, -2, 1),
        jnp.where(
            k == 1,
            roll(r_a, -1, 1),
            jnp.where(
                k == 2,
                flux1 + f * v0,
                jnp.where(k == 4, roll(r_b, 2, 1), jnp.where(k == 5, roll(flux2 - r_b, 3, 1), 0.0)),
            ),
        ),
    )
    y_part = jnp.where(
        k == 1, roll(v1_dn, -7, 1), jnp.where(k == 4, roll(v0_up, 2, 1), roll(v0_up, 3, 1))
    )
    w_part = roll(v1_dn, -1, 1)

    lane = lax.broadcasted_iota(jnp.int32, (8, 128), 1)
    parts = [
        roll(gap_tile(x, core), 6 * n, 1) if n else gap_tile(x, core)
        for n, x in enumerate((a_part, x_part, z_part, b_part, y_part, w_part))
    ]
    for z in range(16):
        part = (((lane - 6 * (z + 2)) & 127) * 43) >> 8
        extra = parts[5]
        for n in range(5):
            extra = jnp.where(part == n, parts[n], extra)
        out[z, :, 256:384] = extra
    copies.append(pltpu.make_async_copy(out.at[:, :, last], hbm.at[:, :, last], sem.at[3]))
    copies[3].start()
    for copy in copies:
        copy.wait()


def edge_kernel(skew, kept, rim, sol_in, res_in, sol, out, table):
    offset = 256 * lax.broadcasted_iota(jnp.int32, (16, MH), 0) - skew[lax.axis_index("az")]
    turns = (offset * lax.broadcasted_iota(jnp.int32, (16, MH), 1)) & (NA - 1)
    angle = turns.astype(F32) * (2.0 * math.pi / NA)
    table[0] = jnp.cos(angle)
    table[1] = jnp.sin(angle)

    def step(z, c):
        return rim[RIM.step(c, z)] if z in (-1, 0, 15, 16) else kept[KEPT.step(c, z)]

    def materials_of(z):
        return materials(rim[RIM.code] if z < 0 else kept[KEPT.field(3, z)])

    def h_of(z):
        return strength(
            step(z, 0), step(z, 1), step(z, 2), step(z + 1, 1), step(z + 1, 2), materials_of(z)[0]
        )

    for z in (0, 14):
        _, h1, h2 = h_of(z - 1)
        for n in range(2):
            h = h_of(z + n)
            a = image([step(z + n, c) for c in range(3)], h, h1, h2, materials_of(z + n)[1])
            h1, h2 = h[1], h[2]
            for c in range(3):
                x = z + n
                before = rim[RIM.res(c, x)] if x in (0, 15) else kept[KEPT.res(c, x)]
                out[c, x] = before - a[c][:16]
    for c in range(3):
        out[c, 2:14] = res_in[c, 2:14]
        sol[c, 1:15] = sol_in[c, 1:15]
        for z in (0, 15):
            sol[c, z] = FIRST * kept[KEPT.field(c, z)][:16] + rim[RIM.step(c, z)][:16]


def seam_kernel(rim, sol_in, res_in, from_left, from_right, sol, res, a_sol, a_res, sems):
    lane = lax.broadcasted_iota(jnp.int32, (24, 128), 1)
    plane = (lane * 43) >> 8
    k = lane - 6 * plane

    def full(x, msg, halo, shifts):
        return [
            jnp.where(halo, roll(msg[t], shift, 1) if shift else msg[t], x[c])
            for c, (t, shift) in enumerate(zip((0, 0, 0, 1), shifts))
        ]

    def solve(x):
        reluct, mass = materials(x[3])
        v = x[:3]
        h = strength(*v, roll(v[1], -6, 1), roll(v[2], -6, 1), reluct)
        a = image(v, h, roll(h[1], 6, 1), roll(h[2], 6, 1), mass)
        step = second_of(v, a, mass)
        h = strength(*step, roll(step[1], -6, 1), roll(step[2], -6, 1), reluct)
        a2 = image(step, h, roll(h[1], 6, 1), roll(h[2], 6, 1), mass)
        return (
            [(FIRST * v[c] + step[c])[:16] for c in range(3)],
            [(v[c] - FIRST * a[c] - a2[c])[:16] for c in range(3)],
        )

    right = solve(full([rim[RIM.strips(c, 0)] for c in range(4)], from_right, k > 3, (2, 0, 4, 2)))
    left = solve(full([rim[RIM.strips(c, 1)] for c in range(4)], from_left, k < 2, (-2, -4, 0, -2)))
    k = k[:16]
    merged = [
        [jnp.where(k < 4, right[n][c], roll(left[n][c], 2, 1)) for c in range(3)] for n in range(2)
    ]
    lane = lax.broadcasted_iota(jnp.int32, (16, 128), 1)
    copies = []
    for z in range(16):
        i = z + 2
        for n, buf in ((0, a_sol), (1, a_res)):
            for c in range(3):
                x = (sol_in, res_in)[n][c, z]
                edge = roll(merged[n][c], 124 - 6 * i, 1)
                buf[z // 4, c, z % 4, :, 0:128] = jnp.where(lane < 2, edge, x[:, :128])
                buf[z // 4, c, z % 4, :, 128:256] = jnp.where(lane >= 126, edge, x[:, 128:])
        if z % 4 == 3:
            t = z // 4
            for n, (buf, dst) in enumerate(((a_sol, sol), (a_res, res))):
                copy = pltpu.make_async_copy(
                    buf.at[t], dst.at[:, pl.ds(4 * t, 4)], sems.at[n, t]
                )
                copy.start()
                copies.append(copy)
    for copy in copies:
        copy.wait()


def seam_call(*args):
    out = jax.ShapeDtypeStruct((3, 16, 16, 256), F32)
    return pl.pallas_call(
        seam_kernel,
        out_shape=[out, out],
        in_specs=[VMEM] * len(args),
        out_specs=[HBM] * 2,
        scratch_shapes=[
            pltpu.VMEM((4, 3, 4, 16, 256), F32),
            pltpu.VMEM((4, 3, 4, 16, 256), F32),
            pltpu.SemaphoreType.DMA((2, 4)),
        ],
        compiler_params=pltpu.CompilerParams(vmem_limit_bytes=12 * 2**20),
        cost_estimate=pl.CostEstimate(flops=4_000_000, bytes_accessed=4_000_000, transcendentals=0),
        name="seams",
    )(*args)


def harmonics_kernel(block, basis_hi, basis_lo, table, out):
    lane = lax.broadcasted_iota(jnp.int32, (16, 8, 128), 2)
    seam = block[:, :, 256:384]
    right = jnp.concatenate([seam[1:], seam[:1]], axis=0).reshape(128, 128)
    first = 6 * (lax.axis_index("az") + 2)
    right = pltpu.roll(right, lax.rem(256 - first - 18, 128), 1)
    seam = pltpu.roll(seam.reshape(128, 128), lax.rem(256 - first, 128), 1)
    product = seam * right
    flux = seam + right + roll(product, -6, 1) + roll(product, -12, 1)
    square = 0.5 * (flux * flux)
    fixed = roll(square - roll(square, -3, 1), -2, 1).reshape(16, 8, 128)
    moved = jnp.concatenate([fixed[15:], fixed[:15]], axis=0)
    low = jnp.where(lane == 0, moved, block[:, :, 0:128])
    high = jnp.where(lane >= 126, fixed, block[:, :, 128:256])
    x = jnp.concatenate([low.reshape(128, 128), high.reshape(128, 128)], axis=1)
    x_hi = x.astype(jnp.bfloat16)
    x_lo = (x - x_hi.astype(F32)).astype(jnp.bfloat16)

    def dot(a, b):
        return jnp.dot(a, b[...], preferred_element_type=F32)

    both = dot(jnp.concatenate([x_hi, x_lo], axis=0), basis_hi)
    local = both[:128] + (both[128:] + dot(x_hi, basis_lo))
    local = local.reshape(16, 8, 2 * MH)
    real = jnp.zeros((8, MH), F32)
    imag = jnp.zeros((8, MH), F32)
    for j in range(16):
        c, s = table[0, j : j + 1, :], table[1, j : j + 1, :]
        pc, ps = local[j, :, :MH], local[j, :, MH:]
        real = real + (pc * c - ps * s)
        imag = imag - (pc * s + ps * c)
    out[0, 0] = real
    out[1, 0] = imag


def harmonics_call(block, table):
    turns = np.arange(256)[:, None] * np.arange(MH)[None, :] / NA
    angle = 2.0 * math.pi * turns
    basis = np.concatenate([np.cos(angle), np.sin(angle)], axis=1) / math.sqrt(NA)
    hi = basis.astype(jnp.bfloat16)
    lo = (basis - hi.astype(np.float64)).astype(jnp.bfloat16)
    return pl.pallas_call(
        harmonics_kernel,
        out_shape=jax.ShapeDtypeStruct((2, 1, 8, MH), F32),
        in_specs=[VMEM] * 4,
        out_specs=VMEM,
        compiler_params=pltpu.CompilerParams(vmem_limit_bytes=8 * 2**20),
        cost_estimate=pl.CostEstimate(flops=100_000_000, bytes_accessed=1_000_000, transcendentals=0),
        name="harmonics",
    )(block, jnp.asarray(hi), jnp.asarray(lo), table)


def ring(axis, size, step):
    return functools.partial(
        lax.ppermute, axis_name=axis, perm=[(i, (i + step) % size) for i in range(size)]
    )


def on_device(source, region, skew_shift):
    n_az, n_ax = lax.axis_size("az"), lax.axis_size("ax")
    up, dn, sw = send_call(source, region)
    sw = ring("rad", 2, 1)(sw)
    up = ring("ax", n_ax, 1)(jnp.concatenate([up, sw[14:16].reshape(1, 16, 256)], axis=0))
    dn = ring("ax", n_ax, -1)(jnp.concatenate([dn, sw[0:2].reshape(1, 16, 256)], axis=0))
    block, tall = (3, 16, 16, 256), (16, 24, 256)
    kept, sol, res = call(
        inner_kernel,
        "inner",
        [(Kept.planes, 24, 256), block, block],
        [
            (4, *tall),
            (3, *tall),
            (3, *tall),
            block,
            block,
            pltpu.VMEM((16, 16, 256), jnp.int32),
            pltpu.SemaphoreType.DMA((4,)),
        ],
        16,
        [HBM, HBM, VMEM],
        [VMEM, HBM, HBM],
    )(source, region, sw)
    stress, az_up, az_dn, rim = call(
        rim_kernel,
        "rim",
        [(16, 8, 384), (2, 24, 128), (2, 24, 128), (Rim.planes, 24, 256)],
        [
            (4, 8, 24, 256),
            (16, 8, 384),
            (2, 24, 128),
            (2, 24, 128),
            pltpu.SemaphoreType.DMA((4,)),
        ],
        8,
        [VMEM] * 3,
        [HBM, HBM, HBM, VMEM],
    )(kept, up, dn)
    circle = lax.all_to_all(stress, "az", split_axis=0, concat_axis=0, tiled=True)
    from_left = ring("az", n_az, 1)(az_up)
    from_right = ring("az", n_az, -1)(az_dn)
    sol, res, table = call(
        edge_kernel, "edge", [block, block, (2, 16, MH)], [], 8, [SMEM] + [VMEM] * 4, [VMEM] * 3
    )(skew_shift, kept, rim, sol, res)
    solution, residual = seam_call(rim, sol, res, from_left, from_right)
    harmonics = harmonics_call(circle, table)
    return (solution, residual, harmonics)


def solution(mesh):
    in_specs = (P(None, "ax", "rad", "az"), P("ax", "rad", "az"), P("ax"))
    out_specs = (
        P(None, "ax", "rad", "az"),
        P(None, "ax", "rad", "az"),
        P(None, ("ax", "az"), "rad", None),
    )
    return jax.shard_map(
        on_device, mesh=mesh, in_specs=in_specs, out_specs=out_specs, check_vma=False
    )
```

```python
import functools
import math

import jax
import jax.numpy as jnp
import numpy as np
from jax import lax
from jax.experimental import pallas as pl
from jax.experimental.pallas import tpu as pltpu
from jax.sharding import PartitionSpec as P

NA = 4096
MH = 256
F32 = jnp.float32

cheb_center = 7.1
cheb_radius = 6.9
ratio_sigma = cheb_center / cheb_radius
rho_first = 1.0 / ratio_sigma
rho_second = 1.0 / (2.0 * ratio_sigma - rho_first)
keep_weight = rho_second * rho_first
fresh_weight = 2.0 * rho_second / cheb_radius

FIRST = 1.0 / cheb_center
SECOND_SRC = keep_weight / cheb_center + fresh_weight
SECOND_A = fresh_weight / cheb_center
SUM_SRC = FIRST + SECOND_SRC

VMEM = pl.BlockSpec(memory_space=pltpu.VMEM)
SMEM = pl.BlockSpec(memory_space=pltpu.SMEM)
HBM = pl.BlockSpec(memory_space=pltpu.HBM)

UNROLL = 2
SEND_KIB = 54656


def materials(code):
    iron, magnet, outside = code == 1.0, code == 2.0, code < 0.0
    reluct = jnp.where(iron, 0.05, jnp.where(magnet, 0.95, jnp.where(outside, 0.0, 1.0)))
    mass = jnp.where(
        iron,
        1.5,
        jnp.where(magnet, 0.6, jnp.where(outside, 0.0, jnp.where(code == 0.0, 0.2, 2.0))),
    )
    return reluct.astype(F32), mass.astype(F32)


def roll(x, shift, axis):
    return pltpu.roll(x, shift % x.shape[axis], axis)


def from_partner(shape, core):
    sub = lax.broadcasted_iota(jnp.int32, shape, len(shape) - 2)
    return (sub >= 6 * core) & (sub < 6 * core + 2)


class Kept:
    planes = 53
    of_field, of_step, of_res = (0, 1, 13, 14, 15), (1, 2, 13, 14), (1, 14)

    def field(self, c, z):
        return 5 * c + self.of_field.index(z)

    def step(self, c, z):
        return 20 + 4 * c + self.of_step.index(z)

    def res(self, c, z):
        return (32 + 2 * c + self.of_res.index(z), slice(0, 16))

    def strips(self, c, side):
        return (38 + c, slice(None), slice(128 * side, 128 * side + 128))

    def stress(self, z):
        return (42 + z // 3, slice(8 * (z % 3), 8 * (z % 3) + 8))

    def strength(self, c, z):
        return 48 + c if z == 0 else 50 + c


class Rim:
    planes = 9 + 6 + 4 + 8

    def step(self, c, z):
        return 3 * c + (0, 15, 16).index(z)

    def res(self, c, z):
        return (9 + 2 * c + (0, 15).index(z), slice(0, 16))

    def strips(self, c, side):
        return (15 + c, slice(None), slice(128 * side, 128 * side + 128))

    def field(self, c, z):
        return 19 + 2 * c + (-2, -1).index(z)


KEPT, RIM = Kept(), Rim()


def gap_tile(x, core):
    return jnp.where(core == 1, x[0:8], x[8:16])


def loop(first, last, body, unroll):
    rounds = (last - first) // unroll

    def several(t, carry):
        for k in range(unroll):
            body(first + t * unroll + k)
        return carry

    lax.fori_loop(0, rounds, several, 0)
    for k in range(first + rounds * unroll, last):
        body(k)


def curl(v0, v1, v2, v0a, v1a, v0r, v2r, v1n, v2n):
    return (
        (v2r - v2) - (v1a - v1),
        (v0a - v0) - (v2n - v2),
        (v1n - v1) - (v0r - v0),
    )


def strength(v0, v1, v2, v1n, v2n, reluct):
    c0, c1, c2 = curl(
        v0, v1, v2, roll(v0, -1, 1), roll(v1, -1, 1), roll(v0, -1, 0), roll(v2, -1, 0), v1n, v2n
    )
    return reluct * c0, reluct * c1, reluct * c2


def image(v, h, h1p, h2p, mass):
    h0, h1, h2 = h
    return (
        (h2 - roll(h2, 1, 0)) - (h1 - roll(h1, 1, 1)) + mass * v[0],
        (h0 - roll(h0, 1, 1)) - (h2 - h2p) + mass * v[1],
        (h1 - h1p) - (h0 - roll(h0, 1, 0)) + mass * v[2],
    )


def second_of(v, a, mass):
    return [jnp.where(mass > 0.0, SECOND_SRC * v[c] - SECOND_A * a[c], 0.0) for c in range(3)]


def fluxes(u0, u1, u2, u1n, u2n):
    return (roll(u0, -1, 1) - u0) - (u2n - u2), (u1n - u1) - (roll(u0, -1, 0) - u0)


def stress_of(u0, u1, u2, u1n, u2n, core):
    flux1, flux2 = fluxes(u0, u1, u2, u1n, u2n)
    flux1, flux2 = gap_tile(flux1, core), gap_tile(flux2, core)
    return 0.5 * (flux1 * flux1 - flux2 * flux2)


def pack_plane(rights, lefts, x, i, lane):
    here = (lane >= 6 * i) & (lane < 6 * i + 6)
    right = jnp.where(here, roll(x[:, 128:], 6 * i + 4, 1), rights)
    left = jnp.where(here, roll(x[:, :128], 6 * i + 2, 1), lefts)
    return right, left


def send_kernel(src, reg, up, dn, sw, rows, ids, tiles, sems):
    core = lax.axis_index("rad")
    tile = pl.ds(pl.multiple_of(8 * (1 - core), 8), 8)
    pairs = [(reg.at[:, tile, :], ids)]
    for c in range(3):
        pairs.append((src.at[c, :, tile, :], tiles.at[c]))
    later = [
        (reg.at[14:16], rows.at[0:2]),
        (reg.at[0], rows.at[2]),
        (src.at[1, 1], dn.at[4]),
        (src.at[2, 1], dn.at[5]),
    ]
    for c in range(3):
        later.append((src.at[c, 14:16], up.at[2 * c : 2 * c + 2]))
        later.append((src.at[c, 0], dn.at[c]))
    copies = [
        pltpu.make_async_copy(x, y, sems.at[n]) for n, (x, y) in enumerate(pairs + later)
    ]
    for copy in copies:
        copy.start()
    for copy in copies[:4]:
        copy.wait()
    sub = lax.broadcasted_iota(jnp.int32, (16, 8, 256), 1) >> 1
    packed = jnp.zeros((16, 8, 256), F32)
    for c in range(4):
        x = tiles[c] if c < 3 else ids[...].astype(F32)
        first = pltpu.roll(x, 2 * c, 1) if c else x
        last = pltpu.roll(x, (2 * c + 2) % 8, 1) if c < 3 else x
        packed = jnp.where(sub == c, jnp.where(core == 1, first, last), packed)
    sw[...] = packed
    for copy in copies[4:]:
        copy.wait()
    up[6:8] = rows[0:2].astype(F32)
    dn[3] = rows[2].astype(F32)


def send_call(src, reg):
    shapes = [(8, 16, 256), (6, 16, 256), (16, 8, 256)]
    return pl.pallas_call(
        send_kernel,
        out_shape=[jax.ShapeDtypeStruct(shape, F32) for shape in shapes],
        in_specs=[HBM, HBM],
        out_specs=[VMEM] * 3,
        scratch_shapes=[
            pltpu.VMEM((3, 16, 256), jnp.int32),
            pltpu.VMEM((16, 8, 256), jnp.int32),
            pltpu.VMEM((3, 16, 8, 256), F32),
            pltpu.SemaphoreType.DMA((14,)),
        ],
        compiler_params=pltpu.CompilerParams(vmem_limit_bytes=SEND_KIB * 2**10),
        name="send",
    )(src, reg)


def partner_rows(packed, c, core):
    first = roll(packed, -2 * c, 0) if c else packed
    last = roll(packed, 6 - 2 * c, 0) if c < 3 else packed
    return jnp.where(core == 1, last, first)


def call(kernel, name, outs, scratch, limit, in_specs, out_specs):
    return pl.pallas_call(
        kernel,
        out_shape=[
            pltpu.HBM(shape, F32) if spec is HBM else jax.ShapeDtypeStruct(shape, F32)
            for shape, spec in zip(outs, out_specs)
        ],
        in_specs=in_specs,
        out_specs=out_specs,
        scratch_shapes=[pltpu.VMEM(x, F32) if isinstance(x, tuple) else x for x in scratch],
        compiler_params=pltpu.CompilerParams(vmem_limit_bytes=limit * 2**20),
        cost_estimate=pl.CostEstimate(flops=10_000_000, bytes_accessed=2_000_000, transcendentals=0),
        name=name,
    )


def inner_kernel(src, reg, sw, kept, flag, sol_out, res_out, field, s, hh, sol, res, ids, sems):
    flag[...] = jnp.zeros((8, 128), F32)
    core = lax.axis_index("rad")
    pick = from_partner((8, 256), core)
    lane = lax.broadcasted_iota(jnp.int32, (24, 128), 1)
    copies = [pltpu.make_async_copy(src.at[c], field.at[c, :, 0:16, :], sems.at[c]) for c in range(3)]
    copies.append(pltpu.make_async_copy(reg, ids, sems.at[3]))
    for copy in copies:
        copy.start()
    for copy in copies:
        copy.wait()

    def assemble(z):
        for c in range(4):
            rows = partner_rows(sw[z], c, core)
            field[c, z, 16:24, :] = jnp.where(pick, rows, 0.0 if c < 3 else -1.0)
        field[3, z, 0:16, :] = ids[z].astype(F32)

    loop(0, 16, assemble, 4)

    def vec(z):
        return [field[c, z] for c in range(3)]

    def first_h(z):
        reluct, _ = materials(field[3, z])
        h = strength(*vec(z), field[1, z + 1], field[2, z + 1], reluct)
        for c in range(3):
            hh[c, z] = h[c]

    loop(0, 15, first_h, UNROLL)

    def first_a(z):
        v = vec(z)
        _, mass = materials(field[3, z])
        a = image(v, [hh[c, z] for c in range(3)], hh[1, z - 1], hh[2, z - 1], mass)
        step = second_of(v, a, mass)
        for c in range(3):
            s[c, z] = step[c]
            res[c, z] = (v[c] - FIRST * a[c])[:16]
            sol[c, z] = (FIRST * v[c] + step[c])[:16]

    loop(1, 15, first_a, UNROLL)

    copies = [pltpu.make_async_copy(sol, sol_out, sems.at[0])]
    copies[0].start()

    def stress_plane(z):
        u0, u1, u2 = [FIRST * field[c, z] + s[c, z] for c in range(3)]
        u1n, u2n = [FIRST * field[c, z + 1] + s[c, z + 1] for c in (1, 2)]
        kept[KEPT.stress(z)] = stress_of(u0, u1, u2, u1n, u2n, core)

    for z in range(1, 14):
        stress_plane(z)

    def second_h(z):
        reluct, _ = materials(field[3, z])
        h = strength(s[0, z], s[1, z], s[2, z], s[1, z + 1], s[2, z + 1], reluct)
        for c in range(3):
            hh[c, z] = h[c]

    loop(1, 14, second_h, UNROLL)

    def second_a(z):
        _, mass = materials(field[3, z])
        v = [s[c, z] for c in range(3)]
        a = image(v, [hh[c, z] for c in range(3)], hh[1, z - 1], hh[2, z - 1], mass)
        for c in range(3):
            res[c, z] = res[c, z] - a[c][:16]

    loop(2, 14, second_a, UNROLL)
    copies.append(pltpu.make_async_copy(res, res_out, sems.at[1]))
    copies[1].start()
    for c in range(3):
        for z in KEPT.of_step:
            kept[KEPT.step(c, z)] = s[c, z]
        for z in KEPT.of_res:
            kept[KEPT.res(c, z)] = res[c, z]
        kept[KEPT.strength(c, 0)] = hh[c, 0]
        if c > 0:
            kept[KEPT.strength(c, 14)] = hh[c, 14]
    for c in range(4):
        for z in KEPT.of_field:
            kept[KEPT.field(c, z)] = field[c, z]

    for c in range(4):
        right = left = jnp.full((24, 128), 0.0 if c < 3 else -1.0, F32)
        for z in range(16):
            right, left = pack_plane(right, left, field[c, z], z + 2, lane)
        kept[KEPT.strips(c, 0)] = right
        kept[KEPT.strips(c, 1)] = left

    for copy in copies:
        copy.wait()


def rim_kernel(kept, up, sw, dn, _, hbm, az_up, az_dn, rim, w, out, up_msg, dn_msg, sem):
    core, ax = lax.axis_index("rad"), lax.axis_index("ax")
    lo = jnp.where(ax > 0, 1.0, 0.0)
    hi = jnp.where(ax < lax.axis_size("ax") - 1, 1.0, 0.0)
    pick = from_partner((8, 256), core)
    for c in range(4):
        empty = 0.0 if c < 3 else -1.0

        def put(i, value, beside, valid):
            w[c, i, 0:16, :] = (value - empty) * valid + empty
            w[c, i, 16:24, :] = jnp.where(pick, (beside - empty) * valid + empty, empty)

        put(0, up[2 * c], sw[2 * c], lo)
        put(1, up[2 * c + 1], sw[2 * c + 1], lo)
        put(6, dn[c], partner_rows(dn[6, 0:8], c, core), hi)
        if c in (1, 2):
            put(7, dn[3 + c], partner_rows(dn[6, 8:16], c, core), hi)
        else:
            w[c, 7] = jnp.full((24, 256), empty, F32)
        for z in (-2, -1):
            rim[RIM.field(c, z)] = w[c, z + 2]
        w[c, 2] = kept[KEPT.field(c, 0)]
        w[c, 3] = kept[KEPT.field(c, 1)]
        w[c, 4] = kept[KEPT.field(c, 14)]
        w[c, 5] = kept[KEPT.field(c, 15)]

    def vec(i):
        return [w[c, i] for c in range(3)]

    def h_of(i, reluct):
        return strength(*vec(i), w[1, i + 1], w[2, i + 1], reluct)

    def step_of(i, z, h, h1p, h2p):
        v, mass = vec(i), materials(w[3, i])[1]
        a = image(v, h, h1p, h2p, mass)
        step = second_of(v, a, mass)
        for c in range(3):
            rim[RIM.step(c, z)] = step[c]
            if z < 16:
                rim[RIM.res(c, z)] = (v[c] - FIRST * a[c])[:16]
        return [FIRST * v[c] + step[c] for c in range(3)]

    h_before = h_of(1, materials(w[3, 1])[0])
    h_last = h_of(5, materials(w[3, 5])[0])
    h_after = h_of(6, materials(w[3, 6])[0])
    h_zero = [kept[KEPT.strength(c, 0)] for c in range(3)]
    u_first = step_of(2, 0, h_zero, h_before[1], h_before[2])
    u_last = step_of(5, 15, h_last, kept[KEPT.strength(1, 14)], kept[KEPT.strength(2, 14)])
    u_after = step_of(6, 16, h_after, h_last[1], h_last[2])
    u_one = [FIRST * w[c, 3] + kept[KEPT.step(c, 1)] for c in range(3)]
    u_14 = [FIRST * w[c, 4] + kept[KEPT.step(c, 14)] for c in range(3)]
    for z in range(1, 14):
        out[z, :, 0:256] = kept[KEPT.stress(z)]
    out[0, :, 0:256] = stress_of(*u_first, u_one[1], u_one[2], core)
    out[14, :, 0:256] = stress_of(*u_14, u_last[1], u_last[2], core)
    out[15, :, 0:256] = stress_of(*u_last, u_after[1], u_after[2], core)
    main, last = [slice(0, 256), slice(256, 384)]
    copies = [pltpu.make_async_copy(out.at[:, :, main], hbm.at[:, :, main], sem.at[0])]
    copies[0].start()

    lane = lax.broadcasted_iota(jnp.int32, (24, 128), 1)
    plane = (lane * 43) >> 8
    k = lane - 6 * plane
    right, left = [], []
    for c in range(4):
        r, l = kept[KEPT.strips(c, 0)], kept[KEPT.strips(c, 1)]
        for i, n in ((0, 0), (1, 1), (18, 6), (19, 7)):
            r, l = pack_plane(r, l, w[c, n], i, lane)
        empty = 0.0 if c < 3 else -1.0
        r = jnp.where(k < 4, r, empty)
        l = jnp.where(k > 1, l, empty)
        rim[RIM.strips(c, 0)] = r
        rim[RIM.strips(c, 1)] = l
        right.append(r)
        left.append(l)
    for msg, x in ((up_msg, right), (dn_msg, left)):
        msg[0] = jnp.where(
            k < 2, roll(x[2], -2, 1), jnp.where(k < 4, x[0], roll(x[1], 2, 1))
        )
        msg[1] = x[3]
    copies.append(pltpu.make_async_copy(up_msg, az_up, sem.at[1]))
    copies.append(pltpu.make_async_copy(dn_msg, az_dn, sem.at[2]))
    copies[1].start()
    copies[2].start()

    f = SECOND_A

    def partial(x):
        reluct, mass = materials(x[3])
        v = x[:3]
        h = strength(*v, roll(v[1], -6, 1), roll(v[2], -6, 1), reluct)
        a = image(v, h, roll(h[1], 6, 1), roll(h[2], 6, 1), mass)
        step = second_of(v, a, mass)
        u = [FIRST * v[c] + step[c] for c in range(3)]
        return reluct, h, u, fluxes(*u, roll(u[1], -6, 1), roll(u[2], -6, 1))

    reluct, (h0, h1, _), _, (flux1, flux2) = partial(right)
    fh1 = f * h1
    rest = f * ((roll(h0, -6, 1) - h0) + (roll(h1, -1, 0) - h1))
    rel_up, rel_dn = f * roll(reluct, -1, 0), f * roll(reluct, 1, 0)
    a_part = jnp.where(
        k < 2,
        roll(jnp.where(k == 3, flux1 - fh1, flux1), -2, 1),
        jnp.where(k == 2, roll(fh1, -1, 1), jnp.where(k < 5, roll(flux2, 1, 1), roll(rest, 2, 1))),
    )
    x_part = jnp.where(
        k == 1,
        -roll(rel_dn, -8, 1),
        jnp.where(k == 4, -roll(rel_up, 1, 1), jnp.where(k == 5, roll(rel_up, 2, 1), 0.0)),
    )
    z_part = jnp.where(k == 1, roll(rel_dn, -2, 1), 0.0)

    _, _, u, (flux1, flux2) = partial(left)
    v0, v1 = left[0], left[1]
    v1n = roll(v1, -6, 1)
    v1_dn = roll(v1, 1, 0)
    v0_up = roll(v0, -1, 0)
    inside = jnp.where(plane == 17, hi, 1.0)
    r_a = u[0] + f * ((roll(v0, -6, 1) + roll(v0, 6, 1)) - (3.0 + inside) * v0 + (v1n - v1))
    r_b = f * ((v1n - v1) + v0)
    b_part = jnp.where(
        k == 0,
        roll(f * v0, -2, 1),
        jnp.where(
            k == 1,
            roll(r_a, -1, 1),
            jnp.where(
                k == 2,
                flux1 + f * v0,
                jnp.where(k == 4, roll(r_b, 2, 1), jnp.where(k == 5, roll(flux2 - r_b, 3, 1), 0.0)),
            ),
        ),
    )
    y_part = jnp.where(
        k == 1, roll(v1_dn, -7, 1), jnp.where(k == 4, roll(v0_up, 2, 1), roll(v0_up, 3, 1))
    )
    w_part = roll(v1_dn, -1, 1)

    lane = lax.broadcasted_iota(jnp.int32, (8, 128), 1)
    parts = [
        roll(gap_tile(x, core), 6 * n, 1) if n else gap_tile(x, core)
        for n, x in enumerate((a_part, x_part, z_part, b_part, y_part, w_part))
    ]
    for z in range(16):
        part = (((lane - 6 * (z + 2)) & 127) * 43) >> 8
        extra = parts[5]
        for n in range(5):
            extra = jnp.where(part == n, parts[n], extra)
        out[z, :, 256:384] = extra
    copies.append(pltpu.make_async_copy(out.at[:, :, last], hbm.at[:, :, last], sem.at[3]))
    copies[3].start()
    for copy in copies:
        copy.wait()


def edge_kernel(skew, kept, rim, sol_in, res_in, sol, out, table):
    offset = 256 * lax.broadcasted_iota(jnp.int32, (16, MH), 0) - skew[lax.axis_index("az")]
    turns = (offset * lax.broadcasted_iota(jnp.int32, (16, MH), 1)) & (NA - 1)
    angle = turns.astype(F32) * (2.0 * math.pi / NA)
    table[0] = jnp.cos(angle)
    table[1] = jnp.sin(angle)

    v2, v1 = [[rim[RIM.field(c, z)] for c in range(4)] for z in (-2, -1)]
    v0 = [kept[KEPT.field(c, 0)] for c in range(3)]
    rim_code = materials(v1[3])
    _, h1, h2 = strength(*v2[:3], v1[1], v1[2], materials(v2[3])[0])
    h = strength(*v1[:3], v0[1], v0[2], rim_code[0])
    before_first = second_of(v1, image(v1, h, h1, h2, rim_code[1]), rim_code[1])

    def step(z, c):
        if z < 0:
            return before_first[c]
        return rim[RIM.step(c, z)] if z in (0, 15, 16) else kept[KEPT.step(c, z)]

    def materials_of(z):
        return rim_code if z < 0 else materials(kept[KEPT.field(3, z)])

    def h_of(z):
        return strength(
            step(z, 0), step(z, 1), step(z, 2), step(z + 1, 1), step(z + 1, 2), materials_of(z)[0]
        )

    for z in (0, 14):
        _, h1, h2 = h_of(z - 1)
        for n in range(2):
            h = h_of(z + n)
            a = image([step(z + n, c) for c in range(3)], h, h1, h2, materials_of(z + n)[1])
            h1, h2 = h[1], h[2]
            for c in range(3):
                x = z + n
                before = rim[RIM.res(c, x)] if x in (0, 15) else kept[KEPT.res(c, x)]
                out[c, x] = before - a[c][:16]
    for c in range(3):
        out[c, 2:14] = res_in[c, 2:14]
        sol[c, 1:15] = sol_in[c, 1:15]
        for z in (0, 15):
            sol[c, z] = FIRST * kept[KEPT.field(c, z)][:16] + rim[RIM.step(c, z)][:16]


def seam_kernel(rim, sol_in, res_in, from_left, from_right, sol, res, a_sol, a_res, sems):
    lane = lax.broadcasted_iota(jnp.int32, (24, 128), 1)
    plane = (lane * 43) >> 8
    k = lane - 6 * plane

    def full(x, msg, halo, shifts):
        return [
            jnp.where(halo, roll(msg[t], shift, 1) if shift else msg[t], x[c])
            for c, (t, shift) in enumerate(zip((0, 0, 0, 1), shifts))
        ]

    def solve(x):
        reluct, mass = materials(x[3])
        v = x[:3]
        h = strength(*v, roll(v[1], -6, 1), roll(v[2], -6, 1), reluct)
        a = image(v, h, roll(h[1], 6, 1), roll(h[2], 6, 1), mass)
        step = second_of(v, a, mass)
        h = strength(*step, roll(step[1], -6, 1), roll(step[2], -6, 1), reluct)
        a2 = image(step, h, roll(h[1], 6, 1), roll(h[2], 6, 1), mass)
        return (
            [(FIRST * v[c] + step[c])[:16] for c in range(3)],
            [(v[c] - FIRST * a[c] - a2[c])[:16] for c in range(3)],
        )

    right = solve(full([rim[RIM.strips(c, 0)] for c in range(4)], from_right, k > 3, (2, 0, 4, 2)))
    left = solve(full([rim[RIM.strips(c, 1)] for c in range(4)], from_left, k < 2, (-2, -4, 0, -2)))
    k = k[:16]
    merged = [
        [jnp.where(k < 4, right[n][c], roll(left[n][c], 2, 1)) for c in range(3)] for n in range(2)
    ]
    lane = lax.broadcasted_iota(jnp.int32, (16, 128), 1)
    copies = []
    for z in range(16):
        i = z + 2
        for n, buf in ((0, a_sol), (1, a_res)):
            for c in range(3):
                x = (sol_in, res_in)[n][c, z]
                edge = roll(merged[n][c], 124 - 6 * i, 1)
                buf[z // 8, c, z % 8, :, 0:128] = jnp.where(lane < 2, edge, x[:, :128])
                buf[z // 8, c, z % 8, :, 128:256] = jnp.where(lane >= 126, edge, x[:, 128:])
        if z % 8 == 7:
            t = z // 8
            for n, (buf, dst) in enumerate(((a_sol, sol), (a_res, res))):
                copy = pltpu.make_async_copy(
                    buf.at[t], dst.at[:, pl.ds(8 * t, 8)], sems.at[n, t]
                )
                copy.start()
                copies.append(copy)
    for copy in copies:
        copy.wait()


def seam_call(*args):
    out = jax.ShapeDtypeStruct((3, 16, 16, 256), F32)
    return pl.pallas_call(
        seam_kernel,
        out_shape=[out, out],
        in_specs=[VMEM] * len(args),
        out_specs=[HBM] * 2,
        scratch_shapes=[
            pltpu.VMEM((2, 3, 8, 16, 256), F32),
            pltpu.VMEM((2, 3, 8, 16, 256), F32),
            pltpu.SemaphoreType.DMA((2, 2)),
        ],
        compiler_params=pltpu.CompilerParams(vmem_limit_bytes=12 * 2**20),
        cost_estimate=pl.CostEstimate(flops=4_000_000, bytes_accessed=4_000_000, transcendentals=0),
        name="seams",
    )(*args)


def harmonics_kernel(block, basis_hi, basis_lo, table, out):
    lane = lax.broadcasted_iota(jnp.int32, (16, 8, 128), 2)
    seam = block[:, :, 256:384]
    right = jnp.concatenate([seam[1:], seam[:1]], axis=0).reshape(128, 128)
    first = 6 * (lax.axis_index("az") + 2)
    right = pltpu.roll(right, lax.rem(256 - first - 18, 128), 1)
    seam = pltpu.roll(seam.reshape(128, 128), lax.rem(256 - first, 128), 1)
    product = seam * right
    flux = seam + right + roll(product, -6, 1) + roll(product, -12, 1)
    square = 0.5 * (flux * flux)
    fixed = roll(square - roll(square, -3, 1), -2, 1).reshape(16, 8, 128)
    moved = jnp.concatenate([fixed[15:], fixed[:15]], axis=0)
    low = jnp.where(lane == 0, moved, block[:, :, 0:128])
    high = jnp.where(lane >= 126, fixed, block[:, :, 128:256])
    x = jnp.concatenate([low.reshape(128, 128), high.reshape(128, 128)], axis=1)
    x_hi = x.astype(jnp.bfloat16)
    x_lo = (x - x_hi.astype(F32)).astype(jnp.bfloat16)

    def dot(a, b):
        return jnp.dot(a, b[...], preferred_element_type=F32)

    both = dot(jnp.concatenate([x_hi, x_lo], axis=0), basis_hi)
    local = both[:128] + (both[128:] + dot(x_hi, basis_lo))
    local = local.reshape(16, 8, 2 * MH)
    real = jnp.zeros((8, MH), F32)
    imag = jnp.zeros((8, MH), F32)
    for j in range(16):
        c, s = table[0, j : j + 1, :], table[1, j : j + 1, :]
        pc, ps = local[j, :, :MH], local[j, :, MH:]
        real = real + (pc * c - ps * s)
        imag = imag - (pc * s + ps * c)
    out[0, 0] = real
    out[1, 0] = imag


def harmonics_call(block, table):
    turns = np.arange(256)[:, None] * np.arange(MH)[None, :] / NA
    angle = 2.0 * math.pi * turns
    basis = np.concatenate([np.cos(angle), np.sin(angle)], axis=1) / math.sqrt(NA)
    hi = basis.astype(jnp.bfloat16)
    lo = (basis - hi.astype(np.float64)).astype(jnp.bfloat16)
    return pl.pallas_call(
        harmonics_kernel,
        out_shape=jax.ShapeDtypeStruct((2, 1, 8, MH), F32),
        in_specs=[VMEM] * 4,
        out_specs=VMEM,
        compiler_params=pltpu.CompilerParams(vmem_limit_bytes=8 * 2**20),
        cost_estimate=pl.CostEstimate(flops=100_000_000, bytes_accessed=1_000_000, transcendentals=0),
        name="harmonics",
    )(block, jnp.asarray(hi), jnp.asarray(lo), table)


def ring(axis, size, step):
    return functools.partial(
        lax.ppermute, axis_name=axis, perm=[(i, (i + step) % size) for i in range(size)]
    )


def on_device(source, region, skew_shift):
    n_az, n_ax = lax.axis_size("az"), lax.axis_size("ax")
    up, dn, sw = send_call(source, region)
    swap = ring("rad", 2, 1)
    sw = swap(sw)
    up = ring("ax", n_ax, 1)(up)
    dn = ring("ax", n_ax, -1)(jnp.concatenate([dn, sw[0:2].reshape(1, 16, 256)], axis=0))
    block, tall = (3, 16, 16, 256), (16, 24, 256)
    kept, flag, sol, res = call(
        inner_kernel,
        "inner",
        [(Kept.planes, 24, 256), (8, 128), block, block],
        [
            (4, *tall),
            (3, *tall),
            (3, *tall),
            block,
            block,
            pltpu.VMEM((16, 16, 256), jnp.int32),
            pltpu.SemaphoreType.DMA((4,)),
        ],
        16,
        [HBM, HBM, VMEM],
        [VMEM, VMEM, HBM, HBM],
    )(source, region, sw)
    start, flag = lax.optimization_barrier((8 * (1 - lax.axis_index("rad")), flag))
    sw_up = swap(lax.dynamic_slice_in_dim(up, start, 8, axis=1))
    stress, az_up, az_dn, rim = call(
        rim_kernel,
        "rim",
        [(16, 8, 384), (2, 24, 128), (2, 24, 128), (Rim.planes, 24, 256)],
        [
            (4, 8, 24, 256),
            (16, 8, 384),
            (2, 24, 128),
            (2, 24, 128),
            pltpu.SemaphoreType.DMA((4,)),
        ],
        8,
        [VMEM] * 4 + [pl.BlockSpec(memory_space=pl.ANY)],
        [HBM, HBM, HBM, VMEM],
    )(kept, up, sw_up, dn, flag)
    circle = lax.all_to_all(stress, "az", split_axis=0, concat_axis=0, tiled=True)
    from_left = ring("az", n_az, 1)(az_up)
    from_right = ring("az", n_az, -1)(az_dn)
    sol, res, table = call(
        edge_kernel, "edge", [block, block, (2, 16, MH)], [], 8, [SMEM] + [VMEM] * 4, [VMEM] * 3
    )(skew_shift, kept, rim, sol, res)
    solution, residual = seam_call(rim, sol, res, from_left, from_right)
    harmonics = harmonics_call(circle, table)
    return (solution, residual, harmonics)


def solution(mesh):
    in_specs = (P(None, "ax", "rad", "az"), P("ax", "rad", "az"), P("ax"))
    out_specs = (
        P(None, "ax", "rad", "az"),
        P(None, "ax", "rad", "az"),
        P(None, ("ax", "az"), "rad", None),
    )
    return jax.shard_map(
        on_device, mesh=mesh, in_specs=in_specs, out_specs=out_specs, check_vma=False
    )
```

```python
import functools
import math

import jax
import jax.numpy as jnp
import numpy as np
from jax import lax
from jax.experimental import pallas as pl
from jax.experimental.pallas import tpu as pltpu
from jax.sharding import PartitionSpec as P

NA = 4096
MH = 256
F32 = jnp.float32

cheb_center = 7.1
cheb_radius = 6.9
ratio_sigma = cheb_center / cheb_radius
rho_first = 1.0 / ratio_sigma
rho_second = 1.0 / (2.0 * ratio_sigma - rho_first)
keep_weight = rho_second * rho_first
fresh_weight = 2.0 * rho_second / cheb_radius

FIRST = 1.0 / cheb_center
SECOND_SRC = keep_weight / cheb_center + fresh_weight
SECOND_A = fresh_weight / cheb_center
SUM_SRC = FIRST + SECOND_SRC

VMEM = pl.BlockSpec(memory_space=pltpu.VMEM)
SMEM = pl.BlockSpec(memory_space=pltpu.SMEM)
HBM = pl.BlockSpec(memory_space=pltpu.HBM)

UNROLL = 2
SEND_KIB = 54656


def materials(code):
    iron, magnet, outside = code == 1.0, code == 2.0, code < 0.0
    reluct = jnp.where(iron, 0.05, jnp.where(magnet, 0.95, jnp.where(outside, 0.0, 1.0)))
    mass = jnp.where(
        iron,
        1.5,
        jnp.where(magnet, 0.6, jnp.where(outside, 0.0, jnp.where(code == 0.0, 0.2, 2.0))),
    )
    return reluct.astype(F32), mass.astype(F32)


def roll(x, shift, axis):
    return pltpu.roll(x, shift % x.shape[axis], axis)


def from_partner(shape, core):
    sub = lax.broadcasted_iota(jnp.int32, shape, len(shape) - 2)
    return (sub >= 6 * core) & (sub < 6 * core + 2)


class Kept:
    planes = 53
    of_field, of_step, of_res = (0, 1, 13, 14, 15), (1, 2, 13, 14), (1, 14)

    def field(self, c, z):
        return 5 * c + self.of_field.index(z)

    def step(self, c, z):
        return 20 + 4 * c + self.of_step.index(z)

    def res(self, c, z):
        return (32 + 2 * c + self.of_res.index(z), slice(0, 16))

    def strips(self, c, side):
        return (38 + c, slice(None), slice(128 * side, 128 * side + 128))

    def stress(self, z):
        return (42 + z // 3, slice(8 * (z % 3), 8 * (z % 3) + 8))

    def strength(self, c, z):
        return 48 + c if z == 0 else 50 + c


class Rim:
    planes = 9 + 6 + 4 + 8

    def step(self, c, z):
        return 3 * c + (0, 15, 16).index(z)

    def res(self, c, z):
        return (9 + 2 * c + (0, 15).index(z), slice(0, 16))

    def strips(self, c, side):
        return (15 + c, slice(None), slice(128 * side, 128 * side + 128))

    def field(self, c, z):
        return 19 + 2 * c + (-2, -1).index(z)


KEPT, RIM = Kept(), Rim()


def gap_tile(x, core):
    return jnp.where(core == 1, x[0:8], x[8:16])


def loop(first, last, body, unroll):
    rounds = (last - first) // unroll

    def several(t, carry):
        for k in range(unroll):
            body(first + t * unroll + k)
        return carry

    lax.fori_loop(0, rounds, several, 0)
    for k in range(first + rounds * unroll, last):
        body(k)


def curl(v0, v1, v2, v0a, v1a, v0r, v2r, v1n, v2n):
    return (
        (v2r - v2) - (v1a - v1),
        (v0a - v0) - (v2n - v2),
        (v1n - v1) - (v0r - v0),
    )


def strength(v0, v1, v2, v1n, v2n, reluct):
    c0, c1, c2 = curl(
        v0, v1, v2, roll(v0, -1, 1), roll(v1, -1, 1), roll(v0, -1, 0), roll(v2, -1, 0), v1n, v2n
    )
    return reluct * c0, reluct * c1, reluct * c2


def image(v, h, h1p, h2p, mass):
    h0, h1, h2 = h
    return (
        (h2 - roll(h2, 1, 0)) - (h1 - roll(h1, 1, 1)) + mass * v[0],
        (h0 - roll(h0, 1, 1)) - (h2 - h2p) + mass * v[1],
        (h1 - h1p) - (h0 - roll(h0, 1, 0)) + mass * v[2],
    )


def second_of(v, a, mass):
    return [jnp.where(mass > 0.0, SECOND_SRC * v[c] - SECOND_A * a[c], 0.0) for c in range(3)]


def fluxes(u0, u1, u2, u1n, u2n):
    return (roll(u0, -1, 1) - u0) - (u2n - u2), (u1n - u1) - (roll(u0, -1, 0) - u0)


def stress_of(u0, u1, u2, u1n, u2n, core):
    flux1, flux2 = fluxes(u0, u1, u2, u1n, u2n)
    flux1, flux2 = gap_tile(flux1, core), gap_tile(flux2, core)
    return 0.5 * (flux1 * flux1 - flux2 * flux2)


def pack_plane(rights, lefts, x, i, lane):
    here = (lane >= 6 * i) & (lane < 6 * i + 6)
    right = jnp.where(here, roll(x[:, 128:], 6 * i + 4, 1), rights)
    left = jnp.where(here, roll(x[:, :128], 6 * i + 2, 1), lefts)
    return right, left


def send_kernel(src, reg, up, dn, sw, rows, ids, tiles, sems):
    core = lax.axis_index("rad")
    tile = pl.ds(pl.multiple_of(8 * (1 - core), 8), 8)
    pairs = [(reg.at[:, tile, :], ids)]
    for c in range(3):
        pairs.append((src.at[c, :, tile, :], tiles.at[c]))
    later = [
        (reg.at[14:16], rows.at[0:2]),
        (reg.at[0], rows.at[2]),
        (src.at[1, 1], dn.at[4]),
        (src.at[2, 1], dn.at[5]),
    ]
    for c in range(3):
        later.append((src.at[c, 14:16], up.at[2 * c : 2 * c + 2]))
        later.append((src.at[c, 0], dn.at[c]))
    copies = [
        pltpu.make_async_copy(x, y, sems.at[n]) for n, (x, y) in enumerate(pairs + later)
    ]
    for copy in copies:
        copy.start()
    for copy in copies[:4]:
        copy.wait()
    sub = lax.broadcasted_iota(jnp.int32, (16, 8, 256), 1) >> 1
    packed = jnp.zeros((16, 8, 256), F32)
    for c in range(4):
        x = tiles[c] if c < 3 else ids[...].astype(F32)
        packed = jnp.where(sub == c, pltpu.roll(x, (2 * c + 2 - 2 * core) & 7, 1), packed)
    sw[...] = packed
    for copy in copies[4:]:
        copy.wait()
    up[6:8] = rows[0:2].astype(F32)
    dn[3] = rows[2].astype(F32)


def send_call(src, reg):
    shapes = [(8, 16, 256), (6, 16, 256), (16, 8, 256)]
    return pl.pallas_call(
        send_kernel,
        out_shape=[jax.ShapeDtypeStruct(shape, F32) for shape in shapes],
        in_specs=[HBM, HBM],
        out_specs=[VMEM] * 3,
        scratch_shapes=[
            pltpu.VMEM((3, 16, 256), jnp.int32),
            pltpu.VMEM((16, 8, 256), jnp.int32),
            pltpu.VMEM((3, 16, 8, 256), F32),
            pltpu.SemaphoreType.DMA((14,)),
        ],
        compiler_params=pltpu.CompilerParams(vmem_limit_bytes=SEND_KIB * 2**10),
        name="send",
    )(src, reg)


def partner_rows(packed, c, core):
    first = roll(packed, -2 * c, 0) if c else packed
    last = roll(packed, 6 - 2 * c, 0) if c < 3 else packed
    return jnp.where(core == 1, last, first)


def call(kernel, name, outs, scratch, limit, in_specs, out_specs):
    return pl.pallas_call(
        kernel,
        out_shape=[
            pltpu.HBM(shape, F32) if spec is HBM else jax.ShapeDtypeStruct(shape, F32)
            for shape, spec in zip(outs, out_specs)
        ],
        in_specs=in_specs,
        out_specs=out_specs,
        scratch_shapes=[pltpu.VMEM(x, F32) if isinstance(x, tuple) else x for x in scratch],
        compiler_params=pltpu.CompilerParams(vmem_limit_bytes=limit * 2**20),
        cost_estimate=pl.CostEstimate(flops=10_000_000, bytes_accessed=2_000_000, transcendentals=0),
        name=name,
    )


def inner_kernel(src, reg, sw, kept, flag, sol_out, res_out, field, s, hh, sol, res, ids, sems):
    flag[...] = jnp.zeros((8, 128), F32)
    core = lax.axis_index("rad")
    pick = from_partner((8, 256), core)
    lane = lax.broadcasted_iota(jnp.int32, (24, 128), 1)
    copies = [pltpu.make_async_copy(src.at[c], field.at[c, :, 0:16, :], sems.at[c]) for c in range(3)]
    copies.append(pltpu.make_async_copy(reg, ids, sems.at[3]))
    for copy in copies:
        copy.start()
    for copy in copies:
        copy.wait()

    def assemble(z):
        for c in range(4):
            rows = partner_rows(sw[z], c, core)
            field[c, z, 16:24, :] = jnp.where(pick, rows, 0.0 if c < 3 else -1.0)
        field[3, z, 0:16, :] = ids[z].astype(F32)

    loop(0, 16, assemble, 4)

    def vec(z):
        return [field[c, z] for c in range(3)]

    def first_h(z):
        reluct, _ = materials(field[3, z])
        h = strength(*vec(z), field[1, z + 1], field[2, z + 1], reluct)
        for c in range(3):
            hh[c, z] = h[c]

    loop(0, 15, first_h, UNROLL)

    def first_a(z):
        v = vec(z)
        _, mass = materials(field[3, z])
        a = image(v, [hh[c, z] for c in range(3)], hh[1, z - 1], hh[2, z - 1], mass)
        step = second_of(v, a, mass)
        for c in range(3):
            s[c, z] = step[c]
            res[c, z] = (v[c] - FIRST * a[c])[:16]
            sol[c, z] = (FIRST * v[c] + step[c])[:16]

    loop(1, 15, first_a, UNROLL)

    copies = [pltpu.make_async_copy(sol, sol_out, sems.at[0])]
    copies[0].start()

    def stress_plane(z):
        u0, u1, u2 = [FIRST * field[c, z] + s[c, z] for c in range(3)]
        u1n, u2n = [FIRST * field[c, z + 1] + s[c, z + 1] for c in (1, 2)]
        kept[KEPT.stress(z)] = stress_of(u0, u1, u2, u1n, u2n, core)

    for z in range(1, 14):
        stress_plane(z)

    def second_h(z):
        reluct, _ = materials(field[3, z])
        h = strength(s[0, z], s[1, z], s[2, z], s[1, z + 1], s[2, z + 1], reluct)
        for c in range(3):
            hh[c, z] = h[c]

    loop(1, 14, second_h, UNROLL)

    def second_a(z):
        _, mass = materials(field[3, z])
        v = [s[c, z] for c in range(3)]
        a = image(v, [hh[c, z] for c in range(3)], hh[1, z - 1], hh[2, z - 1], mass)
        for c in range(3):
            res[c, z] = res[c, z] - a[c][:16]

    loop(2, 14, second_a, UNROLL)
    copies.append(pltpu.make_async_copy(res, res_out, sems.at[1]))
    copies[1].start()
    for c in range(3):
        for z in KEPT.of_step:
            kept[KEPT.step(c, z)] = s[c, z]
        for z in KEPT.of_res:
            kept[KEPT.res(c, z)] = res[c, z]
        kept[KEPT.strength(c, 0)] = hh[c, 0]
        if c > 0:
            kept[KEPT.strength(c, 14)] = hh[c, 14]
    for c in range(4):
        for z in KEPT.of_field:
            kept[KEPT.field(c, z)] = field[c, z]

    for c in range(4):
        right = left = jnp.full((24, 128), 0.0 if c < 3 else -1.0, F32)
        for z in range(16):
            right, left = pack_plane(right, left, field[c, z], z + 2, lane)
        kept[KEPT.strips(c, 0)] = right
        kept[KEPT.strips(c, 1)] = left

    for copy in copies:
        copy.wait()


def rim_kernel(kept, up, sw, dn, _, hbm, az_up, az_dn, rim, w, out, up_msg, dn_msg, sem):
    core, ax = lax.axis_index("rad"), lax.axis_index("ax")
    lo = jnp.where(ax > 0, 1.0, 0.0)
    hi = jnp.where(ax < lax.axis_size("ax") - 1, 1.0, 0.0)
    pick = from_partner((8, 256), core)
    for c in range(4):
        empty = 0.0 if c < 3 else -1.0

        def put(i, value, beside, valid):
            w[c, i, 0:16, :] = (value - empty) * valid + empty
            w[c, i, 16:24, :] = jnp.where(pick, (beside - empty) * valid + empty, empty)

        put(0, up[2 * c], sw[2 * c], lo)
        put(1, up[2 * c + 1], sw[2 * c + 1], lo)
        put(6, dn[c], partner_rows(dn[6, 0:8], c, core), hi)
        if c in (1, 2):
            put(7, dn[3 + c], partner_rows(dn[6, 8:16], c, core), hi)
        else:
            w[c, 7] = jnp.full((24, 256), empty, F32)
        for z in (-2, -1):
            rim[RIM.field(c, z)] = w[c, z + 2]
        w[c, 2] = kept[KEPT.field(c, 0)]
        w[c, 3] = kept[KEPT.field(c, 1)]
        w[c, 4] = kept[KEPT.field(c, 14)]
        w[c, 5] = kept[KEPT.field(c, 15)]

    def vec(i):
        return [w[c, i] for c in range(3)]

    def h_of(i, reluct):
        return strength(*vec(i), w[1, i + 1], w[2, i + 1], reluct)

    def step_of(i, z, h, h1p, h2p):
        v, mass = vec(i), materials(w[3, i])[1]
        a = image(v, h, h1p, h2p, mass)
        step = second_of(v, a, mass)
        for c in range(3):
            rim[RIM.step(c, z)] = step[c]
            if z < 16:
                rim[RIM.res(c, z)] = (v[c] - FIRST * a[c])[:16]
        return [FIRST * v[c] + step[c] for c in range(3)]

    h_before = h_of(1, materials(w[3, 1])[0])
    h_last = h_of(5, materials(w[3, 5])[0])
    h_after = h_of(6, materials(w[3, 6])[0])
    h_zero = [kept[KEPT.strength(c, 0)] for c in range(3)]
    u_first = step_of(2, 0, h_zero, h_before[1], h_before[2])
    u_last = step_of(5, 15, h_last, kept[KEPT.strength(1, 14)], kept[KEPT.strength(2, 14)])
    u_after = step_of(6, 16, h_after, h_last[1], h_last[2])
    u_one = [FIRST * w[c, 3] + kept[KEPT.step(c, 1)] for c in range(3)]
    u_14 = [FIRST * w[c, 4] + kept[KEPT.step(c, 14)] for c in range(3)]
    for z in range(1, 14):
        out[z, :, 0:256] = kept[KEPT.stress(z)]
    out[0, :, 0:256] = stress_of(*u_first, u_one[1], u_one[2], core)
    out[14, :, 0:256] = stress_of(*u_14, u_last[1], u_last[2], core)
    out[15, :, 0:256] = stress_of(*u_last, u_after[1], u_after[2], core)
    main, last = [slice(0, 256), slice(256, 384)]
    copies = [pltpu.make_async_copy(out.at[:, :, main], hbm.at[:, :, main], sem.at[0])]
    copies[0].start()

    lane = lax.broadcasted_iota(jnp.int32, (24, 128), 1)
    plane = (lane * 43) >> 8
    k = lane - 6 * plane
    right, left = [], []
    for c in range(4):
        r, l = kept[KEPT.strips(c, 0)], kept[KEPT.strips(c, 1)]
        for i, n in ((0, 0), (1, 1), (18, 6), (19, 7)):
            r, l = pack_plane(r, l, w[c, n], i, lane)
        empty = 0.0 if c < 3 else -1.0
        r = jnp.where(k < 4, r, empty)
        l = jnp.where(k > 1, l, empty)
        rim[RIM.strips(c, 0)] = r
        rim[RIM.strips(c, 1)] = l
        right.append(r)
        left.append(l)
    for msg, x in ((up_msg, right), (dn_msg, left)):
        msg[0] = jnp.where(
            k < 2, roll(x[2], -2, 1), jnp.where(k < 4, x[0], roll(x[1], 2, 1))
        )
        msg[1] = x[3]
    copies.append(pltpu.make_async_copy(up_msg, az_up, sem.at[1]))
    copies.append(pltpu.make_async_copy(dn_msg, az_dn, sem.at[2]))
    copies[1].start()
    copies[2].start()

    f = SECOND_A

    def partial(x):
        reluct, mass = materials(x[3])
        v = x[:3]
        h = strength(*v, roll(v[1], -6, 1), roll(v[2], -6, 1), reluct)
        a = image(v, h, roll(h[1], 6, 1), roll(h[2], 6, 1), mass)
        step = second_of(v, a, mass)
        u = [FIRST * v[c] + step[c] for c in range(3)]
        return reluct, h, u, fluxes(*u, roll(u[1], -6, 1), roll(u[2], -6, 1))

    reluct, (h0, h1, _), _, (flux1, flux2) = partial(right)
    fh1 = f * h1
    rest = f * ((roll(h0, -6, 1) - h0) + (roll(h1, -1, 0) - h1))
    rel_up, rel_dn = f * roll(reluct, -1, 0), f * roll(reluct, 1, 0)
    a_part = jnp.where(
        k < 2,
        roll(jnp.where(k == 3, flux1 - fh1, flux1), -2, 1),
        jnp.where(k == 2, roll(fh1, -1, 1), jnp.where(k < 5, roll(flux2, 1, 1), roll(rest, 2, 1))),
    )
    x_part = jnp.where(
        k == 1,
        -roll(rel_dn, -8, 1),
        jnp.where(k == 4, -roll(rel_up, 1, 1), jnp.where(k == 5, roll(rel_up, 2, 1), 0.0)),
    )
    z_part = jnp.where(k == 1, roll(rel_dn, -2, 1), 0.0)

    _, _, u, (flux1, flux2) = partial(left)
    v0, v1 = left[0], left[1]
    v1n = roll(v1, -6, 1)
    v1_dn = roll(v1, 1, 0)
    v0_up = roll(v0, -1, 0)
    inside = jnp.where(plane == 17, hi, 1.0)
    r_a = u[0] + f * ((roll(v0, -6, 1) + roll(v0, 6, 1)) - (3.0 + inside) * v0 + (v1n - v1))
    r_b = f * ((v1n - v1) + v0)
    b_part = jnp.where(
        k == 0,
        roll(f * v0, -2, 1),
        jnp.where(
            k == 1,
            roll(r_a, -1, 1),
            jnp.where(
                k == 2,
                flux1 + f * v0,
                jnp.where(k == 4, roll(r_b, 2, 1), jnp.where(k == 5, roll(flux2 - r_b, 3, 1), 0.0)),
            ),
        ),
    )
    y_part = jnp.where(
        k == 1, roll(v1_dn, -7, 1), jnp.where(k == 4, roll(v0_up, 2, 1), roll(v0_up, 3, 1))
    )
    w_part = roll(v1_dn, -1, 1)

    lane = lax.broadcasted_iota(jnp.int32, (8, 128), 1)
    parts = [
        roll(gap_tile(x, core), 6 * n, 1) if n else gap_tile(x, core)
        for n, x in enumerate((a_part, x_part, z_part, b_part, y_part, w_part))
    ]
    for z in range(16):
        part = (((lane - 6 * (z + 2)) & 127) * 43) >> 8
        extra = parts[5]
        for n in range(5):
            extra = jnp.where(part == n, parts[n], extra)
        out[z, :, 256:384] = extra
    copies.append(pltpu.make_async_copy(out.at[:, :, last], hbm.at[:, :, last], sem.at[3]))
    copies[3].start()
    for copy in copies:
        copy.wait()


def edge_kernel(skew, kept, rim, sol_in, res_in, sol, out, table):
    offset = 256 * lax.broadcasted_iota(jnp.int32, (16, MH), 0) - skew[lax.axis_index("az")]
    turns = (offset * lax.broadcasted_iota(jnp.int32, (16, MH), 1)) & (NA - 1)
    angle = turns.astype(F32) * (2.0 * math.pi / NA)
    table[0] = jnp.cos(angle)
    table[1] = jnp.sin(angle)

    v2, v1 = [[rim[RIM.field(c, z)] for c in range(4)] for z in (-2, -1)]
    v0 = [kept[KEPT.field(c, 0)] for c in range(3)]
    rim_code = materials(v1[3])
    _, h1, h2 = strength(*v2[:3], v1[1], v1[2], materials(v2[3])[0])
    h = strength(*v1[:3], v0[1], v0[2], rim_code[0])
    before_first = second_of(v1, image(v1, h, h1, h2, rim_code[1]), rim_code[1])

    def step(z, c):
        if z < 0:
            return before_first[c]
        return rim[RIM.step(c, z)] if z in (0, 15, 16) else kept[KEPT.step(c, z)]

    def materials_of(z):
        return rim_code if z < 0 else materials(kept[KEPT.field(3, z)])

    def h_of(z):
        return strength(
            step(z, 0), step(z, 1), step(z, 2), step(z + 1, 1), step(z + 1, 2), materials_of(z)[0]
        )

    for z in (0, 14):
        _, h1, h2 = h_of(z - 1)
        for n in range(2):
            h = h_of(z + n)
            a = image([step(z + n, c) for c in range(3)], h, h1, h2, materials_of(z + n)[1])
            h1, h2 = h[1], h[2]
            for c in range(3):
                x = z + n
                before = rim[RIM.res(c, x)] if x in (0, 15) else kept[KEPT.res(c, x)]
                out[c, x] = before - a[c][:16]
    for c in range(3):
        out[c, 2:14] = res_in[c, 2:14]
        sol[c, 1:15] = sol_in[c, 1:15]
        for z in (0, 15):
            sol[c, z] = FIRST * kept[KEPT.field(c, z)][:16] + rim[RIM.step(c, z)][:16]


def seam_kernel(rim, sol_in, res_in, from_left, from_right, sol, res, a_sol, a_res, sems):
    lane = lax.broadcasted_iota(jnp.int32, (24, 128), 1)
    plane = (lane * 43) >> 8
    k = lane - 6 * plane

    def full(x, msg, halo, shifts):
        return [
            jnp.where(halo, roll(msg[t], shift, 1) if shift else msg[t], x[c])
            for c, (t, shift) in enumerate(zip((0, 0, 0, 1), shifts))
        ]

    right = full([rim[RIM.strips(c, 0)] for c in range(4)], from_right, k > 3, (2, 0, 4, 2))
    left = full([rim[RIM.strips(c, 1)] for c in range(4)], from_left, k < 2, (-2, -4, 0, -2))
    copies = []

    def operator(v, reluct, mass):
        h = strength(*v, roll(v[1], -6, 1), roll(v[2], -6, 1), reluct)
        return image(v, h, roll(h[1], 6, 1), roll(h[2], 6, 1), mass)

    def send(n, buf, dst, inner, rights, lefts):
        lane = lax.broadcasted_iota(jnp.int32, (16, 128), 1)
        for c in range(3):
            merged = jnp.where(k[:16] < 4, rights[c][:16], roll(lefts[c][:16], 2, 1))
            for z in range(16):
                edge = roll(merged, 124 - 6 * (z + 2), 1)
                buf[c, z, :, 0:128] = jnp.where(lane < 2, edge, inner[c, z, :, 0:128])
                buf[c, z, :, 128:256] = jnp.where(lane >= 126, edge, inner[c, z, :, 128:256])
            copies.append(pltpu.make_async_copy(buf.at[c], dst.at[c], sems.at[n, c]))
            copies[-1].start()

    sides = []
    for x in (right, left):
        reluct, mass = materials(x[3])
        a = operator(x[:3], reluct, mass)
        sides.append((x[:3], reluct, mass, a, second_of(x, a, mass)))
    send(
        0, a_sol, sol, sol_in, *[[FIRST * v[c] + step[c] for c in range(3)] for v, _, _, _, step in sides]
    )
    rest = []
    for v, reluct, mass, a, step in sides:
        a2 = operator(step, reluct, mass)
        rest.append([v[c] - FIRST * a[c] - a2[c] for c in range(3)])
    send(1, a_res, res, res_in, *rest)
    for copy in copies:
        copy.wait()


def seam_call(*args):
    out = jax.ShapeDtypeStruct((3, 16, 16, 256), F32)
    return pl.pallas_call(
        seam_kernel,
        out_shape=[out, out],
        in_specs=[VMEM] * len(args),
        out_specs=[HBM] * 2,
        scratch_shapes=[
            pltpu.VMEM((3, 16, 16, 256), F32),
            pltpu.VMEM((3, 16, 16, 256), F32),
            pltpu.SemaphoreType.DMA((2, 3)),
        ],
        compiler_params=pltpu.CompilerParams(vmem_limit_bytes=12 * 2**20),
        cost_estimate=pl.CostEstimate(flops=4_000_000, bytes_accessed=4_000_000, transcendentals=0),
        name="seams",
    )(*args)


def harmonics_kernel(block, basis_hi, basis_lo, table, out):
    lane = lax.broadcasted_iota(jnp.int32, (16, 8, 128), 2)
    seam = block[:, :, 256:384]
    right = jnp.concatenate([seam[1:], seam[:1]], axis=0).reshape(128, 128)
    first = 6 * (lax.axis_index("az") + 2)
    right = pltpu.roll(right, lax.rem(256 - first - 18, 128), 1)
    seam = pltpu.roll(seam.reshape(128, 128), lax.rem(256 - first, 128), 1)
    product = seam * right
    flux = seam + right + roll(product, -6, 1) + roll(product, -12, 1)
    square = 0.5 * (flux * flux)
    fixed = roll(square - roll(square, -3, 1), -2, 1).reshape(16, 8, 128)
    moved = jnp.concatenate([fixed[15:], fixed[:15]], axis=0)
    low = jnp.where(lane == 0, moved, block[:, :, 0:128])
    high = jnp.where(lane >= 126, fixed, block[:, :, 128:256])
    x = jnp.concatenate([low.reshape(128, 128), high.reshape(128, 128)], axis=1)
    x_hi = x.astype(jnp.bfloat16)
    x_lo = (x - x_hi.astype(F32)).astype(jnp.bfloat16)

    def dot(a, b):
        return jnp.dot(a, b[...], preferred_element_type=F32)

    both = dot(jnp.concatenate([x_hi, x_lo], axis=0), basis_hi)
    local = both[:128] + (both[128:] + dot(x_hi, basis_lo))
    local = local.reshape(16, 8, 2 * MH)
    real = jnp.zeros((8, MH), F32)
    imag = jnp.zeros((8, MH), F32)
    for j in range(16):
        c, s = table[0, j : j + 1, :], table[1, j : j + 1, :]
        pc, ps = local[j, :, :MH], local[j, :, MH:]
        real = real + (pc * c - ps * s)
        imag = imag - (pc * s + ps * c)
    out[0, 0] = real
    out[1, 0] = imag


def harmonics_call(block, table):
    turns = np.arange(256)[:, None] * np.arange(MH)[None, :] / NA
    angle = 2.0 * math.pi * turns
    basis = np.concatenate([np.cos(angle), np.sin(angle)], axis=1) / math.sqrt(NA)
    hi = basis.astype(jnp.bfloat16)
    lo = (basis - hi.astype(np.float64)).astype(jnp.bfloat16)
    return pl.pallas_call(
        harmonics_kernel,
        out_shape=jax.ShapeDtypeStruct((2, 1, 8, MH), F32),
        in_specs=[VMEM] * 4,
        out_specs=VMEM,
        compiler_params=pltpu.CompilerParams(vmem_limit_bytes=8 * 2**20),
        cost_estimate=pl.CostEstimate(flops=100_000_000, bytes_accessed=1_000_000, transcendentals=0),
        name="harmonics",
    )(block, jnp.asarray(hi), jnp.asarray(lo), table)


def ring(axis, size, step):
    return functools.partial(
        lax.ppermute, axis_name=axis, perm=[(i, (i + step) % size) for i in range(size)]
    )


def on_device(source, region, skew_shift):
    n_az, n_ax = lax.axis_size("az"), lax.axis_size("ax")
    up, dn, sw = send_call(source, region)
    swap = ring("rad", 2, 1)
    sw = swap(sw)
    up = ring("ax", n_ax, 1)(up)
    dn = ring("ax", n_ax, -1)(jnp.concatenate([dn, sw[0:2].reshape(1, 16, 256)], axis=0))
    block, tall = (3, 16, 16, 256), (16, 24, 256)
    kept, flag, sol, res = call(
        inner_kernel,
        "inner",
        [(Kept.planes, 24, 256), (8, 128), block, block],
        [
            (4, *tall),
            (3, *tall),
            (3, *tall),
            block,
            block,
            pltpu.VMEM((16, 16, 256), jnp.int32),
            pltpu.SemaphoreType.DMA((4,)),
        ],
        16,
        [HBM, HBM, VMEM],
        [VMEM, VMEM, HBM, HBM],
    )(source, region, sw)
    start, flag = lax.optimization_barrier((8 * (1 - lax.axis_index("rad")), flag))
    sw_up = swap(lax.dynamic_slice_in_dim(up, start, 8, axis=1))
    stress, az_up, az_dn, rim = call(
        rim_kernel,
        "rim",
        [(16, 8, 384), (2, 24, 128), (2, 24, 128), (Rim.planes, 24, 256)],
        [
            (4, 8, 24, 256),
            (16, 8, 384),
            (2, 24, 128),
            (2, 24, 128),
            pltpu.SemaphoreType.DMA((4,)),
        ],
        8,
        [VMEM] * 4 + [pl.BlockSpec(memory_space=pl.ANY)],
        [HBM, HBM, HBM, VMEM],
    )(kept, up, sw_up, dn, flag)
    circle = lax.all_to_all(stress, "az", split_axis=0, concat_axis=0, tiled=True)
    from_left = ring("az", n_az, 1)(az_up)
    from_right = ring("az", n_az, -1)(az_dn)
    sol, res, table = call(
        edge_kernel, "edge", [block, block, (2, 16, MH)], [], 8, [SMEM] + [VMEM] * 4, [VMEM] * 3
    )(skew_shift, kept, rim, sol, res)
    solution, residual = seam_call(rim, sol, res, from_left, from_right)
    harmonics = harmonics_call(circle, table)
    return (solution, residual, harmonics)


def solution(mesh):
    in_specs = (P(None, "ax", "rad", "az"), P("ax", "rad", "az"), P("ax"))
    out_specs = (
        P(None, "ax", "rad", "az"),
        P(None, "ax", "rad", "az"),
        P(None, ("ax", "az"), "rad", None),
    )
    return jax.shard_map(
        on_device, mesh=mesh, in_specs=in_specs, out_specs=out_specs, check_vma=False
    )
```

```python
import functools
import math

import jax
import jax.numpy as jnp
import numpy as np
from jax import lax
from jax.experimental import pallas as pl
from jax.experimental.pallas import tpu as pltpu
from jax.sharding import PartitionSpec as P

NA = 4096
MH = 256
F32 = jnp.float32

cheb_center = 7.1
cheb_radius = 6.9
ratio_sigma = cheb_center / cheb_radius
rho_first = 1.0 / ratio_sigma
rho_second = 1.0 / (2.0 * ratio_sigma - rho_first)
keep_weight = rho_second * rho_first
fresh_weight = 2.0 * rho_second / cheb_radius

FIRST = 1.0 / cheb_center
SECOND_SRC = keep_weight / cheb_center + fresh_weight
SECOND_A = fresh_weight / cheb_center
SUM_SRC = FIRST + SECOND_SRC

VMEM = pl.BlockSpec(memory_space=pltpu.VMEM)
SMEM = pl.BlockSpec(memory_space=pltpu.SMEM)
HBM = pl.BlockSpec(memory_space=pltpu.HBM)

UNROLL = 2
SEND_KIB = 54656


def materials(code):
    iron, magnet, outside = code == 1.0, code == 2.0, code < 0.0
    reluct = jnp.where(iron, 0.05, jnp.where(magnet, 0.95, jnp.where(outside, 0.0, 1.0)))
    mass = jnp.where(
        iron,
        1.5,
        jnp.where(magnet, 0.6, jnp.where(outside, 0.0, jnp.where(code == 0.0, 0.2, 2.0))),
    )
    return reluct.astype(F32), mass.astype(F32)


def roll(x, shift, axis):
    return pltpu.roll(x, shift % x.shape[axis], axis)


def from_partner(shape, core):
    sub = lax.broadcasted_iota(jnp.int32, shape, len(shape) - 2)
    return (sub >= 6 * core) & (sub < 6 * core + 2)


class Kept:
    planes = 53
    of_field, of_step, of_res = (0, 1, 13, 14, 15), (1, 2, 13, 14), (1, 14)

    def field(self, c, z):
        return 5 * c + self.of_field.index(z)

    def step(self, c, z):
        return 20 + 4 * c + self.of_step.index(z)

    def res(self, c, z):
        return (32 + 2 * c + self.of_res.index(z), slice(0, 16))

    def strips(self, c, side):
        return (38 + c, slice(None), slice(128 * side, 128 * side + 128))

    def stress(self, z):
        return (42 + z // 3, slice(8 * (z % 3), 8 * (z % 3) + 8))

    def strength(self, c, z):
        return 48 + c if z == 0 else 50 + c


class Rim:
    planes = 9 + 6 + 4 + 8

    def step(self, c, z):
        return 3 * c + (0, 15, 16).index(z)

    def res(self, c, z):
        return (9 + 2 * c + (0, 15).index(z), slice(0, 16))

    def strips(self, c, side):
        return (15 + c, slice(None), slice(128 * side, 128 * side + 128))

    def field(self, c, z):
        return 19 + 2 * c + (-2, -1).index(z)


KEPT, RIM = Kept(), Rim()


def gap_tile(x, core):
    return jnp.where(core == 1, x[0:8], x[8:16])


def loop(first, last, body, unroll):
    rounds = (last - first) // unroll

    def several(t, carry):
        for k in range(unroll):
            body(first + t * unroll + k)
        return carry

    lax.fori_loop(0, rounds, several, 0)
    for k in range(first + rounds * unroll, last):
        body(k)


def curl(v0, v1, v2, v0a, v1a, v0r, v2r, v1n, v2n):
    return (
        (v2r - v2) - (v1a - v1),
        (v0a - v0) - (v2n - v2),
        (v1n - v1) - (v0r - v0),
    )


def strength(v0, v1, v2, v1n, v2n, reluct):
    c0, c1, c2 = curl(
        v0, v1, v2, roll(v0, -1, 1), roll(v1, -1, 1), roll(v0, -1, 0), roll(v2, -1, 0), v1n, v2n
    )
    return reluct * c0, reluct * c1, reluct * c2


def image(v, h, h1p, h2p, mass):
    h0, h1, h2 = h
    return (
        (h2 - roll(h2, 1, 0)) - (h1 - roll(h1, 1, 1)) + mass * v[0],
        (h0 - roll(h0, 1, 1)) - (h2 - h2p) + mass * v[1],
        (h1 - h1p) - (h0 - roll(h0, 1, 0)) + mass * v[2],
    )


def second_of(v, a, mass):
    return [jnp.where(mass > 0.0, SECOND_SRC * v[c] - SECOND_A * a[c], 0.0) for c in range(3)]


def fluxes(u0, u1, u2, u1n, u2n):
    return (roll(u0, -1, 1) - u0) - (u2n - u2), (u1n - u1) - (roll(u0, -1, 0) - u0)


def stress_of(u0, u1, u2, u1n, u2n, core):
    flux1, flux2 = fluxes(u0, u1, u2, u1n, u2n)
    flux1, flux2 = gap_tile(flux1, core), gap_tile(flux2, core)
    return 0.5 * (flux1 * flux1 - flux2 * flux2)


def pack_plane(rights, lefts, x, i, lane):
    here = (lane >= 6 * i) & (lane < 6 * i + 6)
    right = jnp.where(here, roll(x[:, 128:], 6 * i + 4, 1), rights)
    left = jnp.where(here, roll(x[:, :128], 6 * i + 2, 1), lefts)
    return right, left


def send_kernel(src, reg, up, dn, sw, rows, ids, tiles, sems):
    core = lax.axis_index("rad")
    tile = pl.ds(pl.multiple_of(8 * (1 - core), 8), 8)
    pairs = [(reg.at[:, tile, :], ids)]
    for c in range(3):
        pairs.append((src.at[c, :, tile, :], tiles.at[c]))
    later = [
        (reg.at[14:16], rows.at[0:2]),
        (reg.at[0], rows.at[2]),
        (src.at[1, 1], dn.at[4]),
        (src.at[2, 1], dn.at[5]),
    ]
    for c in range(3):
        later.append((src.at[c, 14:16], up.at[2 * c : 2 * c + 2]))
        later.append((src.at[c, 0], dn.at[c]))
    copies = [
        pltpu.make_async_copy(x, y, sems.at[n]) for n, (x, y) in enumerate(pairs + later)
    ]
    for copy in copies:
        copy.start()
    for copy in copies[:4]:
        copy.wait()
    sub = lax.broadcasted_iota(jnp.int32, (16, 8, 256), 1) >> 1
    packed = jnp.zeros((16, 8, 256), F32)
    for c in range(4):
        x = tiles[c] if c < 3 else ids[...].astype(F32)
        packed = jnp.where(sub == c, pltpu.roll(x, (2 * c + 2 - 2 * core) & 7, 1), packed)
    sw[...] = packed
    for copy in copies[4:]:
        copy.wait()
    up[6:8] = rows[0:2].astype(F32)
    dn[3] = rows[2].astype(F32)


def send_call(src, reg):
    shapes = [(8, 16, 256), (6, 16, 256), (16, 8, 256)]
    return pl.pallas_call(
        send_kernel,
        out_shape=[jax.ShapeDtypeStruct(shape, F32) for shape in shapes],
        in_specs=[HBM, HBM],
        out_specs=[VMEM] * 3,
        scratch_shapes=[
            pltpu.VMEM((3, 16, 256), jnp.int32),
            pltpu.VMEM((16, 8, 256), jnp.int32),
            pltpu.VMEM((3, 16, 8, 256), F32),
            pltpu.SemaphoreType.DMA((14,)),
        ],
        compiler_params=pltpu.CompilerParams(vmem_limit_bytes=SEND_KIB * 2**10),
        name="send",
    )(src, reg)


def partner_rows(packed, c, core):
    first = roll(packed, -2 * c, 0) if c else packed
    last = roll(packed, 6 - 2 * c, 0) if c < 3 else packed
    return jnp.where(core == 1, last, first)


def call(kernel, name, outs, scratch, limit, in_specs, out_specs):
    return pl.pallas_call(
        kernel,
        out_shape=[
            pltpu.HBM(shape, F32) if spec is HBM else jax.ShapeDtypeStruct(shape, F32)
            for shape, spec in zip(outs, out_specs)
        ],
        in_specs=in_specs,
        out_specs=out_specs,
        scratch_shapes=[pltpu.VMEM(x, F32) if isinstance(x, tuple) else x for x in scratch],
        compiler_params=pltpu.CompilerParams(vmem_limit_bytes=limit * 2**20),
        cost_estimate=pl.CostEstimate(flops=10_000_000, bytes_accessed=2_000_000, transcendentals=0),
        name=name,
    )


def inner_kernel(src, reg, sw, kept, flag, sol_out, res_out, field, s, hh, sol, res, ids, sems):
    flag[...] = jnp.zeros((8, 128), F32)
    core = lax.axis_index("rad")
    pick = from_partner((8, 256), core)
    lane = lax.broadcasted_iota(jnp.int32, (24, 128), 1)
    copies = [pltpu.make_async_copy(src.at[c], field.at[c, :, 0:16, :], sems.at[c]) for c in range(3)]
    copies.append(pltpu.make_async_copy(reg, ids, sems.at[3]))
    for copy in copies:
        copy.start()
    for copy in copies:
        copy.wait()

    def assemble(z):
        for c in range(4):
            rows = partner_rows(sw[z], c, core)
            field[c, z, 16:24, :] = jnp.where(pick, rows, 0.0 if c < 3 else -1.0)
        field[3, z, 0:16, :] = ids[z].astype(F32)

    loop(0, 16, assemble, 4)

    def vec(z):
        return [field[c, z] for c in range(3)]

    def first_h(z):
        reluct, _ = materials(field[3, z])
        h = strength(*vec(z), field[1, z + 1], field[2, z + 1], reluct)
        for c in range(3):
            hh[c, z] = h[c]

    loop(0, 15, first_h, UNROLL)

    def first_a(z):
        v = vec(z)
        _, mass = materials(field[3, z])
        a = image(v, [hh[c, z] for c in range(3)], hh[1, z - 1], hh[2, z - 1], mass)
        step = second_of(v, a, mass)
        for c in range(3):
            s[c, z] = step[c]
            res[c, z] = (v[c] - FIRST * a[c])[:16]
            sol[c, z] = (FIRST * v[c] + step[c])[:16]

    loop(1, 15, first_a, UNROLL)

    copies = [pltpu.make_async_copy(sol, sol_out, sems.at[0])]
    copies[0].start()

    def stress_plane(z):
        u0, u1, u2 = [FIRST * field[c, z] + s[c, z] for c in range(3)]
        u1n, u2n = [FIRST * field[c, z + 1] + s[c, z + 1] for c in (1, 2)]
        kept[KEPT.stress(z)] = stress_of(u0, u1, u2, u1n, u2n, core)

    for z in range(1, 14):
        stress_plane(z)

    def second_h(z):
        reluct, _ = materials(field[3, z])
        h = strength(s[0, z], s[1, z], s[2, z], s[1, z + 1], s[2, z + 1], reluct)
        for c in range(3):
            hh[c, z] = h[c]

    loop(1, 14, second_h, UNROLL)

    def second_a(z):
        _, mass = materials(field[3, z])
        v = [s[c, z] for c in range(3)]
        a = image(v, [hh[c, z] for c in range(3)], hh[1, z - 1], hh[2, z - 1], mass)
        for c in range(3):
            res[c, z] = res[c, z] - a[c][:16]

    loop(2, 14, second_a, UNROLL)
    copies.append(pltpu.make_async_copy(res, res_out, sems.at[1]))
    copies[1].start()
    for c in range(3):
        for z in KEPT.of_step:
            kept[KEPT.step(c, z)] = s[c, z]
        for z in KEPT.of_res:
            kept[KEPT.res(c, z)] = res[c, z]
        kept[KEPT.strength(c, 0)] = hh[c, 0]
        if c > 0:
            kept[KEPT.strength(c, 14)] = hh[c, 14]
    for c in range(4):
        for z in KEPT.of_field:
            kept[KEPT.field(c, z)] = field[c, z]

    for c in range(4):
        right = left = jnp.full((24, 128), 0.0 if c < 3 else -1.0, F32)
        for z in range(16):
            right, left = pack_plane(right, left, field[c, z], z + 2, lane)
        kept[KEPT.strips(c, 0)] = right
        kept[KEPT.strips(c, 1)] = left

    for copy in copies:
        copy.wait()


def rim_kernel(kept, up, sw, dn, _, hbm, up_msg, dn_msg, rim, w, out, sem):
    core, ax = lax.axis_index("rad"), lax.axis_index("ax")
    lo = jnp.where(ax > 0, 1.0, 0.0)
    hi = jnp.where(ax < lax.axis_size("ax") - 1, 1.0, 0.0)
    pick = from_partner((8, 256), core)
    for c in range(4):
        empty = 0.0 if c < 3 else -1.0

        def put(i, value, beside, valid):
            w[c, i, 0:16, :] = (value - empty) * valid + empty
            w[c, i, 16:24, :] = jnp.where(pick, (beside - empty) * valid + empty, empty)

        put(0, up[2 * c], sw[2 * c], lo)
        put(1, up[2 * c + 1], sw[2 * c + 1], lo)
        put(6, dn[c], partner_rows(dn[6, 0:8], c, core), hi)
        if c in (1, 2):
            put(7, dn[3 + c], partner_rows(dn[6, 8:16], c, core), hi)
        else:
            w[c, 7] = jnp.full((24, 256), empty, F32)
        for z in (-2, -1):
            rim[RIM.field(c, z)] = w[c, z + 2]
        w[c, 2] = kept[KEPT.field(c, 0)]
        w[c, 3] = kept[KEPT.field(c, 1)]
        w[c, 4] = kept[KEPT.field(c, 14)]
        w[c, 5] = kept[KEPT.field(c, 15)]

    def vec(i):
        return [w[c, i] for c in range(3)]

    def h_of(i, reluct):
        return strength(*vec(i), w[1, i + 1], w[2, i + 1], reluct)

    def step_of(i, z, h, h1p, h2p):
        v, mass = vec(i), materials(w[3, i])[1]
        a = image(v, h, h1p, h2p, mass)
        step = second_of(v, a, mass)
        for c in range(3):
            rim[RIM.step(c, z)] = step[c]
            if z < 16:
                rim[RIM.res(c, z)] = (v[c] - FIRST * a[c])[:16]
        return [FIRST * v[c] + step[c] for c in range(3)]

    h_before = h_of(1, materials(w[3, 1])[0])
    h_last = h_of(5, materials(w[3, 5])[0])
    h_after = h_of(6, materials(w[3, 6])[0])
    h_zero = [kept[KEPT.strength(c, 0)] for c in range(3)]
    u_first = step_of(2, 0, h_zero, h_before[1], h_before[2])
    u_last = step_of(5, 15, h_last, kept[KEPT.strength(1, 14)], kept[KEPT.strength(2, 14)])
    u_after = step_of(6, 16, h_after, h_last[1], h_last[2])
    u_one = [FIRST * w[c, 3] + kept[KEPT.step(c, 1)] for c in range(3)]
    u_14 = [FIRST * w[c, 4] + kept[KEPT.step(c, 14)] for c in range(3)]
    for z in range(1, 14):
        out[z, :, 0:256] = kept[KEPT.stress(z)]
    out[0, :, 0:256] = stress_of(*u_first, u_one[1], u_one[2], core)
    out[14, :, 0:256] = stress_of(*u_14, u_last[1], u_last[2], core)
    out[15, :, 0:256] = stress_of(*u_last, u_after[1], u_after[2], core)
    main, last = [slice(0, 256), slice(256, 384)]
    copies = [pltpu.make_async_copy(out.at[:, :, main], hbm.at[:, :, main], sem.at[0])]
    copies[0].start()

    lane = lax.broadcasted_iota(jnp.int32, (24, 128), 1)
    plane = (lane * 43) >> 8
    k = lane - 6 * plane
    right, left = [], []
    for c in range(4):
        r, l = kept[KEPT.strips(c, 0)], kept[KEPT.strips(c, 1)]
        for i, n in ((0, 0), (1, 1), (18, 6), (19, 7)):
            r, l = pack_plane(r, l, w[c, n], i, lane)
        empty = 0.0 if c < 3 else -1.0
        r = jnp.where(k < 4, r, empty)
        l = jnp.where(k > 1, l, empty)
        rim[RIM.strips(c, 0)] = r
        rim[RIM.strips(c, 1)] = l
        right.append(r)
        left.append(l)
    for msg, x in ((up_msg, right), (dn_msg, left)):
        msg[0] = jnp.where(
            k < 2, roll(x[2], -2, 1), jnp.where(k < 4, x[0], roll(x[1], 2, 1))
        )
        msg[1] = x[3]

    f = SECOND_A

    def partial(x):
        reluct, mass = materials(x[3])
        v = x[:3]
        h = strength(*v, roll(v[1], -6, 1), roll(v[2], -6, 1), reluct)
        a = image(v, h, roll(h[1], 6, 1), roll(h[2], 6, 1), mass)
        step = second_of(v, a, mass)
        u = [FIRST * v[c] + step[c] for c in range(3)]
        return reluct, h, u, fluxes(*u, roll(u[1], -6, 1), roll(u[2], -6, 1))

    reluct, (h0, h1, _), _, (flux1, flux2) = partial(right)
    fh1 = f * h1
    rest = f * ((roll(h0, -6, 1) - h0) + (roll(h1, -1, 0) - h1))
    rel_up, rel_dn = f * roll(reluct, -1, 0), f * roll(reluct, 1, 0)
    a_part = jnp.where(
        k < 2,
        roll(jnp.where(k == 3, flux1 - fh1, flux1), -2, 1),
        jnp.where(k == 2, roll(fh1, -1, 1), jnp.where(k < 5, roll(flux2, 1, 1), roll(rest, 2, 1))),
    )
    x_part = jnp.where(
        k == 1,
        -roll(rel_dn, -8, 1),
        jnp.where(k == 4, -roll(rel_up, 1, 1), jnp.where(k == 5, roll(rel_up, 2, 1), 0.0)),
    )
    z_part = jnp.where(k == 1, roll(rel_dn, -2, 1), 0.0)

    _, _, u, (flux1, flux2) = partial(left)
    v0, v1 = left[0], left[1]
    v1n = roll(v1, -6, 1)
    v1_dn = roll(v1, 1, 0)
    v0_up = roll(v0, -1, 0)
    inside = jnp.where(plane == 17, hi, 1.0)
    r_a = u[0] + f * ((roll(v0, -6, 1) + roll(v0, 6, 1)) - (3.0 + inside) * v0 + (v1n - v1))
    r_b = f * ((v1n - v1) + v0)
    b_part = jnp.where(
        k == 0,
        roll(f * v0, -2, 1),
        jnp.where(
            k == 1,
            roll(r_a, -1, 1),
            jnp.where(
                k == 2,
                flux1 + f * v0,
                jnp.where(k == 4, roll(r_b, 2, 1), jnp.where(k == 5, roll(flux2 - r_b, 3, 1), 0.0)),
            ),
        ),
    )
    y_part = jnp.where(
        k == 1, roll(v1_dn, -7, 1), jnp.where(k == 4, roll(v0_up, 2, 1), roll(v0_up, 3, 1))
    )
    w_part = roll(v1_dn, -1, 1)

    lane = lax.broadcasted_iota(jnp.int32, (8, 128), 1)
    parts = [
        roll(gap_tile(x, core), 6 * n, 1) if n else gap_tile(x, core)
        for n, x in enumerate((a_part, x_part, z_part, b_part, y_part, w_part))
    ]
    for z in range(16):
        part = (((lane - 6 * (z + 2)) & 127) * 43) >> 8
        extra = parts[5]
        for n in range(5):
            extra = jnp.where(part == n, parts[n], extra)
        out[z, :, 256:384] = extra
    copies.append(pltpu.make_async_copy(out.at[:, :, last], hbm.at[:, :, last], sem.at[1]))
    copies[1].start()
    for copy in copies:
        copy.wait()


def edge_kernel(skew, kept, rim, sol_in, res_in, sol, out, table):
    offset = 256 * lax.broadcasted_iota(jnp.int32, (16, MH), 0) - skew[lax.axis_index("az")]
    turns = (offset * lax.broadcasted_iota(jnp.int32, (16, MH), 1)) & (NA - 1)
    angle = turns.astype(F32) * (2.0 * math.pi / NA)
    table[0] = jnp.cos(angle)
    table[1] = jnp.sin(angle)

    v2, v1 = [[rim[RIM.field(c, z)] for c in range(4)] for z in (-2, -1)]
    v0 = [kept[KEPT.field(c, 0)] for c in range(3)]
    rim_code = materials(v1[3])
    _, h1, h2 = strength(*v2[:3], v1[1], v1[2], materials(v2[3])[0])
    h = strength(*v1[:3], v0[1], v0[2], rim_code[0])
    before_first = second_of(v1, image(v1, h, h1, h2, rim_code[1]), rim_code[1])

    def step(z, c):
        if z < 0:
            return before_first[c]
        return rim[RIM.step(c, z)] if z in (0, 15, 16) else kept[KEPT.step(c, z)]

    def materials_of(z):
        return rim_code if z < 0 else materials(kept[KEPT.field(3, z)])

    def h_of(z):
        return strength(
            step(z, 0), step(z, 1), step(z, 2), step(z + 1, 1), step(z + 1, 2), materials_of(z)[0]
        )

    for z in (0, 14):
        _, h1, h2 = h_of(z - 1)
        for n in range(2):
            h = h_of(z + n)
            a = image([step(z + n, c) for c in range(3)], h, h1, h2, materials_of(z + n)[1])
            h1, h2 = h[1], h[2]
            for c in range(3):
                x = z + n
                before = rim[RIM.res(c, x)] if x in (0, 15) else kept[KEPT.res(c, x)]
                out[c, x] = before - a[c][:16]
    for c in range(3):
        out[c, 2:14] = res_in[c, 2:14]
        sol[c, 1:15] = sol_in[c, 1:15]
        for z in (0, 15):
            sol[c, z] = FIRST * kept[KEPT.field(c, z)][:16] + rim[RIM.step(c, z)][:16]


def seam_kernel(rim, sol_in, res_in, from_left, from_right, sol, res, a_sol, a_res, sems):
    lane = lax.broadcasted_iota(jnp.int32, (24, 128), 1)
    plane = (lane * 43) >> 8
    k = lane - 6 * plane

    def full(x, msg, halo, shifts):
        return [
            jnp.where(halo, roll(msg[t], shift, 1) if shift else msg[t], x[c])
            for c, (t, shift) in enumerate(zip((0, 0, 0, 1), shifts))
        ]

    right = full([rim[RIM.strips(c, 0)] for c in range(4)], from_right, k > 3, (2, 0, 4, 2))
    left = full([rim[RIM.strips(c, 1)] for c in range(4)], from_left, k < 2, (-2, -4, 0, -2))
    copies = []

    def operator(v, reluct, mass):
        h = strength(*v, roll(v[1], -6, 1), roll(v[2], -6, 1), reluct)
        return image(v, h, roll(h[1], 6, 1), roll(h[2], 6, 1), mass)

    def send(n, buf, dst, inner, rights, lefts):
        lane = lax.broadcasted_iota(jnp.int32, (16, 128), 1)
        for c in range(3):
            merged = jnp.where(k[:16] < 4, rights[c][:16], roll(lefts[c][:16], 2, 1))
            for z in range(16):
                edge = roll(merged, 124 - 6 * (z + 2), 1)
                buf[c, z, :, 0:128] = jnp.where(lane < 2, edge, inner[c, z, :, 0:128])
                buf[c, z, :, 128:256] = jnp.where(lane >= 126, edge, inner[c, z, :, 128:256])
            copies.append(pltpu.make_async_copy(buf.at[c], dst.at[c], sems.at[n, c]))
            copies[-1].start()

    sides = []
    for x in (right, left):
        reluct, mass = materials(x[3])
        a = operator(x[:3], reluct, mass)
        sides.append((x[:3], reluct, mass, a, second_of(x, a, mass)))
    send(
        0, a_sol, sol, sol_in, *[[FIRST * v[c] + step[c] for c in range(3)] for v, _, _, _, step in sides]
    )
    rest = []
    for v, reluct, mass, a, step in sides:
        a2 = operator(step, reluct, mass)
        rest.append([v[c] - FIRST * a[c] - a2[c] for c in range(3)])
    send(1, a_res, res, res_in, *rest)
    for copy in copies:
        copy.wait()


def seam_call(*args):
    out = jax.ShapeDtypeStruct((3, 16, 16, 256), F32)
    return pl.pallas_call(
        seam_kernel,
        out_shape=[out, out],
        in_specs=[VMEM] * len(args),
        out_specs=[HBM] * 2,
        scratch_shapes=[
            pltpu.VMEM((3, 16, 16, 256), F32),
            pltpu.VMEM((3, 16, 16, 256), F32),
            pltpu.SemaphoreType.DMA((2, 3)),
        ],
        compiler_params=pltpu.CompilerParams(vmem_limit_bytes=12 * 2**20),
        cost_estimate=pl.CostEstimate(flops=4_000_000, bytes_accessed=4_000_000, transcendentals=0),
        name="seams",
    )(*args)


def harmonics_kernel(block, basis_hi, basis_lo, table, out):
    lane = lax.broadcasted_iota(jnp.int32, (16, 8, 128), 2)
    seam = block[:, :, 256:384]
    right = jnp.concatenate([seam[1:], seam[:1]], axis=0).reshape(128, 128)
    first = 6 * (lax.axis_index("az") + 2)
    right = pltpu.roll(right, lax.rem(254 - first - 18, 128), 1)
    seam = pltpu.roll(seam.reshape(128, 128), lax.rem(254 - first, 128), 1)
    product = seam * right
    flux = seam + right + roll(product, -6, 1) + roll(product, -12, 1)
    square = 0.5 * (flux * flux)
    fixed = (square - roll(square, -3, 1)).reshape(16, 8, 128)
    moved = jnp.concatenate([fixed[15:], fixed[:15]], axis=0)
    low = jnp.where(lane == 0, moved, block[:, :, 0:128])
    high = jnp.where(lane >= 126, fixed, block[:, :, 128:256])
    x = jnp.concatenate([low.reshape(128, 128), high.reshape(128, 128)], axis=1)
    x_hi = x.astype(jnp.bfloat16)
    x_lo = (x - x_hi.astype(F32)).astype(jnp.bfloat16)

    def dot(a, b):
        return jnp.dot(a, b[...], preferred_element_type=F32)

    both = dot(jnp.concatenate([x_hi, x_lo], axis=0), basis_hi)
    local = both[:128] + (both[128:] + dot(x_hi, basis_lo))
    local = local.reshape(16, 8, 2 * MH)
    real = jnp.zeros((8, MH), F32)
    imag = jnp.zeros((8, MH), F32)
    for j in range(16):
        c, s = table[0, j : j + 1, :], table[1, j : j + 1, :]
        pc, ps = local[j, :, :MH], local[j, :, MH:]
        real = real + (pc * c - ps * s)
        imag = imag - (pc * s + ps * c)
    out[0, 0] = real
    out[1, 0] = imag


def harmonics_call(block, table):
    turns = np.arange(256)[:, None] * np.arange(MH)[None, :] / NA
    angle = 2.0 * math.pi * turns
    basis = np.concatenate([np.cos(angle), np.sin(angle)], axis=1) / math.sqrt(NA)
    hi = basis.astype(jnp.bfloat16)
    lo = (basis - hi.astype(np.float64)).astype(jnp.bfloat16)
    return pl.pallas_call(
        harmonics_kernel,
        out_shape=jax.ShapeDtypeStruct((2, 1, 8, MH), F32),
        in_specs=[VMEM] * 4,
        out_specs=VMEM,
        compiler_params=pltpu.CompilerParams(vmem_limit_bytes=8 * 2**20),
        cost_estimate=pl.CostEstimate(flops=100_000_000, bytes_accessed=1_000_000, transcendentals=0),
        name="harmonics",
    )(block, jnp.asarray(hi), jnp.asarray(lo), table)


def ring(axis, size, step):
    return functools.partial(
        lax.ppermute, axis_name=axis, perm=[(i, (i + step) % size) for i in range(size)]
    )


def on_device(source, region, skew_shift):
    n_az, n_ax = lax.axis_size("az"), lax.axis_size("ax")
    up, dn, sw = send_call(source, region)
    swap = ring("rad", 2, 1)
    sw = swap(sw)
    up = ring("ax", n_ax, 1)(up)
    dn = ring("ax", n_ax, -1)(jnp.concatenate([dn, sw[0:2].reshape(1, 16, 256)], axis=0))
    block, tall = (3, 16, 16, 256), (16, 24, 256)
    kept, flag, sol, res = call(
        inner_kernel,
        "inner",
        [(Kept.planes, 24, 256), (8, 128), block, block],
        [
            (4, *tall),
            (3, *tall),
            (3, *tall),
            block,
            block,
            pltpu.VMEM((16, 16, 256), jnp.int32),
            pltpu.SemaphoreType.DMA((4,)),
        ],
        16,
        [HBM, HBM, VMEM],
        [VMEM, VMEM, HBM, HBM],
    )(source, region, sw)
    start, flag = lax.optimization_barrier((8 * (1 - lax.axis_index("rad")), flag))
    sw_up = swap(lax.dynamic_slice_in_dim(up, start, 8, axis=1))
    stress, az_up, az_dn, rim = call(
        rim_kernel,
        "rim",
        [(16, 8, 384), (2, 24, 128), (2, 24, 128), (Rim.planes, 24, 256)],
        [
            (4, 8, 24, 256),
            (16, 8, 384),
            pltpu.SemaphoreType.DMA((2,)),
        ],
        8,
        [VMEM] * 4 + [pl.BlockSpec(memory_space=pl.ANY)],
        [HBM, VMEM, VMEM, VMEM],
    )(kept, up, sw_up, dn, flag)
    circle = lax.all_to_all(stress, "az", split_axis=0, concat_axis=0, tiled=True)
    from_left = ring("az", n_az, 1)(az_up)
    from_right = ring("az", n_az, -1)(az_dn)
    sol, res, table = call(
        edge_kernel, "edge", [block, block, (2, 16, MH)], [], 8, [SMEM] + [VMEM] * 4, [VMEM] * 3
    )(skew_shift, kept, rim, sol, res)
    solution, residual = seam_call(rim, sol, res, from_left, from_right)
    harmonics = harmonics_call(circle, table)
    return (solution, residual, harmonics)


def solution(mesh):
    in_specs = (P(None, "ax", "rad", "az"), P("ax", "rad", "az"), P("ax"))
    out_specs = (
        P(None, "ax", "rad", "az"),
        P(None, "ax", "rad", "az"),
        P(None, ("ax", "az"), "rad", None),
    )
    return jax.shard_map(
        on_device, mesh=mesh, in_specs=in_specs, out_specs=out_specs, check_vma=False
    )
```

```python
import functools
import math

import jax
import jax.numpy as jnp
import numpy as np
from jax import lax
from jax.experimental import pallas as pl
from jax.experimental.pallas import tpu as pltpu
from jax.sharding import PartitionSpec as P

NA = 4096
MH = 256
F32 = jnp.float32

cheb_center = 7.1
cheb_radius = 6.9
ratio_sigma = cheb_center / cheb_radius
rho_first = 1.0 / ratio_sigma
rho_second = 1.0 / (2.0 * ratio_sigma - rho_first)
keep_weight = rho_second * rho_first
fresh_weight = 2.0 * rho_second / cheb_radius

FIRST = 1.0 / cheb_center
SECOND_SRC = keep_weight / cheb_center + fresh_weight
SECOND_A = fresh_weight / cheb_center
SUM_SRC = FIRST + SECOND_SRC

VMEM = pl.BlockSpec(memory_space=pltpu.VMEM)
SMEM = pl.BlockSpec(memory_space=pltpu.SMEM)
HBM = pl.BlockSpec(memory_space=pltpu.HBM)

UNROLL = 2
SEND_KIB = 54656


def materials(code):
    iron, magnet, outside = code == 1.0, code == 2.0, code < 0.0
    reluct = jnp.where(iron, 0.05, jnp.where(magnet, 0.95, jnp.where(outside, 0.0, 1.0)))
    mass = jnp.where(
        iron,
        1.5,
        jnp.where(magnet, 0.6, jnp.where(outside, 0.0, jnp.where(code == 0.0, 0.2, 2.0))),
    )
    return reluct.astype(F32), mass.astype(F32)


def roll(x, shift, axis):
    return pltpu.roll(x, shift % x.shape[axis], axis)


def from_partner(shape, core):
    sub = lax.broadcasted_iota(jnp.int32, shape, len(shape) - 2)
    return (sub >= 6 * core) & (sub < 6 * core + 2)


class Kept:
    planes = 53
    of_field, of_step, of_res = (0, 1, 13, 14, 15), (1, 2, 13, 14), (1, 14)

    def field(self, c, z):
        return 5 * c + self.of_field.index(z)

    def step(self, c, z):
        return 20 + 4 * c + self.of_step.index(z)

    def res(self, c, z):
        return (32 + 2 * c + self.of_res.index(z), slice(0, 16))

    def strips(self, c, side):
        return (38 + c, slice(None), slice(128 * side, 128 * side + 128))

    def stress(self, z):
        return (42 + z // 3, slice(8 * (z % 3), 8 * (z % 3) + 8))

    def strength(self, c, z):
        return 48 + c if z == 0 else 50 + c


class Rim:
    planes = 9 + 6 + 4 + 8

    def step(self, c, z):
        return 3 * c + (0, 15, 16).index(z)

    def res(self, c, z):
        return (9 + 2 * c + (0, 15).index(z), slice(0, 16))

    def strips(self, c, side):
        return (15 + c, slice(None), slice(128 * side, 128 * side + 128))

    def field(self, c, z):
        return 19 + 2 * c + (-2, -1).index(z)


KEPT, RIM = Kept(), Rim()


def gap_tile(x, core):
    return jnp.where(core == 1, x[0:8], x[8:16])


def loop(first, last, body, unroll):
    rounds = (last - first) // unroll

    def several(t, carry):
        for k in range(unroll):
            body(first + t * unroll + k)
        return carry

    lax.fori_loop(0, rounds, several, 0)
    for k in range(first + rounds * unroll, last):
        body(k)


def curl(v0, v1, v2, v0a, v1a, v0r, v2r, v1n, v2n):
    return (
        (v2r - v2) - (v1a - v1),
        (v0a - v0) - (v2n - v2),
        (v1n - v1) - (v0r - v0),
    )


def strength(v0, v1, v2, v1n, v2n, reluct):
    c0, c1, c2 = curl(
        v0, v1, v2, roll(v0, -1, 1), roll(v1, -1, 1), roll(v0, -1, 0), roll(v2, -1, 0), v1n, v2n
    )
    return reluct * c0, reluct * c1, reluct * c2


def image(v, h, h1p, h2p, mass):
    h0, h1, h2 = h
    return (
        (h2 - roll(h2, 1, 0)) - (h1 - roll(h1, 1, 1)) + mass * v[0],
        (h0 - roll(h0, 1, 1)) - (h2 - h2p) + mass * v[1],
        (h1 - h1p) - (h0 - roll(h0, 1, 0)) + mass * v[2],
    )


def second_of(v, a, mass):
    return [jnp.where(mass > 0.0, SECOND_SRC * v[c] - SECOND_A * a[c], 0.0) for c in range(3)]


def fluxes(u0, u1, u2, u1n, u2n):
    return (roll(u0, -1, 1) - u0) - (u2n - u2), (u1n - u1) - (roll(u0, -1, 0) - u0)


def stress_of(u0, u1, u2, u1n, u2n, core):
    flux1, flux2 = fluxes(u0, u1, u2, u1n, u2n)
    flux1, flux2 = gap_tile(flux1, core), gap_tile(flux2, core)
    return 0.5 * (flux1 * flux1 - flux2 * flux2)


def pack_plane(rights, lefts, x, i, lane):
    here = (lane >= 6 * i) & (lane < 6 * i + 6)
    right = jnp.where(here, roll(x[:, 128:], 6 * i + 4, 1), rights)
    left = jnp.where(here, roll(x[:, :128], 6 * i + 2, 1), lefts)
    return right, left


def send_kernel(src, reg, up, dn, sw, rows, ids, tiles, sems):
    core = lax.axis_index("rad")
    tile = pl.ds(pl.multiple_of(8 * (1 - core), 8), 8)
    pairs = [(reg.at[:, tile, :], ids)]
    for c in range(3):
        pairs.append((src.at[c, :, tile, :], tiles.at[c]))
    later = [
        (reg.at[14:16], rows.at[0:2]),
        (reg.at[0], rows.at[2]),
        (src.at[1, 1], dn.at[4]),
        (src.at[2, 1], dn.at[5]),
    ]
    for c in range(3):
        later.append((src.at[c, 14:16], up.at[2 * c : 2 * c + 2]))
        later.append((src.at[c, 0], dn.at[c]))
    copies = [
        pltpu.make_async_copy(x, y, sems.at[n]) for n, (x, y) in enumerate(pairs + later)
    ]
    for copy in copies:
        copy.start()
    for copy in copies[:4]:
        copy.wait()
    sub = lax.broadcasted_iota(jnp.int32, (16, 8, 256), 1) >> 1
    packed = jnp.zeros((16, 8, 256), F32)
    for c in range(4):
        x = tiles[c] if c < 3 else ids[...].astype(F32)
        packed = jnp.where(sub == c, pltpu.roll(x, (2 * c + 2 - 2 * core) & 7, 1), packed)
    sw[...] = packed
    for copy in copies[4:]:
        copy.wait()
    up[6:8] = rows[0:2].astype(F32)
    dn[3] = rows[2].astype(F32)


def send_call(src, reg):
    shapes = [(8, 16, 256), (6, 16, 256), (16, 8, 256)]
    return pl.pallas_call(
        send_kernel,
        out_shape=[jax.ShapeDtypeStruct(shape, F32) for shape in shapes],
        in_specs=[HBM, HBM],
        out_specs=[VMEM] * 3,
        scratch_shapes=[
            pltpu.VMEM((3, 16, 256), jnp.int32),
            pltpu.VMEM((16, 8, 256), jnp.int32),
            pltpu.VMEM((3, 16, 8, 256), F32),
            pltpu.SemaphoreType.DMA((14,)),
        ],
        compiler_params=pltpu.CompilerParams(vmem_limit_bytes=SEND_KIB * 2**10),
        name="send",
    )(src, reg)


def partner_rows(packed, c, core):
    first = roll(packed, -2 * c, 0) if c else packed
    last = roll(packed, 6 - 2 * c, 0) if c < 3 else packed
    return jnp.where(core == 1, last, first)


def call(kernel, name, outs, scratch, limit, in_specs, out_specs):
    return pl.pallas_call(
        kernel,
        out_shape=[
            pltpu.HBM(shape, F32) if spec is HBM else jax.ShapeDtypeStruct(shape, F32)
            for shape, spec in zip(outs, out_specs)
        ],
        in_specs=in_specs,
        out_specs=out_specs,
        scratch_shapes=[pltpu.VMEM(x, F32) if isinstance(x, tuple) else x for x in scratch],
        compiler_params=pltpu.CompilerParams(vmem_limit_bytes=limit * 2**20),
        cost_estimate=pl.CostEstimate(flops=10_000_000, bytes_accessed=2_000_000, transcendentals=0),
        name=name,
    )


def inner_kernel(src, reg, sw, kept, flag, sol_out, res_out, field, s, hh, sol, res, ids, sems):
    flag[...] = jnp.zeros((8, 128), F32)
    core = lax.axis_index("rad")
    pick = from_partner((8, 256), core)
    lane = lax.broadcasted_iota(jnp.int32, (24, 128), 1)
    copies = [pltpu.make_async_copy(src.at[c], field.at[c, :, 0:16, :], sems.at[c]) for c in range(3)]
    copies.append(pltpu.make_async_copy(reg, ids, sems.at[3]))
    for copy in copies:
        copy.start()
    for copy in copies:
        copy.wait()

    def assemble(z):
        for c in range(4):
            rows = partner_rows(sw[z], c, core)
            field[c, z, 16:24, :] = jnp.where(pick, rows, 0.0 if c < 3 else -1.0)
        field[3, z, 0:16, :] = ids[z].astype(F32)

    loop(0, 16, assemble, 4)

    def vec(z):
        return [field[c, z] for c in range(3)]

    def first_h(z):
        reluct, _ = materials(field[3, z])
        h = strength(*vec(z), field[1, z + 1], field[2, z + 1], reluct)
        for c in range(3):
            hh[c, z] = h[c]

    loop(0, 15, first_h, UNROLL)

    def first_a(z):
        v = vec(z)
        _, mass = materials(field[3, z])
        a = image(v, [hh[c, z] for c in range(3)], hh[1, z - 1], hh[2, z - 1], mass)
        step = second_of(v, a, mass)
        for c in range(3):
            s[c, z] = step[c]
            res[c, z] = (v[c] - FIRST * a[c])[:16]
            sol[c, z] = (FIRST * v[c] + step[c])[:16]

    loop(1, 15, first_a, UNROLL)

    copies = [pltpu.make_async_copy(sol, sol_out, sems.at[0])]
    copies[0].start()

    def stress_plane(z):
        u0, u1, u2 = [FIRST * field[c, z] + s[c, z] for c in range(3)]
        u1n, u2n = [FIRST * field[c, z + 1] + s[c, z + 1] for c in (1, 2)]
        kept[KEPT.stress(z)] = stress_of(u0, u1, u2, u1n, u2n, core)

    for z in range(1, 14):
        stress_plane(z)

    def second_h(z):
        reluct, _ = materials(field[3, z])
        h = strength(s[0, z], s[1, z], s[2, z], s[1, z + 1], s[2, z + 1], reluct)
        for c in range(3):
            hh[c, z] = h[c]

    loop(1, 14, second_h, UNROLL)

    def second_a(z):
        _, mass = materials(field[3, z])
        v = [s[c, z] for c in range(3)]
        a = image(v, [hh[c, z] for c in range(3)], hh[1, z - 1], hh[2, z - 1], mass)
        for c in range(3):
            res[c, z] = res[c, z] - a[c][:16]

    loop(2, 14, second_a, UNROLL)
    copies.append(pltpu.make_async_copy(res, res_out, sems.at[1]))
    copies[1].start()
    for c in range(3):
        for z in KEPT.of_step:
            kept[KEPT.step(c, z)] = s[c, z]
        for z in KEPT.of_res:
            kept[KEPT.res(c, z)] = res[c, z]
        kept[KEPT.strength(c, 0)] = hh[c, 0]
        if c > 0:
            kept[KEPT.strength(c, 14)] = hh[c, 14]
    for c in range(4):
        for z in KEPT.of_field:
            kept[KEPT.field(c, z)] = field[c, z]

    for c in range(4):
        right = left = jnp.full((24, 128), 0.0 if c < 3 else -1.0, F32)
        for z in range(16):
            right, left = pack_plane(right, left, field[c, z], z + 2, lane)
        kept[KEPT.strips(c, 0)] = right
        kept[KEPT.strips(c, 1)] = left

    for copy in copies:
        copy.wait()


def rim_kernel(kept, up, sw, dn, _, hbm, az_up, az_dn, rim, w, out, up_msg, dn_msg, sem):
    core, ax = lax.axis_index("rad"), lax.axis_index("ax")
    lo = jnp.where(ax > 0, 1.0, 0.0)
    hi = jnp.where(ax < lax.axis_size("ax") - 1, 1.0, 0.0)
    pick = from_partner((8, 256), core)
    for c in range(4):
        empty = 0.0 if c < 3 else -1.0

        def put(i, value, beside, valid):
            w[c, i, 0:16, :] = (value - empty) * valid + empty
            w[c, i, 16:24, :] = jnp.where(pick, (beside - empty) * valid + empty, empty)

        put(0, up[2 * c], sw[2 * c], lo)
        put(1, up[2 * c + 1], sw[2 * c + 1], lo)
        put(6, dn[c], partner_rows(dn[6, 0:8], c, core), hi)
        if c in (1, 2):
            put(7, dn[3 + c], partner_rows(dn[6, 8:16], c, core), hi)
        else:
            w[c, 7] = jnp.full((24, 256), empty, F32)
        for z in (-2, -1):
            rim[RIM.field(c, z)] = w[c, z + 2]
        w[c, 2] = kept[KEPT.field(c, 0)]
        w[c, 3] = kept[KEPT.field(c, 1)]
        w[c, 4] = kept[KEPT.field(c, 14)]
        w[c, 5] = kept[KEPT.field(c, 15)]

    def vec(i):
        return [w[c, i] for c in range(3)]

    def h_of(i, reluct):
        return strength(*vec(i), w[1, i + 1], w[2, i + 1], reluct)

    def step_of(i, z, h, h1p, h2p):
        v, mass = vec(i), materials(w[3, i])[1]
        a = image(v, h, h1p, h2p, mass)
        step = second_of(v, a, mass)
        for c in range(3):
            rim[RIM.step(c, z)] = step[c]
            if z < 16:
                rim[RIM.res(c, z)] = (v[c] - FIRST * a[c])[:16]
        return [FIRST * v[c] + step[c] for c in range(3)]

    h_before = h_of(1, materials(w[3, 1])[0])
    h_last = h_of(5, materials(w[3, 5])[0])
    h_after = h_of(6, materials(w[3, 6])[0])
    h_zero = [kept[KEPT.strength(c, 0)] for c in range(3)]
    u_first = step_of(2, 0, h_zero, h_before[1], h_before[2])
    u_last = step_of(5, 15, h_last, kept[KEPT.strength(1, 14)], kept[KEPT.strength(2, 14)])
    u_after = step_of(6, 16, h_after, h_last[1], h_last[2])
    u_one = [FIRST * w[c, 3] + kept[KEPT.step(c, 1)] for c in range(3)]
    u_14 = [FIRST * w[c, 4] + kept[KEPT.step(c, 14)] for c in range(3)]
    for z in range(1, 14):
        out[z, :, 0:256] = kept[KEPT.stress(z)]
    out[0, :, 0:256] = stress_of(*u_first, u_one[1], u_one[2], core)
    out[14, :, 0:256] = stress_of(*u_14, u_last[1], u_last[2], core)
    out[15, :, 0:256] = stress_of(*u_last, u_after[1], u_after[2], core)
    main, last = [slice(0, 256), slice(256, 384)]
    copies = [pltpu.make_async_copy(out.at[:, :, main], hbm.at[:, :, main], sem.at[0])]
    copies[0].start()

    lane = lax.broadcasted_iota(jnp.int32, (24, 128), 1)
    plane = (lane * 43) >> 8
    k = lane - 6 * plane
    right, left = [], []
    for c in range(4):
        r, l = kept[KEPT.strips(c, 0)], kept[KEPT.strips(c, 1)]
        for i, n in ((0, 0), (1, 1), (18, 6), (19, 7)):
            r, l = pack_plane(r, l, w[c, n], i, lane)
        empty = 0.0 if c < 3 else -1.0
        r = jnp.where(k < 4, r, empty)
        l = jnp.where(k > 1, l, empty)
        rim[RIM.strips(c, 0)] = r
        rim[RIM.strips(c, 1)] = l
        right.append(r)
        left.append(l)
    for msg, x in ((up_msg, right), (dn_msg, left)):
        msg[0] = jnp.where(
            k < 2, roll(x[2], -2, 1), jnp.where(k < 4, x[0], roll(x[1], 2, 1))
        )
        msg[1] = x[3]
    copies.append(pltpu.make_async_copy(up_msg, az_up, sem.at[1]))
    copies.append(pltpu.make_async_copy(dn_msg, az_dn, sem.at[2]))
    copies[1].start()
    copies[2].start()

    f = SECOND_A

    def partial(x):
        reluct, mass = materials(x[3])
        v = x[:3]
        h = strength(*v, roll(v[1], -6, 1), roll(v[2], -6, 1), reluct)
        a = image(v, h, roll(h[1], 6, 1), roll(h[2], 6, 1), mass)
        step = second_of(v, a, mass)
        u = [FIRST * v[c] + step[c] for c in range(3)]
        return reluct, h, u, fluxes(*u, roll(u[1], -6, 1), roll(u[2], -6, 1))

    reluct, (h0, h1, _), _, (flux1, flux2) = partial(right)
    fh1 = f * h1
    rest = f * ((roll(h0, -6, 1) - h0) + (roll(h1, -1, 0) - h1))
    rel_up, rel_dn = f * roll(reluct, -1, 0), f * roll(reluct, 1, 0)
    a_part = jnp.where(
        k < 2,
        roll(jnp.where(k == 3, flux1 - fh1, flux1), -2, 1),
        jnp.where(k == 2, roll(fh1, -1, 1), jnp.where(k < 5, roll(flux2, 1, 1), roll(rest, 2, 1))),
    )
    x_part = jnp.where(
        k == 1,
        -roll(rel_dn, -8, 1),
        jnp.where(k == 4, -roll(rel_up, 1, 1), jnp.where(k == 5, roll(rel_up, 2, 1), 0.0)),
    )
    z_part = jnp.where(k == 1, roll(rel_dn, -2, 1), 0.0)

    _, _, u, (flux1, flux2) = partial(left)
    v0, v1 = left[0], left[1]
    v1n = roll(v1, -6, 1)
    v1_dn = roll(v1, 1, 0)
    v0_up = roll(v0, -1, 0)
    inside = jnp.where(plane == 17, hi, 1.0)
    r_a = u[0] + f * ((roll(v0, -6, 1) + roll(v0, 6, 1)) - (3.0 + inside) * v0 + (v1n - v1))
    r_b = f * ((v1n - v1) + v0)
    b_part = jnp.where(
        k == 0,
        roll(f * v0, -2, 1),
        jnp.where(
            k == 1,
            roll(r_a, -1, 1),
            jnp.where(
                k == 2,
                flux1 + f * v0,
                jnp.where(k == 4, roll(r_b, 2, 1), jnp.where(k == 5, roll(flux2 - r_b, 3, 1), 0.0)),
            ),
        ),
    )
    y_part = jnp.where(
        k == 1, roll(v1_dn, -7, 1), jnp.where(k == 4, roll(v0_up, 2, 1), roll(v0_up, 3, 1))
    )
    w_part = roll(v1_dn, -1, 1)

    lane = lax.broadcasted_iota(jnp.int32, (8, 128), 1)
    parts = [
        roll(gap_tile(x, core), 6 * n, 1) if n else gap_tile(x, core)
        for n, x in enumerate((a_part, x_part, z_part, b_part, y_part, w_part))
    ]
    for z in range(16):
        part = (((lane - 6 * (z + 2)) & 127) * 43) >> 8
        extra = parts[5]
        for n in range(5):
            extra = jnp.where(part == n, parts[n], extra)
        out[z, :, 256:384] = extra
    copies.append(pltpu.make_async_copy(out.at[:, :, last], hbm.at[:, :, last], sem.at[3]))
    copies[3].start()
    for copy in copies:
        copy.wait()


def edge_kernel(skew, kept, rim, sol_in, res_in, sol, out, table):
    offset = 256 * lax.broadcasted_iota(jnp.int32, (16, MH), 0) - skew[lax.axis_index("az")]
    turns = (offset * lax.broadcasted_iota(jnp.int32, (16, MH), 1)) & (NA - 1)
    angle = turns.astype(F32) * (2.0 * math.pi / NA)
    table[0] = jnp.cos(angle)
    table[1] = jnp.sin(angle)

    v2, v1 = [[rim[RIM.field(c, z)] for c in range(4)] for z in (-2, -1)]
    v0 = [kept[KEPT.field(c, 0)] for c in range(3)]
    rim_code = materials(v1[3])
    _, h1, h2 = strength(*v2[:3], v1[1], v1[2], materials(v2[3])[0])
    h = strength(*v1[:3], v0[1], v0[2], rim_code[0])
    before_first = second_of(v1, image(v1, h, h1, h2, rim_code[1]), rim_code[1])

    def step(z, c):
        if z < 0:
            return before_first[c]
        return rim[RIM.step(c, z)] if z in (0, 15, 16) else kept[KEPT.step(c, z)]

    def materials_of(z):
        return rim_code if z < 0 else materials(kept[KEPT.field(3, z)])

    def h_of(z):
        return strength(
            step(z, 0), step(z, 1), step(z, 2), step(z + 1, 1), step(z + 1, 2), materials_of(z)[0]
        )

    for z in (0, 14):
        _, h1, h2 = h_of(z - 1)
        for n in range(2):
            h = h_of(z + n)
            a = image([step(z + n, c) for c in range(3)], h, h1, h2, materials_of(z + n)[1])
            h1, h2 = h[1], h[2]
            for c in range(3):
                x = z + n
                before = rim[RIM.res(c, x)] if x in (0, 15) else kept[KEPT.res(c, x)]
                out[c, x] = before - a[c][:16]
    for c in range(3):
        out[c, 2:14] = res_in[c, 2:14]
        sol[c, 1:15] = sol_in[c, 1:15]
        for z in (0, 15):
            sol[c, z] = FIRST * kept[KEPT.field(c, z)][:16] + rim[RIM.step(c, z)][:16]


def seam_kernel(rim, sol_in, res_in, from_left, from_right, sol, res, a_sol, a_res, sems):
    lane = lax.broadcasted_iota(jnp.int32, (24, 128), 1)
    plane = (lane * 43) >> 8
    k = lane - 6 * plane

    def full(x, msg, halo, shifts):
        return [
            jnp.where(halo, roll(msg[t], shift, 1) if shift else msg[t], x[c])
            for c, (t, shift) in enumerate(zip((0, 0, 0, 1), shifts))
        ]

    right = full([rim[RIM.strips(c, 0)] for c in range(4)], from_right, k > 3, (2, 0, 4, 2))
    left = full([rim[RIM.strips(c, 1)] for c in range(4)], from_left, k < 2, (-2, -4, 0, -2))
    copies = []

    def operator(v, reluct, mass):
        h = strength(*v, roll(v[1], -6, 1), roll(v[2], -6, 1), reluct)
        return image(v, h, roll(h[1], 6, 1), roll(h[2], 6, 1), mass)

    def send(n, buf, dst, inner, rights, lefts):
        lane = lax.broadcasted_iota(jnp.int32, (16, 128), 1)
        for c in range(3):
            merged = jnp.where(k[:16] < 4, rights[c][:16], roll(lefts[c][:16], 2, 1))
            for z in range(16):
                edge = roll(merged, 124 - 6 * (z + 2), 1)
                buf[c, z, :, 0:128] = jnp.where(lane < 2, edge, inner[c, z, :, 0:128])
                buf[c, z, :, 128:256] = jnp.where(lane >= 126, edge, inner[c, z, :, 128:256])
            copies.append(pltpu.make_async_copy(buf.at[c], dst.at[c], sems.at[n, c]))
            copies[-1].start()

    sides = []
    for x in (right, left):
        reluct, mass = materials(x[3])
        a = operator(x[:3], reluct, mass)
        sides.append((x[:3], reluct, mass, a, second_of(x, a, mass)))
    send(
        0, a_sol, sol, sol_in, *[[FIRST * v[c] + step[c] for c in range(3)] for v, _, _, _, step in sides]
    )
    rest = []
    for v, reluct, mass, a, step in sides:
        a2 = operator(step, reluct, mass)
        rest.append([v[c] - FIRST * a[c] - a2[c] for c in range(3)])
    send(1, a_res, res, res_in, *rest)
    for copy in copies:
        copy.wait()


def seam_call(*args):
    out = jax.ShapeDtypeStruct((3, 16, 16, 256), F32)
    return pl.pallas_call(
        seam_kernel,
        out_shape=[out, out],
        in_specs=[VMEM] * len(args),
        out_specs=[HBM] * 2,
        scratch_shapes=[
            pltpu.VMEM((3, 16, 16, 256), F32),
            pltpu.VMEM((3, 16, 16, 256), F32),
            pltpu.SemaphoreType.DMA((2, 3)),
        ],
        compiler_params=pltpu.CompilerParams(vmem_limit_bytes=12 * 2**20),
        cost_estimate=pl.CostEstimate(flops=4_000_000, bytes_accessed=4_000_000, transcendentals=0),
        name="seams",
    )(*args)


def harmonics_kernel(block, basis_hi, basis_lo, table, out):
    lane = lax.broadcasted_iota(jnp.int32, (16, 8, 128), 2)
    seam = block[:, :, 256:384]
    right = jnp.concatenate([seam[1:], seam[:1]], axis=0).reshape(128, 128)
    first = 6 * (lax.axis_index("az") + 2)
    right = pltpu.roll(right, lax.rem(254 - first - 18, 128), 1)
    seam = pltpu.roll(seam.reshape(128, 128), lax.rem(254 - first, 128), 1)
    product = seam * right
    flux = seam + right + roll(product, -6, 1) + roll(product, -12, 1)
    square = 0.5 * (flux * flux)
    fixed = (square - roll(square, -3, 1)).reshape(16, 8, 128)
    moved = jnp.concatenate([fixed[15:], fixed[:15]], axis=0)
    low = jnp.where(lane == 0, moved, block[:, :, 0:128])
    high = jnp.where(lane >= 126, fixed, block[:, :, 128:256])
    x = jnp.concatenate([low.reshape(128, 128), high.reshape(128, 128)], axis=1)
    x_hi = x.astype(jnp.bfloat16)
    x_lo = (x - x_hi.astype(F32)).astype(jnp.bfloat16)

    def dot(a, b):
        return jnp.dot(a, b[...], preferred_element_type=F32)

    both = dot(jnp.concatenate([x_hi, x_lo], axis=0), basis_hi)
    local = both[:128] + (both[128:] + dot(x_hi, basis_lo))
    local = local.reshape(16, 8, 2 * MH)
    real = jnp.zeros((8, MH), F32)
    imag = jnp.zeros((8, MH), F32)
    for j in range(16):
        c, s = table[0, j : j + 1, :], table[1, j : j + 1, :]
        pc, ps = local[j, :, :MH], local[j, :, MH:]
        real = real + (pc * c - ps * s)
        imag = imag - (pc * s + ps * c)
    out[0, 0] = real
    out[1, 0] = imag


def harmonics_call(block, table):
    turns = np.arange(256)[:, None] * np.arange(MH)[None, :] / NA
    angle = 2.0 * math.pi * turns
    basis = np.concatenate([np.cos(angle), np.sin(angle)], axis=1) / math.sqrt(NA)
    hi = basis.astype(jnp.bfloat16)
    lo = (basis - hi.astype(np.float64)).astype(jnp.bfloat16)
    return pl.pallas_call(
        harmonics_kernel,
        out_shape=jax.ShapeDtypeStruct((2, 1, 8, MH), F32),
        in_specs=[VMEM] * 4,
        out_specs=VMEM,
        compiler_params=pltpu.CompilerParams(vmem_limit_bytes=8 * 2**20),
        cost_estimate=pl.CostEstimate(flops=100_000_000, bytes_accessed=1_000_000, transcendentals=0),
        name="harmonics",
    )(block, jnp.asarray(hi), jnp.asarray(lo), table)


def ring(axis, size, step):
    return functools.partial(
        lax.ppermute, axis_name=axis, perm=[(i, (i + step) % size) for i in range(size)]
    )


def on_device(source, region, skew_shift):
    n_az, n_ax = lax.axis_size("az"), lax.axis_size("ax")
    up, dn, sw = send_call(source, region)
    swap = ring("rad", 2, 1)
    sw = swap(sw)
    up = ring("ax", n_ax, 1)(up)
    dn = ring("ax", n_ax, -1)(jnp.concatenate([dn, sw[0:2].reshape(1, 16, 256)], axis=0))
    block, tall = (3, 16, 16, 256), (16, 24, 256)
    kept, flag, sol, res = call(
        inner_kernel,
        "inner",
        [(Kept.planes, 24, 256), (8, 128), block, block],
        [
            (4, *tall),
            (3, *tall),
            (3, *tall),
            block,
            block,
            pltpu.VMEM((16, 16, 256), jnp.int32),
            pltpu.SemaphoreType.DMA((4,)),
        ],
        16,
        [HBM, HBM, VMEM],
        [VMEM, VMEM, HBM, HBM],
    )(source, region, sw)
    start, flag = lax.optimization_barrier((8 * (1 - lax.axis_index("rad")), flag))
    sw_up = swap(lax.dynamic_slice_in_dim(up, start, 8, axis=1))
    stress, az_up, az_dn, rim = call(
        rim_kernel,
        "rim",
        [(16, 8, 384), (2, 24, 128), (2, 24, 128), (Rim.planes, 24, 256)],
        [
            (4, 8, 24, 256),
            (16, 8, 384),
            (2, 24, 128),
            (2, 24, 128),
            pltpu.SemaphoreType.DMA((4,)),
        ],
        8,
        [VMEM] * 4 + [pl.BlockSpec(memory_space=pl.ANY)],
        [HBM, HBM, HBM, VMEM],
    )(kept, up, sw_up, dn, flag)
    circle = lax.all_to_all(stress, "az", split_axis=0, concat_axis=0, tiled=True)
    from_left = ring("az", n_az, 1)(az_up)
    from_right = ring("az", n_az, -1)(az_dn)
    sol, res, table = call(
        edge_kernel, "edge", [block, block, (2, 16, MH)], [], 8, [SMEM] + [VMEM] * 4, [VMEM] * 3
    )(skew_shift, kept, rim, sol, res)
    solution, residual = seam_call(rim, sol, res, from_left, from_right)
    harmonics = harmonics_call(circle, table)
    return (solution, residual, harmonics)


def solution(mesh):
    in_specs = (P(None, "ax", "rad", "az"), P("ax", "rad", "az"), P("ax"))
    out_specs = (
        P(None, "ax", "rad", "az"),
        P(None, "ax", "rad", "az"),
        P(None, ("ax", "az"), "rad", None),
    )
    return jax.shard_map(
        on_device, mesh=mesh, in_specs=in_specs, out_specs=out_specs, check_vma=False
    )
```
